32 devices in a mesh: dp: 4 (over y, x), fsdp: 8 (over z, core).
Axes of the slice: x: 2, y: 2, z: 4, core: 2. Of those that a mesh axis runs over, the one named last changes fastest.
Arguments:
- inputs: bfloat16 [32, 512, 768], P(('dp', 'fsdp')), may hold values from -6 to 6
- seg_ids: int32 [32, 512], P(('dp', 'fsdp')), may hold values from 0 to 7, never falling along the last dimension, each value on 1 to 128 neighbouring positions
- pool_index: int32 [32, 8], P(('dp', 'fsdp')), may hold values from 0 to 7, each once within a row
- w_query: bfloat16 [768, 768], P('fsdp'), may hold values from -0.109375 to 0.109375
- w_key: bfloat16 [768, 768], P('fsdp'), may hold values from -0.109375 to 0.109375
- w_value: bfloat16 [768, 768], P('fsdp'), may hold values from -0.21875 to 0.21875
- w_out: bfloat16 [768, 768], P('fsdp'), may hold values from -0.625 to 0.625
- w_up: bfloat16 [768, 3072], P('fsdp'), may hold values from -0.21875 to 0.21875
- w_down: bfloat16 [3072, 768], P('fsdp'), may hold values from -0.109375 to 0.109375
- w_proj: bfloat16 [768, 768], P('fsdp'), may hold values from -0.21875 to 0.21875
- gain_attn: float32 [768], replicated, may hold values from 0.5 to 1.5
- gain_ffn: float32 [768], replicated, may hold values from 0.5 to 1.5
- gain_final: float32 [768], replicated, may hold values from 0.5 to 1.5
- bias_table: float32 [32, 12], replicated, may hold values from -4 to 4
- emb_grad: float32 [32, 8, 768], P(('dp', 'fsdp')), may hold values from -6 to 6
Outputs:
- embeddings: float32 [32, 8, 768], P(('dp', 'fsdp'))
- input_grad: float32 [32, 512, 768], P(('dp', 'fsdp'))
- grad_query: float32 [768, 768], P('fsdp')
- grad_key: float32 [768, 768], P('fsdp')
- grad_value: float32 [768, 768], P('fsdp')
- grad_out: float32 [768, 768], P('fsdp')
- grad_up: float32 [768, 3072], P('fsdp')
- grad_down: float32 [3072, 768], P('fsdp')
- grad_proj: float32 [768, 768], P('fsdp')
- grad_gain_attn: float32 [768], replicated
- grad_gain_ffn: float32 [768], replicated
- grad_gain_final: float32 [768], replicated
- grad_table: float32 [32, 12], replicated
The draws below stay inside these ranges and needn't reach their ends.
Inputs may be any that keep to these rules, and one draw needn't show every extreme that they name: `seg_ids`: within a row the ids never fall, and each of 0 to 7 holds 1 to 128 tokens. `pool_index`: each row is a permutation of 0 to 7.
All inputs are finite; a program needn't handle non-finite values.
Results may differ from the reference program's by a relative error of at most 0.015.
Values may be sent and summed in bfloat16 or wider, within the bound.
A program may use at most 192 MiB of HBM per device.

```python
import math
import jax
import jax.numpy as jnp
import numpy as np
from jax import lax

D = 768
HEADS = 12
HEAD = 64
FF = 3072
BUCKETS = 32
REACH = 128
SEQ = 512
PASS = 8
ROWS = 32


def levels(key, dims, cuts, least, high):
    def one(dim, blocks):
        draws = jax.random.uniform(jax.random.fold_in(jax.random.fold_in(key, 6), dim), (blocks,), jnp.float32, least / len(cuts), high / len(cuts))
        return jnp.repeat(jnp.exp(draws), dims[dim] // blocks).reshape((-1,) + (1,) * (len(dims) - dim - 1))

    level = one(*cuts[0])
    for cut in cuts[1:]:
        level = level * one(*cut)
    return level


def split_up(amount, total, limit, slope):
    loads = [(1 << 20) // math.isqrt(rank ** slope) + 1 for rank in range(2, amount + 1)]
    surplus, holding = total - limit - (amount - 1), [1] * (amount - 1)
    while surplus > 0:
        candidates = [i for i in range(amount - 1) if holding[i] < limit]
        mass, left = sum([loads[i] for i in candidates]), surplus
        for i in candidates:
            more = min(limit - holding[i], max(1, left * loads[i] // mass), surplus)
            holding[i] = holding[i] + more
            surplus = surplus - more
    return np.array([limit] + holding)


def uneven_parts(key, amount, total, bound, slope):
    if amount == 2:
        one = jax.random.randint(key, (), max(1, total - bound), min(bound, total - 1) + 1)
        return jnp.stack([one, total - one])
    tallies = jnp.asarray(split_up(amount, total, bound, slope), jnp.int32)
    couples = (amount - 1) // 2
    donor, taker = tallies[1:1 + 2 * couples:2], tallies[2:2 + 2 * couples:2]
    slack = jnp.minimum(donor - 1, bound - taker)
    passed = jax.random.randint(jax.random.fold_in(key, 1), (couples,), 0, 1 << 20) % (slack + 1)
    tallies = tallies.at[1:1 + 2 * couples:2].set(donor - passed).at[2:2 + 2 * couples:2].set(taker + passed)
    return tallies[jax.random.permutation(jax.random.fold_in(key, 2), amount)]


def noise(rng, dims, deviation, bound, cuts=(), kind=jnp.bfloat16):
    values = jax.random.normal(rng, dims, jnp.float32) * deviation
    if len(cuts) > 0:
        values = levels(rng, dims, cuts, -0.22, 0.18) * values
    return jnp.clip(values, min=-bound, max=bound).astype(kind)


def setup_inputs(seed: int = 0) -> dict:
    streams_of = jax.random.split(jax.random.key(seed), 16)
    return {
        "inputs": noise(streams_of[0], (ROWS, SEQ, D), 1.0, 6.0, ((0, 32),)),
        "seg_ids": jax.vmap(lambda own: jnp.searchsorted(jnp.cumsum(uneven_parts(own, PASS, SEQ, 2 * SEQ // PASS, 1)), jnp.arange(SEQ), side="right"))(jax.random.split(streams_of[1], ROWS)).reshape((ROWS, SEQ)).astype(jnp.int32),
        "pool_index": jax.vmap(lambda own: jax.random.permutation(own, PASS))(jax.random.split(streams_of[2], ROWS)).reshape((ROWS, PASS)).astype(jnp.int32),
        "w_query": noise(streams_of[3], (D, D), (4 * D) ** -0.5, 0.109375, ((0, 8),)),
        "w_key": noise(streams_of[4], (D, D), (4 * D) ** -0.5, 0.109375, ((0, 8),)),
        "w_value": noise(streams_of[5], (D, D), D ** -0.5, 0.21875, ((0, 8),)),
        "w_out": noise(streams_of[6], (D, D), (D // 8) ** -0.5, 0.625, ((0, 8),)),
        "w_up": noise(streams_of[7], (D, FF), D ** -0.5, 0.21875, ((0, 8),)),
        "w_down": noise(streams_of[8], (FF, D), FF ** -0.5, 0.109375, ((0, 8),)),
        "w_proj": noise(streams_of[9], (D, D), D ** -0.5, 0.21875, ((0, 8),)),
        "gain_attn": jnp.clip(1.0 + 0.1 * jax.random.normal(streams_of[10], (D,), jnp.float32), 0.5, 1.5),
        "gain_ffn": jnp.clip(1.0 + 0.1 * jax.random.normal(streams_of[11], (D,), jnp.float32), 0.5, 1.5),
        "gain_final": jnp.clip(1.0 + 0.1 * jax.random.normal(streams_of[12], (D,), jnp.float32), 0.5, 1.5),
        "bias_table": noise(streams_of[13], (BUCKETS, HEADS), 1.0, 4.0, (), jnp.float32),
        "emb_grad": noise(streams_of[14], (ROWS, PASS, D), 1.0, 6.0, ((0, 32),), jnp.float32),
    }


EPSILON = 1e-06
HIGH = lax.Precision.HIGHEST

@jax.custom_vjp
def low(v):
    return lax.optimization_barrier(v.astype(jnp.bfloat16)).astype(jnp.float32)

@jax.custom_vjp
def low_back(v):
    return v

def low_keep(v):
    return (low(v), None)

def low_pass(kept, grad):
    return (grad,)

def back_keep(v):
    return (v, None)

def back_low(kept, grad):
    return (low(grad),)
low.defvjp(low_keep, low_pass)
low_back.defvjp(back_keep, back_low)

def bucket_table(length, buckets, reach):
    positions = np.arange(length)
    relative = positions[None, :] - positions[:, None]
    halfway = buckets // 2
    exact_span = halfway // 2
    distance = np.abs(relative)
    logged = exact_span + (np.log(np.maximum(distance, 1) / exact_span) / np.log(reach / exact_span) * (halfway - exact_span)).astype(np.int64)
    logged = np.minimum(logged, halfway - 1)
    result = (relative > 0).astype(np.int64) * halfway + np.where(distance < exact_span, distance, logged)
    return result.astype(np.int32)

def rms_norm(values, gain):
    return values * lax.rsqrt(lax.optimization_barrier(jnp.mean(values * values, axis=-1, keepdims=True)) + EPSILON) * gain

def both_round(values):
    return low(low_back(values))

def matmul(left, right):
    return jnp.matmul(left, right, precision=HIGH)

def forward(params, seg_ids, pool_index):
    inputs, w_query, w_key, w_value, w_out, w_up, w_down, w_proj, gain_attn, gain_ffn, gain_final, bias_table = params
    rows = inputs.shape[0]
    head_shape = (rows, SEQ, HEADS, HEAD)
    normed_one = low(rms_norm(inputs, gain_attn))
    queries = both_round(matmul(normed_one, w_query)).reshape(head_shape)
    key_rows = both_round(matmul(normed_one, w_key)).reshape(head_shape)
    value_rows = both_round(matmul(normed_one, w_value)).reshape(head_shape)
    bucket_ids = jnp.asarray(bucket_table(SEQ, BUCKETS, REACH))
    bias = jnp.transpose(bias_table[bucket_ids], (2, 0, 1))

    def attend_row(pieces):
        query_row, key_row, value_row, seg_row = pieces
        raw_scores = jnp.einsum('qhd,khd->hqk', query_row, key_row, precision=HIGH)
        scores = low_back(raw_scores + bias)
        same_doc = (seg_row[:, None] == seg_row[None, :])[None]
        scores = jnp.where(same_doc, scores, -1e+30)
        row_peak = lax.optimization_barrier(jnp.max(scores, axis=-1, keepdims=True))
        powered = jnp.exp(scores - row_peak)
        softmax_rows = powered / lax.optimization_barrier(jnp.sum(powered, axis=-1, keepdims=True))
        mixed = jnp.einsum('hqk,khd->qhd', low(softmax_rows), value_row, precision=HIGH)
        return both_round(mixed).reshape(SEQ, D)
    attended = lax.map(jax.checkpoint(attend_row), (queries, key_rows, value_rows, seg_ids))
    branch_attn = low_back(matmul(attended, w_out))
    hidden_one = inputs + branch_attn
    normed_two = low(rms_norm(hidden_one, gain_ffn))
    pre_act = low_back(matmul(normed_two, w_up))
    activated = low(jax.nn.gelu(pre_act, approximate=True))
    branch_ffn = low_back(matmul(activated, w_down))
    hidden_two = hidden_one + branch_ffn
    final_rows = rms_norm(hidden_two, gain_final)
    member = (seg_ids[:, None, :] == pool_index[:, :, None]).astype(jnp.float32)
    counts = lax.optimization_barrier(jnp.sum(member, axis=-1, keepdims=True))
    pooled = jnp.einsum('rpl,rld->rpd', member, final_rows, precision=HIGH) / counts
    projected = matmul(pooled, w_proj)
    return projected * lax.rsqrt(lax.optimization_barrier(jnp.sum(projected * projected, axis=-1, keepdims=True)) + EPSILON)

def reference(inputs, seg_ids, pool_index, w_query, w_key, w_value, w_out, w_up, w_down, w_proj, gain_attn, gain_ffn, gain_final, bias_table, emb_grad):
    params = tuple((array.astype(jnp.float32) for array in (inputs, w_query, w_key, w_value, w_out, w_up, w_down, w_proj, gain_attn, gain_ffn, gain_final, bias_table)))

    def wrapped(*values):
        return forward(values, seg_ids, pool_index)
    embeddings, pullback = jax.vjp(wrapped, *params)
    grads = pullback(emb_grad.astype(jnp.float32))
    return (embeddings, grads[0], grads[1], grads[2], grads[3], grads[4], grads[5], grads[6], grads[7], grads[8], grads[9], grads[10], grads[11])
```

```python
from functools import partial

import jax
import jax.numpy as jnp
import numpy as np
from jax import lax
from jax.experimental import pallas as pl
from jax.experimental.pallas import tpu as pltpu
from jax.sharding import PartitionSpec as P

REACH = 128


EPSILON = 1e-06
VMEM_BYTES = 60 * 2**20
HIGH = lax.Precision.HIGHEST


def bucket_table(length, buckets, reach):
    positions = np.arange(length)
    relative = positions[None, :] - positions[:, None]
    halfway = buckets // 2
    exact_span = halfway // 2
    distance = np.abs(relative)
    logged = exact_span + (
        np.log(np.maximum(distance, 1) / exact_span)
        / np.log(reach / exact_span)
        * (halfway - exact_span)
    ).astype(np.int64)
    logged = np.minimum(logged, halfway - 1)
    result = (relative > 0).astype(np.int64) * halfway + np.where(
        distance < exact_span, distance, logged
    )
    return result.astype(np.int32)


def rms_forward(values, gain):
    factor = lax.rsqrt(jnp.mean(values * values, axis=-1, keepdims=True) + EPSILON)
    return (values * factor * gain, factor)


def rms_backward(values, factor, gain, upstream):
    normed = values * factor
    gain_grad = jnp.sum(upstream * normed, axis=0)
    inner = upstream * gain
    return (factor * (inner - normed * jnp.mean(inner * normed, axis=-1, keepdims=True)), gain_grad)


def matmul(left, right):
    return jnp.dot(left, right, preferred_element_type=jnp.float32)


def matmul_left(left, right):
    return lax.dot_general(
        left, right, (((0,), (0,)), ((), ())), preferred_element_type=jnp.float32
    )


def matmul_right(left, right):
    return lax.dot_general(
        left, right, (((1,), (1,)), ((), ())), preferred_element_type=jnp.float32
    )


def row_scores(query_row, key_row, seg_row, bias):
    raw_scores = jnp.einsum("qhd,khd->hqk", query_row, key_row, preferred_element_type=jnp.float32)
    same_doc = (seg_row[:, None] == seg_row[None, :])[None]
    return jnp.where(same_doc, raw_scores + bias, -1e30)


MESH = pl.DeviceIdType.MESH
LANES = 128


class Place:
    def __init__(self):
        self.dp, self.fsdp = lax.axis_index("dp"), lax.axis_index("fsdp")
        self.y, self.x = self.dp // 2, self.dp % 2
        self.z, self.c = self.fsdp // 2, self.fsdp % 2

    def core(self):
        return (self.dp, self.z * 2 + (1 - self.c))

    def at_x(self):
        return (self.y * 2 + (1 - self.x), self.fsdp)

    def at_y(self):
        return ((1 - self.y) * 2 + self.x, self.fsdp)

    def at_xy(self):
        return ((1 - self.y) * 2 + (1 - self.x), self.fsdp)

    def up(self, d):
        return lax.rem(self.z + d, 4)

    def down(self, d):
        return lax.rem(self.z + 4 - d, 4)

    def at_z(self, d):
        return (self.dp, self.up(d) * 2 + self.c)

    def greet(self):
        barrier = pltpu.get_barrier_semaphore()
        partners = [self.core(), self.at_x(), self.at_y(), self.at_xy()]
        partners += [self.at_z(d) for d in (1, 2, 3)]
        for partner in partners:
            pl.semaphore_signal(barrier, inc=1, device_id=partner, device_id_type=MESH)
        pl.semaphore_wait(barrier, len(partners))


def remote(src, dst, send, recv, device):
    return pltpu.make_async_remote_copy(
        src_ref=src, dst_ref=dst, send_sem=send, recv_sem=recv, device_id=device, device_id_type=MESH
    )


def half(which, size, start=0):
    return pl.ds(pl.multiple_of(start + which * (size // 2), size // 2 if start % (size // 2) == 0 else 16), size // 2)


class Unit:
    def __init__(self, array, first, rows, left, wide):
        self.array, self.first, self.rows, self.left, self.wide = array, first, rows, left, wide

    def quarter(self, y, x):
        return (half(y, self.rows, self.first), half(x, self.wide, self.left))

    def whole(self):
        return (pl.ds(self.first, self.rows), pl.ds(self.left, self.wide))


class Gather:
    RECVS = 13

    def __init__(self, place, units, shards, wholes, send, recv):
        self.p, self.units, self.shards, self.wholes = place, units, shards, wholes
        self.send, self.recv = send, recv

    def _part(self, u, z, y, x):
        unit = self.units[u]
        return self.wholes[unit.array].at[(z, self.p.c) + unit.quarter(y, x)]

    def _z(self, u, d):
        p, unit = self.p, self.units[u]
        src = self.shards[unit.array].at[unit.quarter(p.y, p.x)]
        return remote(src, self._part(u, p.z, p.y, p.x), self.send.at[u, d - 1], self.recv.at[u, d - 1], p.at_z(d))

    def _hop(self, u, d, kind, y, x, device):
        ref = self._part(u, self.p.down(d), y, x)
        k = 3 * kind + d - 1
        return remote(ref, ref, self.send.at[u, k], self.recv.at[u, k], device)

    def _to_x(self, u, d):
        return self._hop(u, d, 1, self.p.y, self.p.x, self.p.at_x())

    def _to_y(self, u, d):
        return self._hop(u, d, 2, self.p.y, self.p.x, self.p.at_y())

    def _through_x(self, u, d):
        return (u + d) % 2 == 0

    def _diagonal(self, u, d):
        p = self.p
        if self._through_x(u, d):
            return self._hop(u, d, 3, p.y, 1 - p.x, p.at_y())
        return self._hop(u, d, 3, 1 - p.y, p.x, p.at_x())

    def _core(self, u):
        unit = self.units[u]
        ref = self.wholes[unit.array].at[(slice(None), self.p.c) + unit.whole()]
        return remote(ref, ref, self.send.at[u, 12], self.recv.at[u, 12], self.p.core())

    def start(self, u):
        for d in (1, 2, 3):
            self._z(u, d).start()

    def plane(self, u):
        for d in (1, 2, 3):
            self._z(u, d).wait_recv()
            self._to_x(u, d).start()
            self._to_y(u, d).start()

    def corner(self, u):
        for d in (1, 2, 3):
            first, second = (self._to_x, self._to_y) if self._through_x(u, d) else (self._to_y, self._to_x)
            first(u, d).wait_recv()
            self._diagonal(u, d).start()
            second(u, d).wait_recv()

    def pair(self, u):
        for d in (1, 2, 3):
            self._diagonal(u, d).wait_recv()
        self._core(u).start()

    def arrive(self, u):
        self._core(u).wait_recv()

    def finish(self, u):
        for d in (1, 2, 3):
            self._z(u, d).wait_send()
            self._to_x(u, d).wait_send()
            self._to_y(u, d).wait_send()
            self._diagonal(u, d).wait_send()
        self._core(u).wait_send()


def gather_units():
    small = [Unit(i, 0, 96, 0, 768) for i in range(4)]
    up = [Unit(4, 0, 96, 768 * j, 768) for j in range(4)]
    down = [Unit(5, 128 * j, 128, 0, 768) for j in range(3)]
    return small + up + [Unit(6, 0, 96, 0, 768)] + down


def gather_kernel(units, *refs):
    shards, outs, wholes = refs[:7], refs[7:14], refs[14:21]
    send, recv, local = refs[21:]
    place = Place()
    gather = Gather(place, units, shards, wholes, send, recv)
    own = [
        pltpu.make_async_copy(shard, whole.at[place.z, place.c], local.at[i])
        for i, (shard, whole) in enumerate(zip(shards, wholes))
    ]
    for copy in own:
        copy.start()
    place.greet()
    for u in range(len(units)):
        gather.start(u)
    for copy in own:
        copy.wait()
    stages = (gather.plane, gather.corner, gather.pair, gather.arrive)
    for step in range(len(units) + len(stages) - 1):
        for lag, stage in enumerate(stages):
            if 0 <= step - lag < len(units):
                stage(step - lag)
    back = [
        pltpu.make_async_copy(whole, out, local.at[i])
        for i, (whole, out) in enumerate(zip(wholes, outs))
    ]
    for copy in back:
        copy.start()
    for u in range(len(units)):
        gather.finish(u)
    for copy in back:
        copy.wait()


def gather_all(shards):
    units = gather_units()
    full = [(4, 2) + shard.shape for shard in shards]
    wholes = pl.pallas_call(
        partial(gather_kernel, units),
        out_shape=[jax.ShapeDtypeStruct(shape, jnp.bfloat16) for shape in full],
        in_specs=[pl.BlockSpec(memory_space=pl.ANY)] * 7,
        out_specs=[pl.BlockSpec(memory_space=pl.ANY)] * 7,
        scratch_shapes=[pltpu.VMEM(shape, jnp.bfloat16) for shape in full]
        + [
            pltpu.SemaphoreType.DMA((len(units), Gather.RECVS)),
            pltpu.SemaphoreType.DMA((len(units), Gather.RECVS)),
            pltpu.SemaphoreType.DMA((7,)),
        ],
        compiler_params=pltpu.CompilerParams(
            collective_id=0, has_side_effects=True, vmem_limit_bytes=VMEM_BYTES
        ),
        name="gather_weights",
    )(*shards)
    return [whole.reshape(-1, whole.shape[-1]) for whole in wholes]


class Reduce:
    SEMS = 12

    def __init__(self, place, grad, core, along_x, along_y, second_x, second_y, line, total, send, recv):
        self.p, self.g, self.rc = place, grad, core
        self.rx, self.ry, self.sx, self.sy, self.rz, self.f = along_x, along_y, second_x, second_y, line, total
        self.send, self.recv = send, recv
        self.rows = grad.shape[2]
        rows = self.rows
        p = place
        self.row = [half(i, rows) for i in (p.y, 1 - p.y)]
        self.col = [half(i, 768) for i in (p.x, 1 - p.x)]

    def _copy(self, k, src, dst, device):
        return remote(src, dst, self.send.at[k], self.recv.at[k], device)

    def _core(self):
        return self._copy(0, self.g.at[:, 1 - self.p.c], self.rc, self.p.core())

    def _first(self):
        p, low, high = self.p, pl.ds(0, 2), pl.ds(2, 2)
        return (
            self._copy(1, self.g.at[low, p.c, :, self.col[1]], self.rx, p.at_x()),
            self._copy(2, self.g.at[high, p.c, self.row[1], :], self.ry, p.at_y()),
        )

    def _second(self):
        p, low, high = self.p, pl.ds(0, 2), pl.ds(2, 2)
        return (
            self._copy(3, self.g.at[low, p.c, self.row[1], self.col[0]], self.sy, p.at_y()),
            self._copy(4, self.g.at[high, p.c, self.row[0], self.col[1]], self.sx, p.at_x()),
        )

    def _line(self):
        p = self.p
        return [
            self._copy(4 + d, self.g.at[p.up(d), p.c, self.row[0], self.col[0]], self.rz.at[d - 1], p.at_z(d))
            for d in (1, 2, 3)
        ]

    def _spread(self):
        p, part = self.p, self.f.at[self.row[0], self.col[0]]
        return [self._copy(8 + i, part, part, device) for i, device in enumerate((p.at_x(), p.at_y(), p.at_xy()))]

    def _add(self, ref, other):
        ref[...] = (ref[...].astype(jnp.float32) + other[...].astype(jnp.float32)).astype(jnp.bfloat16)

    def start(self):
        self._core().start()

    def first(self):
        p = self.p
        self._core().wait_recv()
        for i in range(4):
            self._add(self.g.at[i, p.c], self.rc.at[i])
        for copy in self._first():
            copy.start()

    def second(self):
        p = self.p
        along_x, along_y = self._first()
        along_x.wait_recv()
        for i in range(2):
            self._add(self.g.at[i, p.c, :, self.col[0]], self.rx.at[i])
        to_y, to_x = self._second()
        to_y.start()
        along_y.wait_recv()
        for i in range(2):
            self._add(self.g.at[2 + i, p.c, self.row[0], :], self.ry.at[i])
        to_x.start()

    def line(self):
        p = self.p
        for copy in self._second():
            copy.wait_recv()
        for i in range(2):
            self._add(self.g.at[i, p.c, self.row[0], self.col[0]], self.sy.at[i])
            self._add(self.g.at[2 + i, p.c, self.row[0], self.col[0]], self.sx.at[i])
        for copy in self._line():
            copy.start()

    def spread(self):
        p = self.p
        total = self.g[p.z, p.c, self.row[0], self.col[0]].astype(jnp.float32)
        for d, copy in enumerate(self._line()):
            copy.wait_recv()
            total = total + self.rz[d].astype(jnp.float32)
        self.f[self.row[0], self.col[0]] = total.astype(jnp.bfloat16)
        for copy in self._spread():
            copy.start()

    def arrive(self):
        for copy in self._spread():
            copy.wait_recv()

    def finish(self):
        for copy in (self._core(), *self._first(), *self._second(), *self._line(), *self._spread()):
            copy.wait_send()


def reduce_scratch(rows):
    shapes = [
        (4, rows, 768),
        (2, rows, 384),
        (2, rows // 2, 768),
        (2, rows // 2, 384),
        (2, rows // 2, 384),
        (3, rows // 2, 384),
        (rows, 768),
    ]
    return shapes


def reduce_kernel(counts, *refs):
    small, tall = counts
    grads, outs, refs = refs[:7], refs[7:14], refs[14:]
    held, refs = refs[:2], refs[2:]
    buffers, refs = (refs[:7], refs[7:14]), refs[14:]
    send, recv, local = refs
    place = Place()
    order = [(0, 0, 6, 0)]
    order += [(1, j, 5, j) for j in range(tall)]
    order += [(0, 1 + j, 4, j) for j in range(4)]
    order += [(0, 5, 3, 0), (0, 6, 2, 0), (0, 7, 0, 0), (0, 8, 1, 0)]
    loads, works, writes = [], [], []
    for u, (kind, slot, array, j) in enumerate(order):
        hold = held[kind].at[slot]
        if array == 5:
            src = grads[5].at[:, :, pl.ds(128 * j, 128), :]
            dst = outs[5].at[pl.ds(128 * j, 128), :]
        else:
            src = grads[array].at[:, :, :, pl.ds(768 * j, 768)]
            dst = outs[array].at[:, pl.ds(768 * j, 768)]
        loads.append(pltpu.make_async_copy(src, hold, local.at[u, 0]))
        parts = [b.at[slot] for b in buffers[kind]]
        works.append(Reduce(place, hold, *parts, send.at[u], recv.at[u]))
        writes.append(pltpu.make_async_copy(parts[-1], dst, local.at[u, 1]))
    for copy in loads:
        copy.start()
    place.greet()
    n = len(order)

    def begin(u):
        loads[u].wait()
        works[u].start()

    def end(u):
        works[u].arrive()
        writes[u].start()

    stages = (
        begin,
        lambda u: works[u].first(),
        lambda u: works[u].second(),
        lambda u: works[u].line(),
        lambda u: works[u].spread(),
        end,
    )
    for step in range(n + len(stages) - 1):
        for lag, stage in enumerate(stages):
            if 0 <= step - lag < n:
                stage(step - lag)
    for u in range(n):
        works[u].finish()
        writes[u].wait()


def reduce_all(grads):
    grads = [g.astype(jnp.bfloat16).reshape(4, 2, g.shape[0] // 8, g.shape[1]) for g in grads]
    small, tall = 9, 3
    scratch = [pltpu.VMEM((small, 4, 2, 96, 768), jnp.bfloat16), pltpu.VMEM((tall, 4, 2, 128, 768), jnp.bfloat16)]
    for count, rows in ((small, 96), (tall, 128)):
        scratch += [pltpu.VMEM((count,) + shape, jnp.bfloat16) for shape in reduce_scratch(rows)]
    n = small + tall
    return pl.pallas_call(
        partial(reduce_kernel, (small, tall)),
        out_shape=[jax.ShapeDtypeStruct(g.shape[2:], jnp.bfloat16) for g in grads],
        in_specs=[pl.BlockSpec(memory_space=pl.ANY)] * 7,
        out_specs=[pl.BlockSpec(memory_space=pl.ANY)] * 7,
        scratch_shapes=scratch
        + [
            pltpu.SemaphoreType.DMA((n, Reduce.SEMS)),
            pltpu.SemaphoreType.DMA((n, Reduce.SEMS)),
            pltpu.SemaphoreType.DMA((n, 2)),
        ],
        compiler_params=pltpu.CompilerParams(
            collective_id=1, has_side_effects=True, vmem_limit_bytes=VMEM_BYTES
        ),
        name="reduce_gradients",
    )(*grads)


def per_device(
    near,
    inputs,
    seg_ids,
    pool_index,
    w_query,
    w_key,
    w_value,
    w_out,
    w_up,
    w_down,
    w_proj,
    gain_attn,
    gain_ffn,
    gain_final,
    bias_table,
    emb_grad,
):
    rows, length, width = inputs.shape
    buckets, heads = bias_table.shape
    head_dim = width // heads
    tokens = rows * length
    head_shape = (rows, length, heads, head_dim)
    shards = (w_query, w_key, w_value, w_out, w_up, w_down, w_proj)
    gathered = gather_all(shards) if near else [lax.all_gather(w, "fsdp", axis=0, tiled=True) for w in shards]
    full_query, full_key, full_value, full_out, full_up, full_down, full_proj = gathered
    flat = inputs.reshape(tokens, width).astype(jnp.float32)
    normed_one, factor_one = rms_forward(flat, gain_attn)
    normed_one = normed_one.astype(jnp.bfloat16)
    queries = matmul(normed_one, full_query).astype(jnp.bfloat16).reshape(head_shape)
    key_rows = matmul(normed_one, full_key).astype(jnp.bfloat16).reshape(head_shape)
    value_rows = matmul(normed_one, full_value).astype(jnp.bfloat16).reshape(head_shape)
    bucket_ids = jnp.asarray(bucket_table(length, buckets, REACH))
    onehot_cols = (
        jnp.arange(buckets, dtype=jnp.int32)[:, None] == bucket_ids.reshape(1, length * length)
    ).astype(jnp.bfloat16)
    bias = jnp.dot(bias_table.T, onehot_cols.astype(jnp.float32), precision=HIGH).reshape(
        heads, length, length
    )

    def attend_row(pieces):
        query_row, key_row, value_row, seg_row = pieces
        scores = row_scores(query_row, key_row, seg_row, bias)
        row_peak = jnp.max(scores, axis=-1, keepdims=True)
        log_total = row_peak + jnp.log(jnp.sum(jnp.exp(scores - row_peak), axis=-1, keepdims=True))
        soft_low = jnp.exp(scores - log_total).astype(jnp.bfloat16)
        mixed = jnp.einsum("hqk,khd->qhd", soft_low, value_row, preferred_element_type=jnp.float32)
        return (mixed.astype(jnp.bfloat16), log_total)

    attended, log_totals = lax.map(attend_row, (queries, key_rows, value_rows, seg_ids))
    attended_flat = attended.reshape(tokens, width)
    hidden_one = flat + matmul(attended_flat, full_out)
    normed_two, factor_two = rms_forward(hidden_one, gain_ffn)
    normed_two = normed_two.astype(jnp.bfloat16)
    pre_act = matmul(normed_two, full_up)
    activated = jax.nn.gelu(pre_act, approximate=True).astype(jnp.bfloat16)
    hidden_two = hidden_one + matmul(activated, full_down)
    final_rows, factor_three = rms_forward(hidden_two, gain_final)
    member = (seg_ids[:, None, :] == pool_index[:, :, None]).astype(jnp.float32)
    counts = jnp.sum(member, axis=-1, keepdims=True)
    pooled = (
        jnp.einsum("rpl,rld->rpd", member, final_rows.reshape(rows, length, width), precision=HIGH)
        / counts
    )
    proj_full = full_proj.astype(jnp.float32)
    projected = jnp.einsum("rpd,de->rpe", pooled, proj_full, precision=HIGH)
    inverse_len = lax.rsqrt(jnp.sum(projected * projected, axis=-1, keepdims=True) + EPSILON)
    embeddings = projected * inverse_len
    emb_dot = jnp.sum(emb_grad * embeddings, axis=-1, keepdims=True)
    projected_grad = inverse_len * (emb_grad - embeddings * emb_dot)
    grad_proj = jnp.einsum("rpd,rpe->de", pooled, projected_grad, precision=HIGH)
    pooled_grad = jnp.einsum("rpe,de->rpd", projected_grad, proj_full, precision=HIGH) / counts
    final_grad = jnp.einsum("rpl,rpd->rld", member, pooled_grad, precision=HIGH).reshape(
        tokens, width
    )
    stream_two, grad_gain_final = rms_backward(hidden_two, factor_three, gain_final, final_grad)
    back_query, back_key, back_value, back_out, back_up, back_down, back_proj = gathered
    ffn_grad = stream_two.astype(jnp.bfloat16)
    grad_down = matmul_left(activated, ffn_grad)
    act_grad = matmul_right(ffn_grad, back_down)
    gelu_pullback = jax.vjp(partial(jax.nn.gelu, approximate=True), pre_act)[1]
    pre_grad = gelu_pullback(act_grad)[0].astype(jnp.bfloat16)
    grad_up = matmul_left(normed_two, pre_grad)
    normed_two_grad = matmul_right(pre_grad, back_up)
    stream_mid, grad_gain_ffn = rms_backward(hidden_one, factor_two, gain_ffn, normed_two_grad)
    stream_one = stream_two + stream_mid
    attn_grad = stream_one.astype(jnp.bfloat16)
    grad_out = matmul_left(attended_flat, attn_grad)
    mixed_grad = matmul_right(attn_grad, back_out).astype(jnp.bfloat16).reshape(head_shape)

    def attend_back(pieces):
        query_row, key_row, value_row, seg_row, log_total, upstream_row = pieces
        scores = row_scores(query_row, key_row, seg_row, bias)
        soft_rows = jnp.exp(scores - log_total)
        soft_grad = jnp.einsum(
            "qhd,khd->hqk", upstream_row, value_row, preferred_element_type=jnp.float32
        )
        score_grad = (
            soft_rows * (soft_grad - jnp.sum(soft_rows * soft_grad, axis=-1, keepdims=True))
        ).astype(jnp.bfloat16)
        query_grad = jnp.einsum(
            "hqk,khd->qhd", score_grad, key_row, preferred_element_type=jnp.float32
        ).astype(jnp.bfloat16)
        key_grad = jnp.einsum(
            "hqk,qhd->khd", score_grad, query_row, preferred_element_type=jnp.float32
        ).astype(jnp.bfloat16)
        value_grad = jnp.einsum(
            "hqk,qhd->khd",
            soft_rows.astype(jnp.bfloat16),
            upstream_row,
            preferred_element_type=jnp.float32,
        ).astype(jnp.bfloat16)
        table_grad = matmul_right(score_grad.reshape(heads, length * length), onehot_cols)
        return (query_grad, key_grad, value_grad, table_grad)

    query_grads, key_grads, value_grads, table_grads = lax.map(
        attend_back, (queries, key_rows, value_rows, seg_ids, log_totals, mixed_grad)
    )
    grad_table = jnp.sum(table_grads, axis=0).T
    query_flat = query_grads.reshape(tokens, width)
    key_flat = key_grads.reshape(tokens, width)
    value_flat = value_grads.reshape(tokens, width)
    grad_query = matmul_left(normed_one, query_flat)
    grad_key = matmul_left(normed_one, key_flat)
    grad_value = matmul_left(normed_one, value_flat)
    normed_one_grad = (
        matmul_right(query_flat, back_query)
        + matmul_right(key_flat, back_key)
        + matmul_right(value_flat, back_value)
    )
    stream_in, grad_gain_attn = rms_backward(flat, factor_one, gain_attn, normed_one_grad)
    input_grad = (stream_one + stream_in).reshape(rows, length, width)
    grads = (grad_query, grad_key, grad_value, grad_out, grad_up, grad_down, grad_proj)
    if near:
        summed = [shard.astype(jnp.float32) for shard in reduce_all(grads)]
    else:
        shards = [lax.psum_scatter(g, "fsdp", scatter_dimension=0, tiled=True) for g in grads]
        summed = [lax.psum(shard.astype(jnp.bfloat16), "dp").astype(jnp.float32) for shard in shards]
    smalls = lax.psum((grad_gain_attn, grad_gain_ffn, grad_gain_final, grad_table), ("dp", "fsdp"))
    return (
        embeddings,
        input_grad,
        summed[0],
        summed[1],
        summed[2],
        summed[3],
        summed[4],
        summed[5],
        summed[6],
        smalls[0],
        smalls[1],
        smalls[2],
        smalls[3],
    )


def solution(mesh):
    near = (mesh.shape["dp"], mesh.shape["fsdp"]) == (4, 8)
    return jax.shard_map(
        partial(per_device, near),
        mesh=mesh,
        in_specs=(
            P(("dp", "fsdp"), None, None),
            P(("dp", "fsdp"), None),
            P(("dp", "fsdp"), None),
            P("fsdp", None),
            P("fsdp", None),
            P("fsdp", None),
            P("fsdp", None),
            P("fsdp", None),
            P("fsdp", None),
            P("fsdp", None),
            P(),
            P(),
            P(),
            P(),
            P(("dp", "fsdp"), None, None),
        ),
        out_specs=(
            P(("dp", "fsdp"), None, None),
            P(("dp", "fsdp"), None, None),
            P("fsdp", None),
            P("fsdp", None),
            P("fsdp", None),
            P("fsdp", None),
            P("fsdp", None),
            P("fsdp", None),
            P("fsdp", None),
            P(),
            P(),
            P(),
            P(),
        ),
        check_vma=False,
    )
```

```python
import math
from functools import partial

import jax
import jax.numpy as jnp
import numpy as np
from jax import lax
from jax.experimental import pallas as pl
from jax.experimental.pallas import tpu as pltpu
from jax.sharding import PartitionSpec as P

REACH = 128


EPSILON = 1e-06
VMEM_BYTES = 60 * 2**20
HIGH = lax.Precision.HIGHEST


def bucket_table(length, buckets, reach):
    positions = np.arange(length)
    relative = positions[None, :] - positions[:, None]
    halfway = buckets // 2
    exact_span = halfway // 2
    distance = np.abs(relative)
    logged = exact_span + (
        np.log(np.maximum(distance, 1) / exact_span)
        / np.log(reach / exact_span)
        * (halfway - exact_span)
    ).astype(np.int64)
    logged = np.minimum(logged, halfway - 1)
    result = (relative > 0).astype(np.int64) * halfway + np.where(
        distance < exact_span, distance, logged
    )
    return result.astype(np.int32)


def rms_forward(values, gain):
    factor = lax.rsqrt(jnp.mean(values * values, axis=-1, keepdims=True) + EPSILON)
    return (values * factor * gain, factor)


def rms_backward(values, factor, gain, upstream):
    normed = values * factor
    gain_grad = jnp.sum(upstream * normed, axis=0)
    inner = upstream * gain
    return (factor * (inner - normed * jnp.mean(inner * normed, axis=-1, keepdims=True)), gain_grad)


def matmul(left, right):
    return jnp.dot(left, right, preferred_element_type=jnp.float32)


def matmul_left(left, right):
    return lax.dot_general(
        left, right, (((0,), (0,)), ((), ())), preferred_element_type=jnp.float32
    )


def matmul_right(left, right):
    return lax.dot_general(
        left, right, (((1,), (1,)), ((), ())), preferred_element_type=jnp.float32
    )


def row_scores(query_row, key_row, seg_row, bias):
    raw_scores = jnp.einsum("qhd,khd->hqk", query_row, key_row, preferred_element_type=jnp.float32)
    same_doc = (seg_row[:, None] == seg_row[None, :])[None]
    return jnp.where(same_doc, raw_scores + bias, -1e30)


MESH = pl.DeviceIdType.MESH
LANES = 128


class Place:
    def __init__(self):
        self.dp, self.fsdp = lax.axis_index("dp"), lax.axis_index("fsdp")
        self.y, self.x = self.dp // 2, self.dp % 2
        self.z, self.c = self.fsdp // 2, self.fsdp % 2

    def core(self):
        return (self.dp, self.z * 2 + (1 - self.c))

    def at_x(self):
        return (self.y * 2 + (1 - self.x), self.fsdp)

    def at_y(self):
        return ((1 - self.y) * 2 + self.x, self.fsdp)

    def at_xy(self):
        return ((1 - self.y) * 2 + (1 - self.x), self.fsdp)

    def up(self, d):
        return lax.rem(self.z + d, 4)

    def down(self, d):
        return lax.rem(self.z + 4 - d, 4)

    def at_z(self, d):
        return (self.dp, self.up(d) * 2 + self.c)

    def greet(self):
        barrier = pltpu.get_barrier_semaphore()
        partners = [self.core(), self.at_x(), self.at_y(), self.at_xy()]
        partners += [self.at_z(d) for d in (1, 2, 3)]
        for partner in partners:
            pl.semaphore_signal(barrier, inc=1, device_id=partner, device_id_type=MESH)
        pl.semaphore_wait(barrier, len(partners))


def remote(src, dst, send, recv, device):
    return pltpu.make_async_remote_copy(
        src_ref=src, dst_ref=dst, send_sem=send, recv_sem=recv, device_id=device, device_id_type=MESH
    )


def half(which, size, start=0):
    return pl.ds(pl.multiple_of(start + which * (size // 2), size // 2 if start % (size // 2) == 0 else 16), size // 2)


class Unit:
    def __init__(self, array, first, rows, left, wide):
        self.array, self.first, self.rows, self.left, self.wide = array, first, rows, left, wide

    def quarter(self, y, x):
        return (half(y, self.rows, self.first), half(x, self.wide, self.left))

    def whole(self):
        return (pl.ds(self.first, self.rows), pl.ds(self.left, self.wide))


class Gather:
    RECVS = 13

    def __init__(self, place, units, shards, wholes, send, recv):
        self.p, self.units, self.shards, self.wholes = place, units, shards, wholes
        self.send, self.recv = send, recv

    def _part(self, u, z, y, x):
        unit = self.units[u]
        return self.wholes[unit.array].at[(z, self.p.c) + unit.quarter(y, x)]

    def _z(self, u, d):
        p, unit = self.p, self.units[u]
        src = self.shards[unit.array].at[unit.quarter(p.y, p.x)]
        return remote(src, self._part(u, p.z, p.y, p.x), self.send.at[u, d - 1], self.recv.at[u, d - 1], p.at_z(d))

    def _hop(self, u, d, kind, y, x, device):
        ref = self._part(u, self.p.down(d), y, x)
        k = 3 * kind + d - 1
        return remote(ref, ref, self.send.at[u, k], self.recv.at[u, k], device)

    def _to_x(self, u, d):
        return self._hop(u, d, 1, self.p.y, self.p.x, self.p.at_x())

    def _to_y(self, u, d):
        return self._hop(u, d, 2, self.p.y, self.p.x, self.p.at_y())

    def _through_x(self, u, d):
        return (u + d) % 2 == 0

    def _diagonal(self, u, d):
        p = self.p
        if self._through_x(u, d):
            return self._hop(u, d, 3, p.y, 1 - p.x, p.at_y())
        return self._hop(u, d, 3, 1 - p.y, p.x, p.at_x())

    def _core(self, u):
        unit = self.units[u]
        ref = self.wholes[unit.array].at[(slice(None), self.p.c) + unit.whole()]
        return remote(ref, ref, self.send.at[u, 12], self.recv.at[u, 12], self.p.core())

    def start(self, u):
        for d in (1, 2, 3):
            self._z(u, d).start()

    def plane(self, u):
        for d in (1, 2, 3):
            self._z(u, d).wait_recv()
            self._to_x(u, d).start()
            self._to_y(u, d).start()

    def corner(self, u):
        for d in (1, 2, 3):
            first, second = (self._to_x, self._to_y) if self._through_x(u, d) else (self._to_y, self._to_x)
            first(u, d).wait_recv()
            self._diagonal(u, d).start()
            second(u, d).wait_recv()

    def pair(self, u):
        for d in (1, 2, 3):
            self._diagonal(u, d).wait_recv()
        self._core(u).start()

    def arrive(self, u):
        self._core(u).wait_recv()

    def finish(self, u):
        for d in (1, 2, 3):
            self._z(u, d).wait_send()
            self._to_x(u, d).wait_send()
            self._to_y(u, d).wait_send()
            self._diagonal(u, d).wait_send()
        self._core(u).wait_send()


def gather_units():
    small = [Unit(i, 0, 96, 0, 768) for i in range(4)]
    up = [Unit(4, 0, 96, 768 * j, 768) for j in range(4)]
    down = [Unit(5, 128 * j, 128, 0, 768) for j in range(3)]
    return small + up + [Unit(6, 0, 96, 0, 768)] + down


def gather_kernel(units, *refs):
    shards, outs, wholes = refs[:7], refs[7:14], refs[14:21]
    send, recv, local = refs[21:]
    place = Place()
    gather = Gather(place, units, shards, wholes, send, recv)
    own = [
        pltpu.make_async_copy(shard, whole.at[place.z, place.c], local.at[i])
        for i, (shard, whole) in enumerate(zip(shards, wholes))
    ]
    for copy in own:
        copy.start()
    place.greet()
    for u in range(len(units)):
        gather.start(u)
    for copy in own:
        copy.wait()
    stages = (gather.plane, gather.corner, gather.pair, gather.arrive)
    for step in range(len(units) + len(stages) - 1):
        for lag, stage in enumerate(stages):
            if 0 <= step - lag < len(units):
                stage(step - lag)
    back = [
        pltpu.make_async_copy(whole, out, local.at[i])
        for i, (whole, out) in enumerate(zip(wholes, outs))
    ]
    for copy in back:
        copy.start()
    for u in range(len(units)):
        gather.finish(u)
    for copy in back:
        copy.wait()


def gather_all(shards):
    units = gather_units()
    full = [(4, 2) + shard.shape for shard in shards]
    wholes = pl.pallas_call(
        partial(gather_kernel, units),
        out_shape=[jax.ShapeDtypeStruct(shape, jnp.bfloat16) for shape in full],
        in_specs=[pl.BlockSpec(memory_space=pl.ANY)] * 7,
        out_specs=[pl.BlockSpec(memory_space=pl.ANY)] * 7,
        scratch_shapes=[pltpu.VMEM(shape, jnp.bfloat16) for shape in full]
        + [
            pltpu.SemaphoreType.DMA((len(units), Gather.RECVS)),
            pltpu.SemaphoreType.DMA((len(units), Gather.RECVS)),
            pltpu.SemaphoreType.DMA((7,)),
        ],
        compiler_params=pltpu.CompilerParams(
            collective_id=0, has_side_effects=True, vmem_limit_bytes=VMEM_BYTES
        ),
        name="gather_weights",
    )(*shards)
    return [whole.reshape(-1, whole.shape[-1]) for whole in wholes]


class Reduce:
    SEMS = 12

    def __init__(self, place, grad, core, along_x, along_y, second_x, second_y, line, total, send, recv):
        self.p, self.g, self.rc = place, grad, core
        self.rx, self.ry, self.sx, self.sy, self.rz, self.f = along_x, along_y, second_x, second_y, line, total
        self.send, self.recv = send, recv
        self.rows = grad.shape[2]
        rows = self.rows
        p = place
        self.row = [half(i, rows) for i in (p.y, 1 - p.y)]
        self.col = [half(i, 768) for i in (p.x, 1 - p.x)]

    def _copy(self, k, src, dst, device):
        return remote(src, dst, self.send.at[k], self.recv.at[k], device)

    def _core(self):
        return self._copy(0, self.g.at[:, 1 - self.p.c], self.rc, self.p.core())

    def _first(self):
        p, low, high = self.p, pl.ds(0, 2), pl.ds(2, 2)
        return (
            self._copy(1, self.g.at[low, p.c, :, self.col[1]], self.rx, p.at_x()),
            self._copy(2, self.g.at[high, p.c, self.row[1], :], self.ry, p.at_y()),
        )

    def _second(self):
        p, low, high = self.p, pl.ds(0, 2), pl.ds(2, 2)
        return (
            self._copy(3, self.g.at[low, p.c, self.row[1], self.col[0]], self.sy, p.at_y()),
            self._copy(4, self.g.at[high, p.c, self.row[0], self.col[1]], self.sx, p.at_x()),
        )

    def _line(self):
        p = self.p
        return [
            self._copy(4 + d, self.g.at[p.up(d), p.c, self.row[0], self.col[0]], self.rz.at[d - 1], p.at_z(d))
            for d in (1, 2, 3)
        ]

    def _spread(self):
        p, part = self.p, self.f.at[self.row[0], self.col[0]]
        return [self._copy(8 + i, part, part, device) for i, device in enumerate((p.at_x(), p.at_y(), p.at_xy()))]

    def _add(self, ref, other):
        ref[...] = (ref[...].astype(jnp.float32) + other[...].astype(jnp.float32)).astype(jnp.bfloat16)

    def start(self):
        self._core().start()

    def first(self):
        p = self.p
        self._core().wait_recv()
        for i in range(4):
            self._add(self.g.at[i, p.c], self.rc.at[i])
        for copy in self._first():
            copy.start()

    def second(self):
        p = self.p
        along_x, along_y = self._first()
        along_x.wait_recv()
        for i in range(2):
            self._add(self.g.at[i, p.c, :, self.col[0]], self.rx.at[i])
        to_y, to_x = self._second()
        to_y.start()
        along_y.wait_recv()
        for i in range(2):
            self._add(self.g.at[2 + i, p.c, self.row[0], :], self.ry.at[i])
        to_x.start()

    def line(self):
        p = self.p
        for copy in self._second():
            copy.wait_recv()
        for i in range(2):
            self._add(self.g.at[i, p.c, self.row[0], self.col[0]], self.sy.at[i])
            self._add(self.g.at[2 + i, p.c, self.row[0], self.col[0]], self.sx.at[i])
        for copy in self._line():
            copy.start()

    def spread(self):
        p = self.p
        total = self.g[p.z, p.c, self.row[0], self.col[0]].astype(jnp.float32)
        for d, copy in enumerate(self._line()):
            copy.wait_recv()
            total = total + self.rz[d].astype(jnp.float32)
        self.f[self.row[0], self.col[0]] = total.astype(jnp.bfloat16)
        for copy in self._spread():
            copy.start()

    def arrive(self):
        for copy in self._spread():
            copy.wait_recv()

    def finish(self):
        for copy in (self._core(), *self._first(), *self._second(), *self._line(), *self._spread()):
            copy.wait_send()


def reduce_scratch(rows):
    shapes = [
        (4, rows, 768),
        (2, rows, 384),
        (2, rows // 2, 768),
        (2, rows // 2, 384),
        (2, rows // 2, 384),
        (3, rows // 2, 384),
        (rows, 768),
    ]
    return shapes


def reduce_kernel(counts, *refs):
    small, tall = counts
    grads, outs, refs = refs[:7], refs[7:14], refs[14:]
    held, refs = refs[:2], refs[2:]
    buffers, refs = (refs[:7], refs[7:14]), refs[14:]
    send, recv, local = refs
    place = Place()
    order = [(0, 0, 6, 0)]
    order += [(1, j, 5, j) for j in range(tall)]
    order += [(0, 1 + j, 4, j) for j in range(4)]
    order += [(0, 5, 3, 0), (0, 6, 2, 0), (0, 7, 0, 0), (0, 8, 1, 0)]
    loads, works, writes = [], [], []
    for u, (kind, slot, array, j) in enumerate(order):
        hold = held[kind].at[slot]
        if array == 5:
            src = grads[5].at[:, :, pl.ds(128 * j, 128), :]
            dst = outs[5].at[pl.ds(128 * j, 128), :]
        else:
            src = grads[array].at[:, :, :, pl.ds(768 * j, 768)]
            dst = outs[array].at[:, pl.ds(768 * j, 768)]
        loads.append(pltpu.make_async_copy(src, hold, local.at[u, 0]))
        parts = [b.at[slot] for b in buffers[kind]]
        works.append(Reduce(place, hold, *parts, send.at[u], recv.at[u]))
        writes.append(pltpu.make_async_copy(parts[-1], dst, local.at[u, 1]))
    for copy in loads:
        copy.start()
    place.greet()
    n = len(order)

    def begin(u):
        loads[u].wait()
        works[u].start()

    def end(u):
        works[u].arrive()
        writes[u].start()

    stages = (
        begin,
        lambda u: works[u].first(),
        lambda u: works[u].second(),
        lambda u: works[u].line(),
        lambda u: works[u].spread(),
        end,
    )
    for step in range(n + len(stages) - 1):
        for lag, stage in enumerate(stages):
            if 0 <= step - lag < n:
                stage(step - lag)
    for u in range(n):
        works[u].finish()
        writes[u].wait()


def reduce_all(grads):
    grads = [g.astype(jnp.bfloat16).reshape(4, 2, g.shape[0] // 8, g.shape[1]) for g in grads]
    small, tall = 9, 3
    scratch = [pltpu.VMEM((small, 4, 2, 96, 768), jnp.bfloat16), pltpu.VMEM((tall, 4, 2, 128, 768), jnp.bfloat16)]
    for count, rows in ((small, 96), (tall, 128)):
        scratch += [pltpu.VMEM((count,) + shape, jnp.bfloat16) for shape in reduce_scratch(rows)]
    n = small + tall
    return pl.pallas_call(
        partial(reduce_kernel, (small, tall)),
        out_shape=[jax.ShapeDtypeStruct(g.shape[2:], jnp.bfloat16) for g in grads],
        in_specs=[pl.BlockSpec(memory_space=pl.ANY)] * 7,
        out_specs=[pl.BlockSpec(memory_space=pl.ANY)] * 7,
        scratch_shapes=scratch
        + [
            pltpu.SemaphoreType.DMA((n, Reduce.SEMS)),
            pltpu.SemaphoreType.DMA((n, Reduce.SEMS)),
            pltpu.SemaphoreType.DMA((n, 2)),
        ],
        compiler_params=pltpu.CompilerParams(
            collective_id=1, has_side_effects=True, vmem_limit_bytes=VMEM_BYTES
        ),
        name="reduce_gradients",
    )(*grads)


def dot(a, b, ca=1, cb=0):
    return lax.dot_general(a, b, (((ca,), (cb,)), ((), ())), preferred_element_type=jnp.float32)


def dot_exact(a, b, ca=1, cb=0):
    return lax.dot_general(
        a, b, (((ca,), (cb,)), ((), ())), precision=HIGH, preferred_element_type=jnp.float32
    )


def low(v):
    return v.astype(jnp.bfloat16)


def wide(v):
    return v.astype(jnp.float32)


def two_parts(v):
    high = wide(low(v))
    return low(jnp.concatenate([high, v - high], axis=0))


def norm_factor(v):
    return lax.rsqrt(jnp.mean(v * v, axis=-1, keepdims=True) + EPSILON)


def norm_back(v, factor, gain, upstream):
    normed = v * factor
    inner = upstream * gain
    grad = factor * (inner - normed * jnp.mean(inner * normed, axis=-1, keepdims=True))
    return grad, jnp.sum(upstream * normed, axis=0, keepdims=True)


def gelu_both(v):
    scale = math.sqrt(2.0 / math.pi)
    square = v * v
    bent = jnp.tanh(scale * v * (1.0 + 0.044715 * square))
    share = 0.5 + 0.5 * bent
    slope = share + (0.5 * scale) * v * (1.0 - bent * bent) * (1.0 + (3 * 0.044715) * square)
    return v * share, slope


def flat(ref, *where):
    value = ref[where] if where else ref[...]
    return value.reshape(-1, value.shape[-1])


TILE, SPAN = 128, 384


def rows_of(t):
    return pl.ds(t * TILE, TILE)


def span_of(t):
    return pl.ds(t * TILE, SPAN)


def heads_of(p):
    return pl.ds(pl.multiple_of(p * LANES, LANES), LANES)


def stacked(v, axis=0):
    first = lax.broadcasted_iota(jnp.int32, v.shape, 1) < LANES // 2
    zero = jnp.zeros_like(v)
    return jnp.concatenate([jnp.where(first, v, zero), jnp.where(first, zero, v)], axis=axis)


def side_by_side(v):
    return jnp.concatenate([v[:TILE], v[TILE:]], axis=1)


def probs_at(p, t):
    return (pl.ds(pl.multiple_of((p // 2) * 256, 256), 256), pl.ds(pl.multiple_of((p % 2) * 1536, 1536) + t * SPAN, SPAN))


def attend(p, t, q, keys, values, band, mask, probs, mixed):
    scores = dot(stacked(q[rows_of(t), heads_of(p)]), keys[span_of(t), heads_of(p)], 1, 1)
    hidden = mask[t]
    scores = scores + band[p] + jnp.concatenate([hidden, hidden], axis=0)
    powered = jnp.exp(scores - jnp.max(scores, axis=1, keepdims=True))
    soft = low(powered * (1.0 / jnp.sum(powered, axis=1, keepdims=True)))
    probs[probs_at(p, t)] = soft
    out = dot(side_by_side(soft), stacked(values[span_of(t), heads_of(p)]))
    mixed[rows_of(t), heads_of(p)] = low(out)


def forward_kernel(units, *refs):
    x_ref, seg_ref, pool_ref, emb_ref, g1_ref, g2_ref, g3_ref, table_ref, near_ref = refs[:9]
    shards, refs = refs[9:16], refs[16:]
    w_outs, big_outs, small_outs, refs = refs[:6], refs[6:17], refs[17:21], refs[21:]
    wholes, refs = refs[:7], refs[7:]
    held, refs = refs[:10], refs[10:]
    act, slope, n1, n2, mixed, q, keys, values, probs, h1 = held
    h2, band, mask = refs[:3]
    send, recv, local, ready = refs[3:]
    emb_out, pooled_out, eg_out, top_out = small_outs
    wq, wk, wv, wo, wup, wdn, wpj = wholes
    place = Place()
    gather = Gather(place, units, shards, wholes, send, recv)
    own = [
        pltpu.make_async_copy(shard, whole.at[place.z, place.c], local.at[i])
        for i, (shard, whole) in enumerate(zip(shards, wholes))
    ]
    backs = [pltpu.make_async_copy(a, b, local.at[7 + i]) for i, (a, b) in enumerate(zip(wholes[:6], w_outs))]
    keeps = [pltpu.make_async_copy(a, b, ready.at[i]) for i, (a, b) in enumerate(zip(held, big_outs))]
    for copy in own:
        copy.start()
    place.greet()
    n = len(units)
    stages = (gather.plane, gather.corner, gather.pair, gather.arrive)

    def step(t):
        for lag, stage in enumerate(stages):
            if 0 <= t - lag < n:
                stage(t - lag)
                if lag == 0 and t + 2 < n:
                    gather.start(t + 2)

    for u in range(2):
        gather.start(u)
    for copy in own:
        copy.wait()

    x = wide(x_ref[...])
    n1[...] = low(x * norm_factor(x) * g1_ref[...])
    step(0)
    ray = dot_exact(table_ref[...], near_ref[...], 0, 0)
    for h in range(ray.shape[0]):
        rolled = pltpu.roll(jnp.broadcast_to(ray[h : h + 1], (TILE, 512)), 0, 1, stride=1, stride_axis=0)
        band[h // 2, pl.ds((h % 2) * TILE, TILE), :] = rolled[:, :SPAN]
    step(1)
    seg = seg_ref[...]
    seg_f = wide(seg)
    column = jnp.transpose(jnp.broadcast_to(seg_f, (TILE, 512)))
    edge = jnp.full((1, TILE), -1.0, jnp.float32)
    line = jnp.concatenate([edge, seg_f, edge], axis=1)
    for t in range(4):
        own_seg = column[t * TILE : (t + 1) * TILE]
        same = jnp.concatenate([own_seg] * 3, axis=1) == line[:, t * TILE : t * TILE + SPAN]
        mask[t] = jnp.where(same, 0.0, -1e30)
    blank = jnp.zeros((TILE, 768), jnp.bfloat16)
    for ref in (keys, values):
        ref[pl.ds(0, TILE), :] = blank
        ref[pl.ds(640, TILE), :] = blank
    step(2)
    step(3)
    q[...] = low(dot(n1[...], flat(wq)))
    backs[0].start()
    step(4)
    keys[pl.ds(TILE, 512), :] = low(dot(n1[...], flat(wk)))
    backs[1].start()
    step(5)
    values[pl.ds(TILE, 512), :] = low(dot(n1[...], flat(wv)))
    backs[2].start()
    for i in (2, 5, 6, 7):
        keeps[i].start()

    def pairs(first, last):
        @pl.loop(first, last)
        def _(p):
            for t in range(4):
                attend(p, t, q, keys, values, band, mask, probs, mixed)

    pairs(0, 2)
    step(6)
    pairs(2, 4)
    step(7)
    pairs(4, 6)
    backs[3].start()
    keeps[8].start()
    keeps[4].start()
    hidden = wide(x_ref[...]) + dot(mixed[...], flat(wo))
    h1[...] = hidden
    n2[...] = low(hidden * norm_factor(hidden) * g2_ref[...])
    keeps[3].start()
    keeps[9].start()
    for j in range(4):
        cols = pl.ds(768 * j, 768)
        value, grad = gelu_both(dot(n2[...], flat(wup, slice(None), slice(None), slice(None), cols)))
        act[:, cols] = low(value)
        slope[:, cols] = low(grad)
        step(8 + j)
    backs[4].start()
    keeps[0].start()
    keeps[1].start()
    for j in range(3):
        step(12 + j)
        part = jnp.concatenate([act[:, pl.ds(384 * s + 128 * j, 128)] for s in range(8)], axis=1)
        more = dot(part, flat(wdn, slice(None), slice(None), pl.ds(128 * j, 128)))
        h2[...] = (h1[...] if j == 0 else h2[...]) + more
    backs[5].start()
    h = h2[...]
    factor = norm_factor(h)
    fin = h * factor * g3_ref[...]
    eye = lax.broadcasted_iota(jnp.int32, (8, 8), 0) == lax.broadcasted_iota(jnp.int32, (8, 8), 1)
    pool = jnp.sum(jnp.where(eye, wide(pool_ref[...]), 0.0), axis=1, keepdims=True)
    member = jnp.where(seg_f == pool, 1.0, 0.0)
    count = jnp.sum(member, axis=1, keepdims=True)
    fin_high = low(fin)
    pooled = (dot(low(member), fin_high) + dot(low(member), low(fin - wide(fin_high)))) / count
    wp = flat(wpj)
    both = dot(two_parts(pooled), wp)
    projected = both[:8] + both[8:]
    inverse = lax.rsqrt(jnp.sum(projected * projected, axis=-1, keepdims=True) + EPSILON)
    emb = projected * inverse
    up = emb_ref[...].reshape(8, 768)
    eg = inverse * (up - emb * jnp.sum(up * emb, axis=-1, keepdims=True))
    both = dot(two_parts(eg), wp, 1, 1)
    pooled_grad = (both[:8] + both[8:]) / count
    twice = low(jnp.concatenate([member, member], axis=0))
    fin_grad = dot(twice, two_parts(pooled_grad), 0, 0)
    stream, gain_grad = norm_back(h, factor, g3_ref[...], fin_grad)
    emb_out[...] = emb
    pooled_out[...] = pooled
    eg_out[...] = eg
    h2[...] = stream
    top_out[...] = gain_grad
    last = pltpu.make_async_copy(h2, big_outs[10], ready.at[10])
    last.start()
    for u in range(n):
        gather.finish(u)
    for copy in (*backs, *keeps, last):
        copy.wait()


def ray_buckets(buckets):
    near = np.arange(512)
    away = np.where(near < SPAN, near - TILE, near - 512 - TILE)
    halfway = buckets // 2
    exact = halfway // 2
    distance = np.abs(away)
    logged = exact + (
        np.log(np.maximum(distance, 1) / exact) / np.log(REACH / exact) * (halfway - exact)
    ).astype(np.int64)
    bucket = (away > 0) * halfway + np.where(distance < exact, distance, np.minimum(logged, halfway - 1))
    return (np.arange(buckets)[:, None] == bucket[None, :]).astype(np.float32)


def forward_all(x, seg_ids, pool_index, emb_grad, gains, table, shards):
    units = gather_units()
    full = [(4, 2) + shard.shape for shard in shards]
    low_shapes = [(512, 3072)] * 2 + [(512, 768)] * 4 + [(768, 768)] * 2 + [(768, 3072)]
    held = [jax.ShapeDtypeStruct(s, jnp.bfloat16) for s in low_shapes]
    held.append(jax.ShapeDtypeStruct((512, 768), jnp.float32))
    outs = [jax.ShapeDtypeStruct(s, jnp.bfloat16) for s in full[:6]]
    outs += held + [jax.ShapeDtypeStruct((512, 768), jnp.float32)]
    n_large = len(outs)
    outs += [jax.ShapeDtypeStruct((8, 768), jnp.float32)] * 3 + [jax.ShapeDtypeStruct((1, 768), jnp.float32)]
    vmem, large = pl.BlockSpec(memory_space=pltpu.VMEM), pl.BlockSpec(memory_space=pl.ANY)
    return pl.pallas_call(
        partial(forward_kernel, units),
        out_shape=outs,
        in_specs=[vmem] * 9 + [large] * 7,
        out_specs=[large] * n_large + [vmem] * 4,
        scratch_shapes=[pltpu.VMEM(shape, jnp.bfloat16) for shape in full]
        + [pltpu.VMEM(h.shape, h.dtype) for h in held]
        + [
            pltpu.VMEM((512, 768), jnp.float32),
            pltpu.VMEM((6, 2 * TILE, SPAN), jnp.float32),
            pltpu.VMEM((4, TILE, SPAN), jnp.float32),
            pltpu.SemaphoreType.DMA((len(units), Gather.RECVS)),
            pltpu.SemaphoreType.DMA((len(units), Gather.RECVS)),
            pltpu.SemaphoreType.DMA((13,)),
            pltpu.SemaphoreType.DMA((11,)),
        ],
        compiler_params=pltpu.CompilerParams(
            collective_id=0, has_side_effects=True, vmem_limit_bytes=VMEM_BYTES
        ),
        name="forward",
    )(x, seg_ids, pool_index, emb_grad, *gains, table, ray_buckets(table.shape[0]), *shards)


def general(
    inputs,
    seg_ids,
    pool_index,
    w_query,
    w_key,
    w_value,
    w_out,
    w_up,
    w_down,
    w_proj,
    gain_attn,
    gain_ffn,
    gain_final,
    bias_table,
    emb_grad,
):
    rows, length, width = inputs.shape
    buckets, heads = bias_table.shape
    head_dim = width // heads
    tokens = rows * length
    head_shape = (rows, length, heads, head_dim)
    gathered = (
        lax.all_gather(w_query, "fsdp", axis=0, tiled=True),
        lax.all_gather(w_key, "fsdp", axis=0, tiled=True),
        lax.all_gather(w_value, "fsdp", axis=0, tiled=True),
        lax.all_gather(w_out, "fsdp", axis=0, tiled=True),
        lax.all_gather(w_up, "fsdp", axis=0, tiled=True),
        lax.all_gather(w_down, "fsdp", axis=0, tiled=True),
        lax.all_gather(w_proj, "fsdp", axis=0, tiled=True),
    )
    full_query, full_key, full_value, full_out, full_up, full_down, full_proj = gathered
    flat = inputs.reshape(tokens, width).astype(jnp.float32)
    normed_one, factor_one = rms_forward(flat, gain_attn)
    normed_one = normed_one.astype(jnp.bfloat16)
    queries = matmul(normed_one, full_query).astype(jnp.bfloat16).reshape(head_shape)
    key_rows = matmul(normed_one, full_key).astype(jnp.bfloat16).reshape(head_shape)
    value_rows = matmul(normed_one, full_value).astype(jnp.bfloat16).reshape(head_shape)
    bucket_ids = jnp.asarray(bucket_table(length, buckets, REACH))
    onehot_cols = (
        jnp.arange(buckets, dtype=jnp.int32)[:, None] == bucket_ids.reshape(1, length * length)
    ).astype(jnp.bfloat16)
    bias = jnp.dot(bias_table.T, onehot_cols.astype(jnp.float32), precision=HIGH).reshape(
        heads, length, length
    )

    def attend_row(pieces):
        query_row, key_row, value_row, seg_row = pieces
        scores = row_scores(query_row, key_row, seg_row, bias)
        row_peak = jnp.max(scores, axis=-1, keepdims=True)
        log_total = row_peak + jnp.log(jnp.sum(jnp.exp(scores - row_peak), axis=-1, keepdims=True))
        soft_low = jnp.exp(scores - log_total).astype(jnp.bfloat16)
        mixed = jnp.einsum("hqk,khd->qhd", soft_low, value_row, preferred_element_type=jnp.float32)
        return (mixed.astype(jnp.bfloat16), log_total)

    attended, log_totals = lax.map(attend_row, (queries, key_rows, value_rows, seg_ids))
    attended_flat = attended.reshape(tokens, width)
    hidden_one = flat + matmul(attended_flat, full_out)
    normed_two, factor_two = rms_forward(hidden_one, gain_ffn)
    normed_two = normed_two.astype(jnp.bfloat16)
    pre_act = matmul(normed_two, full_up)
    activated = jax.nn.gelu(pre_act, approximate=True).astype(jnp.bfloat16)
    hidden_two = hidden_one + matmul(activated, full_down)
    final_rows, factor_three = rms_forward(hidden_two, gain_final)
    member = (seg_ids[:, None, :] == pool_index[:, :, None]).astype(jnp.float32)
    counts = jnp.sum(member, axis=-1, keepdims=True)
    pooled = (
        jnp.einsum("rpl,rld->rpd", member, final_rows.reshape(rows, length, width), precision=HIGH)
        / counts
    )
    proj_full = full_proj.astype(jnp.float32)
    projected = jnp.einsum("rpd,de->rpe", pooled, proj_full, precision=HIGH)
    inverse_len = lax.rsqrt(jnp.sum(projected * projected, axis=-1, keepdims=True) + EPSILON)
    embeddings = projected * inverse_len
    emb_dot = jnp.sum(emb_grad * embeddings, axis=-1, keepdims=True)
    projected_grad = inverse_len * (emb_grad - embeddings * emb_dot)
    grad_proj = jnp.einsum("rpd,rpe->de", pooled, projected_grad, precision=HIGH)
    pooled_grad = jnp.einsum("rpe,de->rpd", projected_grad, proj_full, precision=HIGH) / counts
    final_grad = jnp.einsum("rpl,rpd->rld", member, pooled_grad, precision=HIGH).reshape(
        tokens, width
    )
    stream_two, grad_gain_final = rms_backward(hidden_two, factor_three, gain_final, final_grad)
    back_weights = (
        lax.all_gather(w_query, "fsdp", axis=0, tiled=True),
        lax.all_gather(w_key, "fsdp", axis=0, tiled=True),
        lax.all_gather(w_value, "fsdp", axis=0, tiled=True),
        lax.all_gather(w_out, "fsdp", axis=0, tiled=True),
        lax.all_gather(w_up, "fsdp", axis=0, tiled=True),
        lax.all_gather(w_down, "fsdp", axis=0, tiled=True),
        lax.all_gather(w_proj, "fsdp", axis=0, tiled=True),
    )
    back_query, back_key, back_value, back_out, back_up, back_down, back_proj = back_weights
    ffn_grad = stream_two.astype(jnp.bfloat16)
    grad_down = matmul_left(activated, ffn_grad)
    act_grad = matmul_right(ffn_grad, back_down)
    gelu_pullback = jax.vjp(partial(jax.nn.gelu, approximate=True), pre_act)[1]
    pre_grad = gelu_pullback(act_grad)[0].astype(jnp.bfloat16)
    grad_up = matmul_left(normed_two, pre_grad)
    normed_two_grad = matmul_right(pre_grad, back_up)
    stream_mid, grad_gain_ffn = rms_backward(hidden_one, factor_two, gain_ffn, normed_two_grad)
    stream_one = stream_two + stream_mid
    attn_grad = stream_one.astype(jnp.bfloat16)
    grad_out = matmul_left(attended_flat, attn_grad)
    mixed_grad = matmul_right(attn_grad, back_out).astype(jnp.bfloat16).reshape(head_shape)

    def attend_back(pieces):
        query_row, key_row, value_row, seg_row, log_total, upstream_row = pieces
        scores = row_scores(query_row, key_row, seg_row, bias)
        soft_rows = jnp.exp(scores - log_total)
        soft_grad = jnp.einsum(
            "qhd,khd->hqk", upstream_row, value_row, preferred_element_type=jnp.float32
        )
        score_grad = (
            soft_rows * (soft_grad - jnp.sum(soft_rows * soft_grad, axis=-1, keepdims=True))
        ).astype(jnp.bfloat16)
        query_grad = jnp.einsum(
            "hqk,khd->qhd", score_grad, key_row, preferred_element_type=jnp.float32
        ).astype(jnp.bfloat16)
        key_grad = jnp.einsum(
            "hqk,qhd->khd", score_grad, query_row, preferred_element_type=jnp.float32
        ).astype(jnp.bfloat16)
        value_grad = jnp.einsum(
            "hqk,qhd->khd",
            soft_rows.astype(jnp.bfloat16),
            upstream_row,
            preferred_element_type=jnp.float32,
        ).astype(jnp.bfloat16)
        table_grad = matmul_right(score_grad.reshape(heads, length * length), onehot_cols)
        return (query_grad, key_grad, value_grad, table_grad)

    query_grads, key_grads, value_grads, table_grads = lax.map(
        attend_back, (queries, key_rows, value_rows, seg_ids, log_totals, mixed_grad)
    )
    grad_table = jnp.sum(table_grads, axis=0).T
    query_flat = query_grads.reshape(tokens, width)
    key_flat = key_grads.reshape(tokens, width)
    value_flat = value_grads.reshape(tokens, width)
    grad_query = matmul_left(normed_one, query_flat)
    grad_key = matmul_left(normed_one, key_flat)
    grad_value = matmul_left(normed_one, value_flat)
    normed_one_grad = (
        matmul_right(query_flat, back_query)
        + matmul_right(key_flat, back_key)
        + matmul_right(value_flat, back_value)
    )
    stream_in, grad_gain_attn = rms_backward(flat, factor_one, gain_attn, normed_one_grad)
    input_grad = (stream_one + stream_in).reshape(rows, length, width)
    shard_query, shard_key, shard_value, shard_out, shard_up, shard_down, shard_proj = (
        lax.psum_scatter(grad_query, "fsdp", scatter_dimension=0, tiled=True),
        lax.psum_scatter(grad_key, "fsdp", scatter_dimension=0, tiled=True),
        lax.psum_scatter(grad_value, "fsdp", scatter_dimension=0, tiled=True),
        lax.psum_scatter(grad_out, "fsdp", scatter_dimension=0, tiled=True),
        lax.psum_scatter(grad_up, "fsdp", scatter_dimension=0, tiled=True),
        lax.psum_scatter(grad_down, "fsdp", scatter_dimension=0, tiled=True),
        lax.psum_scatter(grad_proj, "fsdp", scatter_dimension=0, tiled=True),
    )
    summed = (
        lax.psum(shard_query.astype(jnp.bfloat16), "dp").astype(jnp.float32),
        lax.psum(shard_key.astype(jnp.bfloat16), "dp").astype(jnp.float32),
        lax.psum(shard_value.astype(jnp.bfloat16), "dp").astype(jnp.float32),
        lax.psum(shard_out.astype(jnp.bfloat16), "dp").astype(jnp.float32),
        lax.psum(shard_up.astype(jnp.bfloat16), "dp").astype(jnp.float32),
        lax.psum(shard_down.astype(jnp.bfloat16), "dp").astype(jnp.float32),
        lax.psum(shard_proj.astype(jnp.bfloat16), "dp").astype(jnp.float32),
    )
    smalls = lax.psum((grad_gain_attn, grad_gain_ffn, grad_gain_final, grad_table), ("dp", "fsdp"))
    return (
        embeddings,
        input_grad,
        summed[0],
        summed[1],
        summed[2],
        summed[3],
        summed[4],
        summed[5],
        summed[6],
        smalls[0],
        smalls[1],
        smalls[2],
        smalls[3],
    )


def near_device(
    inputs,
    seg_ids,
    pool_index,
    w_query,
    w_key,
    w_value,
    w_out,
    w_up,
    w_down,
    w_proj,
    gain_attn,
    gain_ffn,
    gain_final,
    bias_table,
    emb_grad,
):
    rows, length, width = inputs.shape
    buckets, heads = bias_table.shape
    head_dim = width // heads
    tokens = rows * length
    shards = (w_query, w_key, w_value, w_out, w_up, w_down, w_proj)
    gains = (gain_attn, gain_ffn, gain_final)
    done = forward_all(
        inputs.reshape(tokens, width), seg_ids, pool_index, emb_grad, [g.reshape(1, width) for g in gains], bias_table, shards
    )
    wholes = [w.reshape(-1, w.shape[-1]) for w in done[:6]]
    back_query, back_key, back_value, back_out, back_up, back_down = wholes
    activated, slope, normed_one, normed_two, attended_flat, queries, keys, values, probs, hidden_one, stream_two = done[6:17]
    embeddings, pooled, projected_grad, grad_gain_final = done[17:]
    flat = inputs.reshape(tokens, width).astype(jnp.float32)
    head_shape = (rows, length, heads, head_dim)
    queries = queries.reshape(head_shape)
    key_rows = keys[128:640].reshape(head_shape)
    value_rows = values[128:640].reshape(head_shape)
    bucket_ids = jnp.asarray(bucket_table(length, buckets, REACH))
    onehot_cols = (
        jnp.arange(buckets, dtype=jnp.int32)[:, None] == bucket_ids.reshape(1, length * length)
    ).astype(jnp.bfloat16)
    bias = jnp.dot(bias_table.T, onehot_cols.astype(jnp.float32), precision=HIGH).reshape(
        heads, length, length
    )
    grad_proj = jnp.einsum("pd,pe->de", pooled, projected_grad, precision=HIGH)
    ffn_grad = stream_two.astype(jnp.bfloat16)
    grad_down = matmul_left(activated, ffn_grad)
    act_grad = matmul_right(ffn_grad, back_down)
    pre_grad = (act_grad * slope.astype(jnp.float32)).astype(jnp.bfloat16)
    grad_up = matmul_left(normed_two, pre_grad)
    normed_two_grad = matmul_right(pre_grad, back_up)
    factor_two = norm_factor(hidden_one)
    stream_mid, grad_gain_ffn = rms_backward(hidden_one, factor_two, gain_ffn, normed_two_grad)
    stream_one = stream_two + stream_mid
    attn_grad = stream_one.astype(jnp.bfloat16)
    grad_out = matmul_left(attended_flat, attn_grad)
    mixed_grad = matmul_right(attn_grad, back_out).astype(jnp.bfloat16).reshape(head_shape)

    def attend_back(pieces):
        query_row, key_row, value_row, seg_row, upstream_row = pieces
        scores = row_scores(query_row, key_row, seg_row, bias)
        soft_rows = jnp.exp(scores - jnp.max(scores, axis=-1, keepdims=True))
        soft_rows = soft_rows / jnp.sum(soft_rows, axis=-1, keepdims=True)
        soft_grad = jnp.einsum(
            "qhd,khd->hqk", upstream_row, value_row, preferred_element_type=jnp.float32
        )
        score_grad = (
            soft_rows * (soft_grad - jnp.sum(soft_rows * soft_grad, axis=-1, keepdims=True))
        ).astype(jnp.bfloat16)
        query_grad = jnp.einsum(
            "hqk,khd->qhd", score_grad, key_row, preferred_element_type=jnp.float32
        ).astype(jnp.bfloat16)
        key_grad = jnp.einsum(
            "hqk,qhd->khd", score_grad, query_row, preferred_element_type=jnp.float32
        ).astype(jnp.bfloat16)
        value_grad = jnp.einsum(
            "hqk,qhd->khd",
            soft_rows.astype(jnp.bfloat16),
            upstream_row,
            preferred_element_type=jnp.float32,
        ).astype(jnp.bfloat16)
        table_grad = matmul_right(score_grad.reshape(heads, length * length), onehot_cols)
        return (query_grad, key_grad, value_grad, table_grad)

    query_grads, key_grads, value_grads, table_grads = lax.map(
        attend_back, (queries, key_rows, value_rows, seg_ids, mixed_grad)
    )
    grad_table = jnp.sum(table_grads, axis=0).T
    query_flat = query_grads.reshape(tokens, width)
    key_flat = key_grads.reshape(tokens, width)
    value_flat = value_grads.reshape(tokens, width)
    grad_query = matmul_left(normed_one, query_flat)
    grad_key = matmul_left(normed_one, key_flat)
    grad_value = matmul_left(normed_one, value_flat)
    normed_one_grad = (
        matmul_right(query_flat, back_query)
        + matmul_right(key_flat, back_key)
        + matmul_right(value_flat, back_value)
    )
    stream_in, grad_gain_attn = rms_backward(flat, norm_factor(flat), gain_attn, normed_one_grad)
    input_grad = (stream_one + stream_in).reshape(rows, length, width)
    grads = (grad_query, grad_key, grad_value, grad_out, grad_up, grad_down, grad_proj)
    summed = [shard.astype(jnp.float32) for shard in reduce_all(grads)]
    grad_gain_final = grad_gain_final[0]
    smalls = lax.psum((grad_gain_attn, grad_gain_ffn, grad_gain_final, grad_table), ("dp", "fsdp"))
    return (
        embeddings.reshape(rows, -1, width),
        input_grad,
        summed[0],
        summed[1],
        summed[2],
        summed[3],
        summed[4],
        summed[5],
        summed[6],
        smalls[0],
        smalls[1],
        smalls[2],
        smalls[3],
    )


def solution(mesh):
    near = (mesh.shape["dp"], mesh.shape["fsdp"]) == (4, 8)
    return jax.shard_map(
        near_device if near else general,
        mesh=mesh,
        in_specs=(
            P(("dp", "fsdp"), None, None),
            P(("dp", "fsdp"), None),
            P(("dp", "fsdp"), None),
            P("fsdp", None),
            P("fsdp", None),
            P("fsdp", None),
            P("fsdp", None),
            P("fsdp", None),
            P("fsdp", None),
            P("fsdp", None),
            P(),
            P(),
            P(),
            P(),
            P(("dp", "fsdp"), None, None),
        ),
        out_specs=(
            P(("dp", "fsdp"), None, None),
            P(("dp", "fsdp"), None, None),
            P("fsdp", None),
            P("fsdp", None),
            P("fsdp", None),
            P("fsdp", None),
            P("fsdp", None),
            P("fsdp", None),
            P("fsdp", None),
            P(),
            P(),
            P(),
            P(),
        ),
        check_vma=False,
    )
```

```python
import math
from functools import partial

import jax
import jax.numpy as jnp
import numpy as np
from jax import lax
from jax.experimental import pallas as pl
from jax.experimental.pallas import tpu as pltpu
from jax.sharding import PartitionSpec as P

REACH = 128


EPSILON = 1e-06
VMEM_BYTES = 60 * 2**20
HIGH = lax.Precision.HIGHEST


def bucket_table(length, buckets, reach):
    positions = np.arange(length)
    relative = positions[None, :] - positions[:, None]
    halfway = buckets // 2
    exact_span = halfway // 2
    distance = np.abs(relative)
    logged = exact_span + (
        np.log(np.maximum(distance, 1) / exact_span)
        / np.log(reach / exact_span)
        * (halfway - exact_span)
    ).astype(np.int64)
    logged = np.minimum(logged, halfway - 1)
    result = (relative > 0).astype(np.int64) * halfway + np.where(
        distance < exact_span, distance, logged
    )
    return result.astype(np.int32)


def rms_forward(values, gain):
    factor = lax.rsqrt(jnp.mean(values * values, axis=-1, keepdims=True) + EPSILON)
    return (values * factor * gain, factor)


def rms_backward(values, factor, gain, upstream):
    normed = values * factor
    gain_grad = jnp.sum(upstream * normed, axis=0)
    inner = upstream * gain
    return (factor * (inner - normed * jnp.mean(inner * normed, axis=-1, keepdims=True)), gain_grad)


def matmul(left, right):
    return jnp.dot(left, right, preferred_element_type=jnp.float32)


def matmul_left(left, right):
    return lax.dot_general(
        left, right, (((0,), (0,)), ((), ())), preferred_element_type=jnp.float32
    )


def matmul_right(left, right):
    return lax.dot_general(
        left, right, (((1,), (1,)), ((), ())), preferred_element_type=jnp.float32
    )


def row_scores(query_row, key_row, seg_row, bias):
    raw_scores = jnp.einsum("qhd,khd->hqk", query_row, key_row, preferred_element_type=jnp.float32)
    same_doc = (seg_row[:, None] == seg_row[None, :])[None]
    return jnp.where(same_doc, raw_scores + bias, -1e30)


MESH = pl.DeviceIdType.MESH
LANES = 128


class Place:
    def __init__(self):
        self.dp, self.fsdp = lax.axis_index("dp"), lax.axis_index("fsdp")
        self.y, self.x = self.dp // 2, self.dp % 2
        self.z, self.c = self.fsdp // 2, self.fsdp % 2

    def core(self):
        return (self.dp, self.z * 2 + (1 - self.c))

    def at_x(self):
        return (self.y * 2 + (1 - self.x), self.fsdp)

    def at_y(self):
        return ((1 - self.y) * 2 + self.x, self.fsdp)

    def at_xy(self):
        return ((1 - self.y) * 2 + (1 - self.x), self.fsdp)

    def up(self, d):
        return lax.rem(self.z + d, 4)

    def down(self, d):
        return lax.rem(self.z + 4 - d, 4)

    def at_z(self, d):
        return (self.dp, self.up(d) * 2 + self.c)

    def greet(self):
        barrier = pltpu.get_barrier_semaphore()
        partners = [self.core(), self.at_x(), self.at_y(), self.at_xy()]
        partners += [self.at_z(d) for d in (1, 2, 3)]
        for partner in partners:
            pl.semaphore_signal(barrier, inc=1, device_id=partner, device_id_type=MESH)
        pl.semaphore_wait(barrier, len(partners))


def remote(src, dst, send, recv, device):
    return pltpu.make_async_remote_copy(
        src_ref=src, dst_ref=dst, send_sem=send, recv_sem=recv, device_id=device, device_id_type=MESH
    )


def half(which, size, start=0):
    return pl.ds(pl.multiple_of(start + which * (size // 2), size // 2 if start % (size // 2) == 0 else 16), size // 2)


class Unit:
    def __init__(self, array, first, rows, left, wide):
        self.array, self.first, self.rows, self.left, self.wide = array, first, rows, left, wide

    def quarter(self, y, x):
        return (half(y, self.rows, self.first), half(x, self.wide, self.left))

    def whole(self):
        return (pl.ds(self.first, self.rows), pl.ds(self.left, self.wide))


class Gather:
    RECVS = 13

    def __init__(self, place, units, shards, wholes, send, recv):
        self.p, self.units, self.shards, self.wholes = place, units, shards, wholes
        self.send, self.recv = send, recv

    def _part(self, u, z, y, x):
        unit = self.units[u]
        return self.wholes[unit.array].at[(z, self.p.c) + unit.quarter(y, x)]

    def _z(self, u, d):
        p, unit = self.p, self.units[u]
        src = self.shards[unit.array].at[unit.quarter(p.y, p.x)]
        return remote(src, self._part(u, p.z, p.y, p.x), self.send.at[u, d - 1], self.recv.at[u, d - 1], p.at_z(d))

    def _hop(self, u, d, kind, y, x, device):
        ref = self._part(u, self.p.down(d), y, x)
        k = 3 * kind + d - 1
        return remote(ref, ref, self.send.at[u, k], self.recv.at[u, k], device)

    def _to_x(self, u, d):
        return self._hop(u, d, 1, self.p.y, self.p.x, self.p.at_x())

    def _to_y(self, u, d):
        return self._hop(u, d, 2, self.p.y, self.p.x, self.p.at_y())

    def _through_x(self, u, d):
        return (u + d) % 2 == 0

    def _diagonal(self, u, d):
        p = self.p
        if self._through_x(u, d):
            return self._hop(u, d, 3, p.y, 1 - p.x, p.at_y())
        return self._hop(u, d, 3, 1 - p.y, p.x, p.at_x())

    def _core(self, u):
        unit = self.units[u]
        ref = self.wholes[unit.array].at[(slice(None), self.p.c) + unit.whole()]
        return remote(ref, ref, self.send.at[u, 12], self.recv.at[u, 12], self.p.core())

    def start(self, u):
        for d in (1, 2, 3):
            self._z(u, d).start()

    def plane(self, u):
        for d in (1, 2, 3):
            self._z(u, d).wait_recv()
            self._to_x(u, d).start()
            self._to_y(u, d).start()

    def corner(self, u):
        for d in (1, 2, 3):
            first, second = (self._to_x, self._to_y) if self._through_x(u, d) else (self._to_y, self._to_x)
            first(u, d).wait_recv()
            self._diagonal(u, d).start()
            second(u, d).wait_recv()

    def pair(self, u):
        for d in (1, 2, 3):
            self._diagonal(u, d).wait_recv()
        self._core(u).start()

    def arrive(self, u):
        self._core(u).wait_recv()

    def finish(self, u):
        for d in (1, 2, 3):
            self._z(u, d).wait_send()
            self._to_x(u, d).wait_send()
            self._to_y(u, d).wait_send()
            self._diagonal(u, d).wait_send()
        self._core(u).wait_send()


def gather_units():
    small = [Unit(i, 0, 96, 0, 768) for i in range(4)]
    up = [Unit(4, 0, 96, 768 * j, 768) for j in range(4)]
    down = [Unit(5, 128 * j, 128, 0, 768) for j in range(3)]
    return small + up + [Unit(6, 0, 96, 0, 768)] + down


def dot(a, b, ca=1, cb=0):
    return lax.dot_general(a, b, (((ca,), (cb,)), ((), ())), preferred_element_type=jnp.float32)


def dot_exact(a, b, ca=1, cb=0):
    return lax.dot_general(
        a, b, (((ca,), (cb,)), ((), ())), precision=HIGH, preferred_element_type=jnp.float32
    )


def low(v):
    return v.astype(jnp.bfloat16)


def wide(v):
    return v.astype(jnp.float32)


def two_parts(v):
    high = wide(low(v))
    return low(jnp.concatenate([high, v - high], axis=0))


def norm_factor(v):
    return lax.rsqrt(jnp.mean(v * v, axis=-1, keepdims=True) + EPSILON)


def norm_back(v, factor, gain, upstream):
    normed = v * factor
    inner = upstream * gain
    grad = factor * (inner - normed * jnp.mean(inner * normed, axis=-1, keepdims=True))
    return grad, jnp.sum(upstream * normed, axis=0, keepdims=True)


def gelu_both(v):
    scale = math.sqrt(2.0 / math.pi)
    square = v * v
    bent = jnp.tanh(scale * v * (1.0 + 0.044715 * square))
    share = 0.5 + 0.5 * bent
    slope = share + (0.5 * scale) * v * (1.0 - bent * bent) * (1.0 + (3 * 0.044715) * square)
    return v * share, slope


def flat(ref, *where):
    value = ref[where] if where else ref[...]
    return value.reshape(-1, value.shape[-1])


TILE, SPAN = 128, 384


def rows_of(t):
    return pl.ds(t * TILE, TILE)


def span_of(t):
    return pl.ds(t * TILE, SPAN)


def heads_of(p):
    return pl.ds(pl.multiple_of(p * LANES, LANES), LANES)


def stacked(v, axis=0):
    first = lax.broadcasted_iota(jnp.int32, v.shape, 1) < LANES // 2
    zero = jnp.zeros_like(v)
    return jnp.concatenate([jnp.where(first, v, zero), jnp.where(first, zero, v)], axis=axis)


def side_by_side(v):
    return jnp.concatenate([v[:TILE], v[TILE:]], axis=1)


def probs_at(p, t):
    return (pl.ds(pl.multiple_of((p // 2) * 256, 256), 256), pl.ds(pl.multiple_of((p % 2) * 1536, 1536) + t * SPAN, SPAN))


def attend(p, t, q, keys, values, band, mask, probs, mixed):
    scores = dot(stacked(q[rows_of(t), heads_of(p)]), keys[span_of(t), heads_of(p)], 1, 1)
    hidden = mask[t]
    scores = scores + band[p] + jnp.concatenate([hidden, hidden], axis=0)
    powered = jnp.exp(scores - jnp.max(scores, axis=1, keepdims=True))
    soft = low(powered * (1.0 / jnp.sum(powered, axis=1, keepdims=True)))
    probs[probs_at(p, t)] = soft
    out = dot(side_by_side(soft), stacked(values[span_of(t), heads_of(p)]))
    mixed[rows_of(t), heads_of(p)] = low(out)


def forward_kernel(units, *refs):
    x_ref, seg_ref, pool_ref, emb_ref, g1_ref, g2_ref, g3_ref, table_ref, near_ref = refs[:9]
    shards, refs = refs[9:16], refs[16:]
    w_outs, big_outs, small_outs, refs = refs[:6], refs[6:17], refs[17:21], refs[21:]
    wholes, refs = refs[:7], refs[7:]
    held, refs = refs[:10], refs[10:]
    act, slope, n1, n2, mixed, q, keys, values, probs, h1 = held
    h2, band, mask = refs[:3]
    send, recv, local, ready = refs[3:]
    emb_out, pooled_out, eg_out, top_out = small_outs
    wq, wk, wv, wo, wup, wdn, wpj = wholes
    place = Place()
    gather = Gather(place, units, shards, wholes, send, recv)
    own = [
        pltpu.make_async_copy(shard, whole.at[place.z, place.c], local.at[i])
        for i, (shard, whole) in enumerate(zip(shards, wholes))
    ]
    backs = [pltpu.make_async_copy(a, b, local.at[7 + i]) for i, (a, b) in enumerate(zip(wholes[:6], w_outs))]
    keeps = [pltpu.make_async_copy(a, b, ready.at[i]) for i, (a, b) in enumerate(zip(held, big_outs))]
    for copy in own:
        copy.start()
    place.greet()
    n = len(units)
    stages = (gather.plane, gather.corner, gather.pair, gather.arrive)

    def step(t):
        for lag, stage in enumerate(stages):
            if 0 <= t - lag < n:
                stage(t - lag)
                if lag == 0 and t + 2 < n:
                    gather.start(t + 2)

    for u in range(2):
        gather.start(u)
    for copy in own:
        copy.wait()

    x = wide(x_ref[...])
    n1[...] = low(x * norm_factor(x) * g1_ref[...].reshape(1, 768))
    step(0)
    ray = dot_exact(table_ref[...], near_ref[...])
    for h in range(ray.shape[0]):
        rolled = pltpu.roll(jnp.broadcast_to(ray[h : h + 1], (TILE, 512)), 0, 1, stride=1, stride_axis=0)
        band[h // 2, pl.ds((h % 2) * TILE, TILE), :] = rolled[:, :SPAN]
    step(1)
    seg = seg_ref[...]
    seg_f = wide(seg)
    column = jnp.transpose(jnp.broadcast_to(seg_f, (TILE, 512)))
    edge = jnp.full((1, TILE), -1.0, jnp.float32)
    line = jnp.concatenate([edge, seg_f, edge], axis=1)
    for t in range(4):
        own_seg = column[t * TILE : (t + 1) * TILE]
        same = jnp.concatenate([own_seg] * 3, axis=1) == line[:, t * TILE : t * TILE + SPAN]
        mask[t] = jnp.where(same, 0.0, -1e30)
    blank = jnp.zeros((TILE, 768), jnp.bfloat16)
    for ref in (keys, values):
        ref[pl.ds(0, TILE), :] = blank
        ref[pl.ds(640, TILE), :] = blank
    step(2)
    step(3)
    q[...] = low(dot(n1[...], flat(wq)))
    backs[0].start()
    step(4)
    keys[pl.ds(TILE, 512), :] = low(dot(n1[...], flat(wk)))
    backs[1].start()
    step(5)
    values[pl.ds(TILE, 512), :] = low(dot(n1[...], flat(wv)))
    backs[2].start()
    for i in (2, 5, 6, 7):
        keeps[i].start()

    def pairs(first, last):
        @pl.loop(first, last)
        def _(p):
            for t in range(4):
                attend(p, t, q, keys, values, band, mask, probs, mixed)

    pairs(0, 2)
    step(6)
    pairs(2, 4)
    step(7)
    pairs(4, 6)
    backs[3].start()
    keeps[8].start()
    keeps[4].start()
    hidden = wide(x_ref[...]) + dot(mixed[...], flat(wo))
    h1[...] = hidden
    n2[...] = low(hidden * norm_factor(hidden) * g2_ref[...].reshape(1, 768))
    keeps[3].start()
    keeps[9].start()
    for j in range(4):
        cols = pl.ds(768 * j, 768)
        value, grad = gelu_both(dot(n2[...], flat(wup, slice(None), slice(None), slice(None), cols)))
        act[:, cols] = low(value)
        slope[:, cols] = low(grad)
        step(8 + j)
    backs[4].start()
    keeps[0].start()
    keeps[1].start()
    for j in range(3):
        step(12 + j)
        part = jnp.concatenate([act[:, pl.ds(384 * s + 128 * j, 128)] for s in range(8)], axis=1)
        more = dot(part, flat(wdn, slice(None), slice(None), pl.ds(128 * j, 128)))
        h2[...] = (h1[...] if j == 0 else h2[...]) + more
    backs[5].start()
    h = h2[...]
    factor = norm_factor(h)
    fin = h * factor * g3_ref[...].reshape(1, 768)
    eye = lax.broadcasted_iota(jnp.int32, (8, 8), 0) == lax.broadcasted_iota(jnp.int32, (8, 8), 1)
    pool = jnp.sum(jnp.where(eye, wide(pool_ref[...]), 0.0), axis=1, keepdims=True)
    member = jnp.where(seg_f == pool, 1.0, 0.0)
    count = jnp.sum(member, axis=1, keepdims=True)
    fin_high = low(fin)
    pooled = (dot(low(member), fin_high) + dot(low(member), low(fin - wide(fin_high)))) / count
    wp = flat(wpj)
    both = dot(two_parts(pooled), wp)
    projected = both[:8] + both[8:]
    inverse = lax.rsqrt(jnp.sum(projected * projected, axis=-1, keepdims=True) + EPSILON)
    emb = projected * inverse
    up = emb_ref[...].reshape(8, 768)
    eg = inverse * (up - emb * jnp.sum(up * emb, axis=-1, keepdims=True))
    both = dot(two_parts(eg), wp, 1, 1)
    pooled_grad = (both[:8] + both[8:]) / count
    twice = low(jnp.concatenate([member, member], axis=0))
    fin_grad = dot(twice, two_parts(pooled_grad), 0, 0)
    stream, gain_grad = norm_back(h, factor, g3_ref[...].reshape(1, 768), fin_grad)
    emb_out[...] = emb
    pooled_out[...] = pooled
    eg_out[...] = eg
    h2[...] = stream
    top_out[...] = gain_grad
    last = pltpu.make_async_copy(h2, big_outs[10], ready.at[10])
    last.start()
    for u in range(n):
        gather.finish(u)
    for copy in (*backs, *keeps, last):
        copy.wait()


def bucket_rows(away, buckets):
    halfway = buckets // 2
    exact = halfway // 2
    distance = np.abs(away)
    logged = exact + (
        np.log(np.maximum(distance, 1) / exact) / np.log(REACH / exact) * (halfway - exact)
    ).astype(np.int64)
    bucket = (away > 0) * halfway + np.where(distance < exact, distance, np.minimum(logged, halfway - 1))
    return (np.arange(buckets)[:, None] == bucket[None, :]).astype(np.float32)


def ray_buckets(buckets):
    near = np.arange(512)
    return bucket_rows(np.where(near < SPAN, near - TILE, near - 512 - TILE), buckets)


def forward_all(x, seg_ids, pool_index, emb_grad, gains, table, shards):
    units = gather_units()
    full = [(4, 2) + shard.shape for shard in shards]
    low_shapes = [(512, 3072)] * 2 + [(512, 768)] * 4 + [(768, 768)] * 2 + [(768, 3072)]
    held = [jax.ShapeDtypeStruct(s, jnp.bfloat16) for s in low_shapes]
    held.append(jax.ShapeDtypeStruct((512, 768), jnp.float32))
    outs = [jax.ShapeDtypeStruct(s, jnp.bfloat16) for s in full[:6]]
    outs += held + [jax.ShapeDtypeStruct((512, 768), jnp.float32)]
    n_large = len(outs)
    outs += [jax.ShapeDtypeStruct((8, 768), jnp.float32)] * 3 + [jax.ShapeDtypeStruct((1, 768), jnp.float32)]
    vmem, large = pl.BlockSpec(memory_space=pltpu.VMEM), pl.BlockSpec(memory_space=pl.ANY)
    return pl.pallas_call(
        partial(forward_kernel, units),
        out_shape=outs,
        in_specs=[vmem] * 9 + [large] * 7,
        out_specs=[large] * n_large + [vmem] * 4,
        scratch_shapes=[pltpu.VMEM(shape, jnp.bfloat16) for shape in full]
        + [pltpu.VMEM(h.shape, h.dtype) for h in held]
        + [
            pltpu.VMEM((512, 768), jnp.float32),
            pltpu.VMEM((6, 2 * TILE, SPAN), jnp.float32),
            pltpu.VMEM((4, TILE, SPAN), jnp.float32),
            pltpu.SemaphoreType.DMA((len(units), Gather.RECVS)),
            pltpu.SemaphoreType.DMA((len(units), Gather.RECVS)),
            pltpu.SemaphoreType.DMA((13,)),
            pltpu.SemaphoreType.DMA((11,)),
        ],
        compiler_params=pltpu.CompilerParams(
            collective_id=0, has_side_effects=True, vmem_limit_bytes=VMEM_BYTES
        ),
        name="forward",
    )(x, seg_ids, pool_index, emb_grad, *gains, table, ray_buckets(table.shape[1]), *shards)


class Reduce:
    SEMS = 11

    def __init__(self, place, grad, own, core, along_x, along_y, second_x, second_y, line, total, send, recv):
        self.p, self.g, self.own, self.rc = place, grad, own, core
        self.rx, self.ry, self.sx, self.sy, self.rz, self.f = along_x, along_y, second_x, second_y, line, total
        self.send, self.recv = send, recv
        rows = own.shape[1]
        p = place
        self.row = [half(i, rows) for i in (p.y, 1 - p.y)]
        self.col = [half(i, 768) for i in (p.x, 1 - p.x)]

    def _copy(self, k, src, dst, device):
        return remote(src, dst, self.send.at[k], self.recv.at[k], device)

    def _core(self):
        return self._copy(0, self.g.at[:, 1 - self.p.c], self.rc, self.p.core())

    def _first(self):
        p, low, high = self.p, pl.ds(0, 2), pl.ds(2, 2)
        return (
            self._copy(1, self.own.at[low, :, self.col[1]], self.rx, p.at_x()),
            self._copy(2, self.own.at[high, self.row[1], :], self.ry, p.at_y()),
        )

    def _second(self):
        p, low, high = self.p, pl.ds(0, 2), pl.ds(2, 2)
        return (
            self._copy(3, self.own.at[low, self.row[1], self.col[0]], self.sy, p.at_y()),
            self._copy(4, self.own.at[high, self.row[0], self.col[1]], self.sx, p.at_x()),
        )

    def _line(self):
        p = self.p
        return [
            self._copy(4 + d, self.own.at[p.up(d), self.row[0], self.col[0]], self.rz.at[d - 1], p.at_z(d))
            for d in (1, 2, 3)
        ]

    def _spread(self):
        p, part = self.p, self.f.at[self.row[0], self.col[0]]
        return [self._copy(8 + i, part, part, device) for i, device in enumerate((p.at_x(), p.at_y(), p.at_xy()))]

    def _add(self, where, other):
        self.own[where] = low(wide(self.own[where]) + wide(other[...]))

    def start(self):
        self._core().start()

    def settle(self):
        self._core().wait()
        for i in range(4):
            self.own[i] = low(wide(self.g[i, self.p.c]) + wide(self.rc[i]))

    def first(self):
        for copy in self._first():
            copy.start()

    def second(self):
        along_x, along_y = self._first()
        along_x.wait_recv()
        for i in range(2):
            self._add((i, slice(None), self.col[0]), self.rx.at[i])
        to_y, to_x = self._second()
        to_y.start()
        along_y.wait_recv()
        for i in range(2):
            self._add((2 + i, self.row[0], slice(None)), self.ry.at[i])
        to_x.start()

    def line(self):
        for copy in self._second():
            copy.wait_recv()
        for i in range(2):
            self._add((i, self.row[0], self.col[0]), self.sy.at[i])
            self._add((2 + i, self.row[0], self.col[0]), self.sx.at[i])
        for copy in self._line():
            copy.start()

    def spread(self):
        total = wide(self.own[self.p.z, self.row[0], self.col[0]])
        for d, copy in enumerate(self._line()):
            copy.wait_recv()
            total = total + wide(self.rz[d])
        self.f[self.row[0], self.col[0]] = low(total)
        for copy in self._spread():
            copy.start()

    def arrive(self):
        for copy in self._spread():
            copy.wait_recv()

    def finish(self):
        for copy in (*self._first(), *self._second(), *self._line(), *self._spread()):
            copy.wait_send()


class Small:
    SEMS = 6

    def __init__(self, place, sums, got, line, send, recv):
        self.p, self.sums, self.got, self.line, self.send, self.recv = place, sums, got, line, send, recv

    def _pair(self, i):
        device = (self.p.core, self.p.at_x, self.p.at_y)[i]()
        return remote(self.sums.at[i], self.got.at[i], self.send.at[i], self.recv.at[i], device)

    def _line(self):
        p = self.p
        return [
            remote(self.sums.at[3], self.line.at[p.z], self.send.at[2 + d], self.recv.at[2 + d], p.at_z(d))
            for d in (1, 2, 3)
        ]

    def start(self):
        self._pair(0).start()

    def turn(self, i):
        self._pair(i).wait_recv()
        self.sums[i + 1] = self.sums[i] + self.got[i]
        if i < 2:
            self._pair(i + 1).start()
        else:
            self.line[self.p.z] = self.sums[3]
            for copy in self._line():
                copy.start()

    def finish(self):
        for copy in self._line():
            copy.wait()
        for i in range(3):
            self._pair(i).wait_send()
        return self.line[0] + self.line[1] + self.line[2] + self.line[3]


SMALL, TALL, RING = 9, 3, 3


def attend_back(p, t, held, keys, values, probs, sums, table):
    def heads_at(base):
        return pl.ds(pl.multiple_of(p * LANES + base, LANES), LANES)

    heads = heads_at(0)
    ups = stacked(held[rows_of(t), heads_at(768)])
    qs = stacked(held[rows_of(t), heads])
    soft = probs[probs_at(p, t)]
    weighted = wide(soft) * dot(ups, values[span_of(t), heads], 1, 1)
    grad = weighted - wide(soft) * jnp.sum(weighted, axis=1, keepdims=True)
    grad_low = low(grad)
    out = dot(side_by_side(grad_low), stacked(keys[span_of(t), heads]))
    held[rows_of(t), heads_at(1536)] = low(out)
    sums[pl.ds(t * TILE, SPAN), heads] += dot(grad_low, qs, 0, 0)
    sums[pl.ds(768 + t * TILE, SPAN), heads] += dot(soft, ups, 0, 0)
    table[p] += grad


def backward_kernel(*refs):
    pooled_ref, eg_ref, g1_ref, g2_ref, top_ref, far_ref = refs[:6]
    stream_in, act_in, slope_in, n1_in, n2_in, mixed_in, q_in, keys_in, values_in, probs_in, h1_in, x_in = refs[6:18]
    wq_in, wk_in, wv_in, wo_in, wup_in, wdn_in = refs[18:24]
    outs, input_out, small_out, refs = refs[24:31], refs[31], refs[32], refs[33:]
    held, pre, wup, wdn, n2, mixed, upstream, keys, values, stream, sums, table, rays = refs[:13]
    ring, refs = refs[13], refs[14:]
    buffers, refs = (refs[:8], refs[8:16]), refs[16:]
    small_sums, small_got, small_line = refs[:3]
    send, recv, local, writes, small_send, small_recv = refs[3:]
    place = Place()
    loads = {}

    def load(name, src, dst):
        loads[name] = pltpu.make_async_copy(src, dst, local.at[len(loads)])
        loads[name].start()

    def part(ref, i):
        return ref.at[:, pl.ds(768 * i, 768)]

    load("stream", stream_in, stream)
    load("act", act_in, held)
    load("wdn", wdn_in, wdn)
    load("slope", slope_in, pre)
    load("n2", n2_in, n2)
    load("wup", wup_in, wup)
    load("h1", h1_in, sums.at[pl.ds(0, 512), :])
    load("mixed", mixed_in, mixed)
    load("keys", keys_in, keys)
    load("values", values_in, values)
    place.greet()

    order = [(0, 0, 6, 0)]
    order += [(1, j, 5, j) for j in range(TALL)]
    order += [(0, 1 + j, 4, j) for j in range(4)]
    order += [(0, 5, 3, 0), (0, 6, 2, 0), (0, 7, 1, 0), (0, 8, 0, 0)]
    works, results = [], []
    for u, (kind, slot, array, j) in enumerate(order):
        rows = (96, 128)[kind]
        parts = [b.at[slot] for b in buffers[kind]]
        grad = ring.at[u % RING, :, :, pl.ds(0, rows), :]
        works.append(Reduce(place, grad, *parts, send.at[u], recv.at[u]))
        dst = outs[5].at[pl.ds(128 * j, 128), :] if array == 5 else outs[array].at[:, pl.ds(768 * j, 768)]
        results.append(pltpu.make_async_copy(parts[-1], dst, writes.at[u]))
    n = len(order)

    def produce(u, value):
        work = works[u]
        work.g[...] = low(value).reshape(work.g.shape)
        work.start()

    def settle(u):
        works[u].settle()

    def end(u):
        works[u].arrive()
        results[u].start()

    stages = (
        lambda u: works[u].first(),
        lambda u: works[u].second(),
        lambda u: works[u].line(),
        lambda u: works[u].spread(),
        end,
    )

    def step(t):
        for lag, stage in enumerate(stages):
            if 0 <= t - lag < n:
                stage(t - lag)

    pooled, eg = pooled_ref[...], eg_ref[...]
    pooled_high, eg_high = wide(low(pooled)), wide(low(eg))
    left = jnp.concatenate([pooled_high, pooled_high, pooled - pooled_high], axis=0)
    right = jnp.concatenate([eg_high, eg - eg_high, eg_high], axis=0)
    produce(0, dot(low(left), low(right), 0, 0))
    loads["stream"].wait()
    upstream[...] = low(stream[...])
    loads["act"].wait()
    for j in range(TALL):
        picked = jnp.concatenate([held[:, pl.ds(384 * s + 128 * j, 128)] for s in range(8)], axis=1)
        produce(1 + j, dot(picked, upstream[...], 0, 0))
        settle(j)
        if j == 0:
            step(0)
    settle(3)
    load("q", q_in, part(held, 0))
    load("n1", n1_in, part(held, 3))
    step(1)
    for name in ("wdn", "slope", "n2", "wup"):
        loads[name].wait()
    for j in range(4):
        cols = pl.ds(768 * j, 768)
        grad = low(wide(pre[:, cols]) * dot(upstream[...], wdn[cols, :], 1, 1))
        pre[:, cols] = grad
        produce(4 + j, dot(n2[...], grad, 0, 0))
        more = dot(grad, wup[:, cols], 1, 1)
        where = pl.ds(512, 512)
        sums[where, :] = more if j == 0 else sums[where, :] + more
        settle(4 + j)
        if j % 2 == 1:
            step(2 + j // 2)
    for i, ref in enumerate((wo_in, wq_in, wk_in, wv_in)):
        load(f"w{i}", ref, wdn.at[pl.ds(768 * i, 768), :])
    load("probs", probs_in, wup)
    load("x", x_in, n2)
    loads["h1"].wait()
    h1 = sums[pl.ds(0, 512), :]
    more, gain_two = norm_back(h1, norm_factor(h1), g2_ref[...].reshape(1, 768), sums[pl.ds(512, 512), :])
    through = stream[...] + more
    stream[...] = through
    upstream[...] = low(through)
    loads["mixed"].wait()
    produce(8, dot(mixed[...], upstream[...], 0, 0))
    loads["w0"].wait()
    part(held, 1)[...] = low(dot(upstream[...], wdn[pl.ds(0, 768), :], 1, 1))
    sums[...] = jnp.zeros_like(sums)
    table[...] = jnp.zeros_like(table)
    settle(8)
    for name in ("keys", "values", "q", "probs"):
        loads[name].wait()

    def pairs(first, last):
        @pl.loop(first, last)
        def _(p):
            for t in range(4):
                attend_back(p, t, held, keys, values, wup, sums, table)

    step(4)
    pairs(0, 2)
    step(5)
    pairs(2, 4)
    step(6)
    pairs(4, 6)
    loads["n1"].wait()
    n1 = held[:, pl.ds(2304, 768)]
    vg, kg = low(sums[pl.ds(768 + TILE, 512), :]), low(sums[pl.ds(TILE, 512), :])
    produce(9, dot(n1, vg, 0, 0))
    produce(10, dot(n1, kg, 0, 0))
    settle(9)
    qg = held[:, pl.ds(1536, 768)]
    produce(11, dot(n1, qg, 0, 0))
    settle(10)
    step(7)
    for name in ("w1", "w2", "w3", "x"):
        loads[name].wait()
    n1_grad = dot(qg, wdn[pl.ds(768, 768), :], 1, 1) + dot(kg, wdn[pl.ds(1536, 768), :], 1, 1)
    n1_grad = n1_grad + dot(vg, wdn[pl.ds(2304, 768), :], 1, 1)
    x = wide(n2[...])
    more, gain_one = norm_back(x, norm_factor(x), g1_ref[...].reshape(1, 768), n1_grad)
    stream[...] = stream[...] + more
    settle(11)
    last = pltpu.make_async_copy(stream, input_out, writes.at[n])
    last.start()
    step(8)
    turn = lax.broadcasted_iota(jnp.int32, (TILE, TILE), 0) + lax.broadcasted_iota(jnp.int32, (TILE, TILE), 1)
    mirror = low(jnp.where(turn == TILE - 1, 1.0, 0.0))
    rays[...] = jnp.zeros_like(rays)
    for h in range(12):
        tile = table[h // 2, pl.ds((h % 2) * TILE, TILE), :]
        high = low(tile)
        upside = dot(mirror, high) + dot(mirror, low(tile - wide(high)))
        spread = jnp.concatenate([upside, jnp.zeros((TILE, 512 - SPAN), jnp.float32)], axis=1)
        rolled = pltpu.roll(spread, 0, 1, stride=1, stride_axis=0)
        rays[pl.ds(h, 1), :] = jnp.sum(rolled, axis=0, keepdims=True)
    by_bucket = dot_exact(rays[...], far_ref[...], 1, 1)
    small_sums[0, :, pl.ds(0, 768)] = jnp.concatenate(
        [gain_one, gain_two, top_ref[...], jnp.zeros((5, 768), jnp.float32)], axis=0
    )
    small_sums[0, :, pl.ds(768, 128)] = by_bucket[:8]
    small_sums[0, :, pl.ds(896, 128)] = by_bucket[8:]
    small = Small(place, small_sums, small_got, small_line, small_send, small_recv)
    small.start()
    for t in range(9, n + len(stages) - 1):
        step(t)
        if t < 12:
            small.turn(t - 9)
    small_out[...] = small.finish()
    for u in range(n):
        works[u].finish()
        results[u].wait()
    last.wait()


def far_buckets(buckets):
    rows = np.zeros((LANES, 512), np.float32)
    rows[:buckets] = bucket_rows(np.arange(512) - 255, buckets)
    return rows


def backward_all(smalls, saved, x, weights, buckets):
    f32, b16 = jnp.float32, jnp.bfloat16
    buffers = []
    for count, rows in ((SMALL, 96), (TALL, 128)):
        shapes = [(4, rows, 768), (4, rows, 768), (2, rows, 384), (2, rows // 2, 768)]
        shapes += [(2, rows // 2, 384)] * 2 + [(3, rows // 2, 384), (rows, 768)]
        buffers += [pltpu.VMEM((count,) + shape, b16) for shape in shapes]
    n = SMALL + TALL
    outs = [jax.ShapeDtypeStruct(s, b16) for s in [(96, 768)] * 4 + [(96, 3072), (384, 768), (96, 768)]]
    outs += [jax.ShapeDtypeStruct((512, 768), f32), jax.ShapeDtypeStruct((8, 1024), f32)]
    vmem, large = pl.BlockSpec(memory_space=pltpu.VMEM), pl.BlockSpec(memory_space=pl.ANY)
    operands = (*smalls, far_buckets(buckets), *saved, x, *weights)
    return pl.pallas_call(
        backward_kernel,
        out_shape=outs,
        in_specs=[vmem] * 6 + [large] * 18,
        out_specs=[large] * 8 + [vmem],
        scratch_shapes=[
            pltpu.VMEM((512, 3072), b16),
            pltpu.VMEM((512, 3072), b16),
            pltpu.VMEM((768, 3072), b16),
            pltpu.VMEM((3072, 768), b16),
            pltpu.VMEM((512, 768), b16),
            pltpu.VMEM((512, 768), b16),
            pltpu.VMEM((512, 768), b16),
            pltpu.VMEM((768, 768), b16),
            pltpu.VMEM((768, 768), b16),
            pltpu.VMEM((512, 768), f32),
            pltpu.VMEM((1536, 768), f32),
            pltpu.VMEM((6, 2 * TILE, SPAN), f32),
            pltpu.VMEM((16, 512), f32),
            pltpu.VMEM((RING, 4, 2, 128, 768), b16),
        ]
        + buffers
        + [
            pltpu.VMEM((4, 8, 1024), f32),
            pltpu.VMEM((3, 8, 1024), f32),
            pltpu.VMEM((4, 8, 1024), f32),
            pltpu.SemaphoreType.DMA((n, Reduce.SEMS)),
            pltpu.SemaphoreType.DMA((n, Reduce.SEMS)),
            pltpu.SemaphoreType.DMA((20,)),
            pltpu.SemaphoreType.DMA((n + 1,)),
            pltpu.SemaphoreType.DMA((Small.SEMS,)),
            pltpu.SemaphoreType.DMA((Small.SEMS,)),
        ],
        compiler_params=pltpu.CompilerParams(
            collective_id=1, has_side_effects=True, vmem_limit_bytes=VMEM_BYTES
        ),
        name="backward",
    )(*operands)


def finish_kernel(emb_in, input_in, small_in, *refs):
    grads, outs = refs[:7], refs[7:]
    emb_out, input_out, gains, table = outs[0], outs[1], outs[9:12], outs[12]
    emb_out[...] = emb_in[...].reshape(emb_out.shape)
    input_out[...] = input_in[...].reshape(input_out.shape)
    for grad, out in zip(grads, outs[2:9]):
        out[...] = wide(grad[...])
    for i, gain in enumerate(gains):
        gain[...] = small_in[pl.ds(i, 1), pl.ds(0, 768)].reshape(768)
    both = jnp.concatenate([small_in[:, pl.ds(768, 128)], small_in[:, pl.ds(896, 128)]], axis=0)
    table[...] = both[:12, :32]


def finish_all(emb, input_grad, small, grads):
    f32 = jnp.float32
    shapes = [(1, 8, 768), (1, 512, 768)] + [g.shape for g in grads] + [(768,)] * 3 + [(12, 32)]
    vmem = pl.BlockSpec(memory_space=pltpu.VMEM)
    return pl.pallas_call(
        finish_kernel,
        out_shape=[jax.ShapeDtypeStruct(s, f32) for s in shapes],
        in_specs=[vmem] * 10,
        out_specs=[vmem] * 13,
        compiler_params=pltpu.CompilerParams(vmem_limit_bytes=VMEM_BYTES),
        name="finish",
    )(emb, input_grad, small, *grads)


def near_device(
    inputs,
    seg_ids,
    pool_index,
    w_query,
    w_key,
    w_value,
    w_out,
    w_up,
    w_down,
    w_proj,
    gain_attn,
    gain_ffn,
    gain_final,
    bias_table,
    emb_grad,
):
    x = inputs.reshape(-1, inputs.shape[-1])
    shards = (w_query, w_key, w_value, w_out, w_up, w_down, w_proj)
    gains = (gain_attn, gain_ffn, gain_final)
    done = forward_all(x, seg_ids, pool_index, emb_grad, gains, bias_table.T, shards)
    weights = [w.reshape(-1, w.shape[-1]) for w in done[:6]]
    act, slope, n1, n2, mixed, q, keys, values, probs, h1, stream = done[6:17]
    emb, pooled, eg, top = done[17:]
    saved = (stream, act, slope, n1, n2, mixed, q, keys, values, probs, h1)
    result = backward_all((pooled, eg, gain_attn, gain_ffn, top), saved, x, weights, bias_table.shape[0])
    out = finish_all(emb, result[7], result[8], result[:7])
    return (*out[:12], out[12].T)


def general(
    inputs,
    seg_ids,
    pool_index,
    w_query,
    w_key,
    w_value,
    w_out,
    w_up,
    w_down,
    w_proj,
    gain_attn,
    gain_ffn,
    gain_final,
    bias_table,
    emb_grad,
):
    rows, length, width = inputs.shape
    buckets, heads = bias_table.shape
    head_dim = width // heads
    tokens = rows * length
    head_shape = (rows, length, heads, head_dim)
    gathered = (
        lax.all_gather(w_query, "fsdp", axis=0, tiled=True),
        lax.all_gather(w_key, "fsdp", axis=0, tiled=True),
        lax.all_gather(w_value, "fsdp", axis=0, tiled=True),
        lax.all_gather(w_out, "fsdp", axis=0, tiled=True),
        lax.all_gather(w_up, "fsdp", axis=0, tiled=True),
        lax.all_gather(w_down, "fsdp", axis=0, tiled=True),
        lax.all_gather(w_proj, "fsdp", axis=0, tiled=True),
    )
    full_query, full_key, full_value, full_out, full_up, full_down, full_proj = gathered
    flat = inputs.reshape(tokens, width).astype(jnp.float32)
    normed_one, factor_one = rms_forward(flat, gain_attn)
    normed_one = normed_one.astype(jnp.bfloat16)
    queries = matmul(normed_one, full_query).astype(jnp.bfloat16).reshape(head_shape)
    key_rows = matmul(normed_one, full_key).astype(jnp.bfloat16).reshape(head_shape)
    value_rows = matmul(normed_one, full_value).astype(jnp.bfloat16).reshape(head_shape)
    bucket_ids = jnp.asarray(bucket_table(length, buckets, REACH))
    onehot_cols = (
        jnp.arange(buckets, dtype=jnp.int32)[:, None] == bucket_ids.reshape(1, length * length)
    ).astype(jnp.bfloat16)
    bias = jnp.dot(bias_table.T, onehot_cols.astype(jnp.float32), precision=HIGH).reshape(
        heads, length, length
    )

    def attend_row(pieces):
        query_row, key_row, value_row, seg_row = pieces
        scores = row_scores(query_row, key_row, seg_row, bias)
        row_peak = jnp.max(scores, axis=-1, keepdims=True)
        log_total = row_peak + jnp.log(jnp.sum(jnp.exp(scores - row_peak), axis=-1, keepdims=True))
        soft_low = jnp.exp(scores - log_total).astype(jnp.bfloat16)
        mixed = jnp.einsum("hqk,khd->qhd", soft_low, value_row, preferred_element_type=jnp.float32)
        return (mixed.astype(jnp.bfloat16), log_total)

    attended, log_totals = lax.map(attend_row, (queries, key_rows, value_rows, seg_ids))
    attended_flat = attended.reshape(tokens, width)
    hidden_one = flat + matmul(attended_flat, full_out)
    normed_two, factor_two = rms_forward(hidden_one, gain_ffn)
    normed_two = normed_two.astype(jnp.bfloat16)
    pre_act = matmul(normed_two, full_up)
    activated = jax.nn.gelu(pre_act, approximate=True).astype(jnp.bfloat16)
    hidden_two = hidden_one + matmul(activated, full_down)
    final_rows, factor_three = rms_forward(hidden_two, gain_final)
    member = (seg_ids[:, None, :] == pool_index[:, :, None]).astype(jnp.float32)
    counts = jnp.sum(member, axis=-1, keepdims=True)
    pooled = (
        jnp.einsum("rpl,rld->rpd", member, final_rows.reshape(rows, length, width), precision=HIGH)
        / counts
    )
    proj_full = full_proj.astype(jnp.float32)
    projected = jnp.einsum("rpd,de->rpe", pooled, proj_full, precision=HIGH)
    inverse_len = lax.rsqrt(jnp.sum(projected * projected, axis=-1, keepdims=True) + EPSILON)
    embeddings = projected * inverse_len
    emb_dot = jnp.sum(emb_grad * embeddings, axis=-1, keepdims=True)
    projected_grad = inverse_len * (emb_grad - embeddings * emb_dot)
    grad_proj = jnp.einsum("rpd,rpe->de", pooled, projected_grad, precision=HIGH)
    pooled_grad = jnp.einsum("rpe,de->rpd", projected_grad, proj_full, precision=HIGH) / counts
    final_grad = jnp.einsum("rpl,rpd->rld", member, pooled_grad, precision=HIGH).reshape(
        tokens, width
    )
    stream_two, grad_gain_final = rms_backward(hidden_two, factor_three, gain_final, final_grad)
    back_weights = (
        lax.all_gather(w_query, "fsdp", axis=0, tiled=True),
        lax.all_gather(w_key, "fsdp", axis=0, tiled=True),
        lax.all_gather(w_value, "fsdp", axis=0, tiled=True),
        lax.all_gather(w_out, "fsdp", axis=0, tiled=True),
        lax.all_gather(w_up, "fsdp", axis=0, tiled=True),
        lax.all_gather(w_down, "fsdp", axis=0, tiled=True),
        lax.all_gather(w_proj, "fsdp", axis=0, tiled=True),
    )
    back_query, back_key, back_value, back_out, back_up, back_down, back_proj = back_weights
    ffn_grad = stream_two.astype(jnp.bfloat16)
    grad_down = matmul_left(activated, ffn_grad)
    act_grad = matmul_right(ffn_grad, back_down)
    gelu_pullback = jax.vjp(partial(jax.nn.gelu, approximate=True), pre_act)[1]
    pre_grad = gelu_pullback(act_grad)[0].astype(jnp.bfloat16)
    grad_up = matmul_left(normed_two, pre_grad)
    normed_two_grad = matmul_right(pre_grad, back_up)
    stream_mid, grad_gain_ffn = rms_backward(hidden_one, factor_two, gain_ffn, normed_two_grad)
    stream_one = stream_two + stream_mid
    attn_grad = stream_one.astype(jnp.bfloat16)
    grad_out = matmul_left(attended_flat, attn_grad)
    mixed_grad = matmul_right(attn_grad, back_out).astype(jnp.bfloat16).reshape(head_shape)

    def attend_back(pieces):
        query_row, key_row, value_row, seg_row, log_total, upstream_row = pieces
        scores = row_scores(query_row, key_row, seg_row, bias)
        soft_rows = jnp.exp(scores - log_total)
        soft_grad = jnp.einsum(
            "qhd,khd->hqk", upstream_row, value_row, preferred_element_type=jnp.float32
        )
        score_grad = (
            soft_rows * (soft_grad - jnp.sum(soft_rows * soft_grad, axis=-1, keepdims=True))
        ).astype(jnp.bfloat16)
        query_grad = jnp.einsum(
            "hqk,khd->qhd", score_grad, key_row, preferred_element_type=jnp.float32
        ).astype(jnp.bfloat16)
        key_grad = jnp.einsum(
            "hqk,qhd->khd", score_grad, query_row, preferred_element_type=jnp.float32
        ).astype(jnp.bfloat16)
        value_grad = jnp.einsum(
            "hqk,qhd->khd",
            soft_rows.astype(jnp.bfloat16),
            upstream_row,
            preferred_element_type=jnp.float32,
        ).astype(jnp.bfloat16)
        table_grad = matmul_right(score_grad.reshape(heads, length * length), onehot_cols)
        return (query_grad, key_grad, value_grad, table_grad)

    query_grads, key_grads, value_grads, table_grads = lax.map(
        attend_back, (queries, key_rows, value_rows, seg_ids, log_totals, mixed_grad)
    )
    grad_table = jnp.sum(table_grads, axis=0).T
    query_flat = query_grads.reshape(tokens, width)
    key_flat = key_grads.reshape(tokens, width)
    value_flat = value_grads.reshape(tokens, width)
    grad_query = matmul_left(normed_one, query_flat)
    grad_key = matmul_left(normed_one, key_flat)
    grad_value = matmul_left(normed_one, value_flat)
    normed_one_grad = (
        matmul_right(query_flat, back_query)
        + matmul_right(key_flat, back_key)
        + matmul_right(value_flat, back_value)
    )
    stream_in, grad_gain_attn = rms_backward(flat, factor_one, gain_attn, normed_one_grad)
    input_grad = (stream_one + stream_in).reshape(rows, length, width)
    shard_query, shard_key, shard_value, shard_out, shard_up, shard_down, shard_proj = (
        lax.psum_scatter(grad_query, "fsdp", scatter_dimension=0, tiled=True),
        lax.psum_scatter(grad_key, "fsdp", scatter_dimension=0, tiled=True),
        lax.psum_scatter(grad_value, "fsdp", scatter_dimension=0, tiled=True),
        lax.psum_scatter(grad_out, "fsdp", scatter_dimension=0, tiled=True),
        lax.psum_scatter(grad_up, "fsdp", scatter_dimension=0, tiled=True),
        lax.psum_scatter(grad_down, "fsdp", scatter_dimension=0, tiled=True),
        lax.psum_scatter(grad_proj, "fsdp", scatter_dimension=0, tiled=True),
    )
    summed = (
        lax.psum(shard_query.astype(jnp.bfloat16), "dp").astype(jnp.float32),
        lax.psum(shard_key.astype(jnp.bfloat16), "dp").astype(jnp.float32),
        lax.psum(shard_value.astype(jnp.bfloat16), "dp").astype(jnp.float32),
        lax.psum(shard_out.astype(jnp.bfloat16), "dp").astype(jnp.float32),
        lax.psum(shard_up.astype(jnp.bfloat16), "dp").astype(jnp.float32),
        lax.psum(shard_down.astype(jnp.bfloat16), "dp").astype(jnp.float32),
        lax.psum(shard_proj.astype(jnp.bfloat16), "dp").astype(jnp.float32),
    )
    smalls = lax.psum((grad_gain_attn, grad_gain_ffn, grad_gain_final, grad_table), ("dp", "fsdp"))
    return (
        embeddings,
        input_grad,
        summed[0],
        summed[1],
        summed[2],
        summed[3],
        summed[4],
        summed[5],
        summed[6],
        smalls[0],
        smalls[1],
        smalls[2],
        smalls[3],
    )


def solution(mesh):
    near = (mesh.shape["dp"], mesh.shape["fsdp"]) == (4, 8)
    return jax.shard_map(
        near_device if near else general,
        mesh=mesh,
        in_specs=(
            P(("dp", "fsdp"), None, None),
            P(("dp", "fsdp"), None),
            P(("dp", "fsdp"), None),
            P("fsdp", None),
            P("fsdp", None),
            P("fsdp", None),
            P("fsdp", None),
            P("fsdp", None),
            P("fsdp", None),
            P("fsdp", None),
            P(),
            P(),
            P(),
            P(),
            P(("dp", "fsdp"), None, None),
        ),
        out_specs=(
            P(("dp", "fsdp"), None, None),
            P(("dp", "fsdp"), None, None),
            P("fsdp", None),
            P("fsdp", None),
            P("fsdp", None),
            P("fsdp", None),
            P("fsdp", None),
            P("fsdp", None),
            P("fsdp", None),
            P(),
            P(),
            P(),
            P(),
        ),
        check_vma=False,
    )
```

```python
import math
from functools import partial

import jax
import jax.numpy as jnp
import numpy as np
from jax import lax
from jax.experimental import pallas as pl
from jax.experimental.pallas import tpu as pltpu
from jax.sharding import PartitionSpec as P

REACH = 128


EPSILON = 1e-06
VMEM_BYTES = 60 * 2**20
HIGH = lax.Precision.HIGHEST


def bucket_table(length, buckets, reach):
    positions = np.arange(length)
    relative = positions[None, :] - positions[:, None]
    halfway = buckets // 2
    exact_span = halfway // 2
    distance = np.abs(relative)
    logged = exact_span + (
        np.log(np.maximum(distance, 1) / exact_span)
        / np.log(reach / exact_span)
        * (halfway - exact_span)
    ).astype(np.int64)
    logged = np.minimum(logged, halfway - 1)
    result = (relative > 0).astype(np.int64) * halfway + np.where(
        distance < exact_span, distance, logged
    )
    return result.astype(np.int32)


def rms_forward(values, gain):
    factor = lax.rsqrt(jnp.mean(values * values, axis=-1, keepdims=True) + EPSILON)
    return (values * factor * gain, factor)


def rms_backward(values, factor, gain, upstream):
    normed = values * factor
    gain_grad = jnp.sum(upstream * normed, axis=0)
    inner = upstream * gain
    return (factor * (inner - normed * jnp.mean(inner * normed, axis=-1, keepdims=True)), gain_grad)


def matmul(left, right):
    return jnp.dot(left, right, preferred_element_type=jnp.float32)


def matmul_left(left, right):
    return lax.dot_general(
        left, right, (((0,), (0,)), ((), ())), preferred_element_type=jnp.float32
    )


def matmul_right(left, right):
    return lax.dot_general(
        left, right, (((1,), (1,)), ((), ())), preferred_element_type=jnp.float32
    )


def row_scores(query_row, key_row, seg_row, bias):
    raw_scores = jnp.einsum("qhd,khd->hqk", query_row, key_row, preferred_element_type=jnp.float32)
    same_doc = (seg_row[:, None] == seg_row[None, :])[None]
    return jnp.where(same_doc, raw_scores + bias, -1e30)


MESH = pl.DeviceIdType.MESH
LANES = 128


class Place:
    def __init__(self):
        self.dp, self.fsdp = lax.axis_index("dp"), lax.axis_index("fsdp")
        self.y, self.x = self.dp // 2, self.dp % 2
        self.z, self.c = self.fsdp // 2, self.fsdp % 2

    def core(self):
        return (self.dp, self.z * 2 + (1 - self.c))

    def at_x(self):
        return (self.y * 2 + (1 - self.x), self.fsdp)

    def at_y(self):
        return ((1 - self.y) * 2 + self.x, self.fsdp)

    def at_xy(self):
        return ((1 - self.y) * 2 + (1 - self.x), self.fsdp)

    def up(self, d):
        return lax.rem(self.z + d, 4)

    def down(self, d):
        return lax.rem(self.z + 4 - d, 4)

    def at_z(self, d):
        return (self.dp, self.up(d) * 2 + self.c)

    def greet(self):
        partners = [self.core(), self.at_x(), self.at_y(), self.at_xy()]
        partners += [self.at_z(d) for d in (1, 2, 3)]
        for partner in partners:
            pl.semaphore_signal(
                pltpu.get_barrier_semaphore(), inc=1, device_id=partner, device_id_type=MESH
            )
        self.greeted = len(partners)

    def meet(self):
        pl.semaphore_wait(pltpu.get_barrier_semaphore(), self.greeted)


def remote(src, dst, send, recv, device):
    return pltpu.make_async_remote_copy(
        src_ref=src, dst_ref=dst, send_sem=send, recv_sem=recv, device_id=device, device_id_type=MESH
    )


def half(which, size, start=0):
    return pl.ds(pl.multiple_of(start + which * (size // 2), size // 2 if start % (size // 2) == 0 else 16), size // 2)


class Unit:
    def __init__(self, array, first, rows, left, wide):
        self.array, self.first, self.rows, self.left, self.wide = array, first, rows, left, wide

    def quarter(self, y, x):
        return (half(y, self.rows, self.first), half(x, self.wide, self.left))

    def whole(self):
        return (pl.ds(self.first, self.rows), pl.ds(self.left, self.wide))


class Gather:
    RECVS = 13

    def __init__(self, place, units, shards, wholes, send, recv):
        self.p, self.units, self.shards, self.wholes = place, units, shards, wholes
        self.send, self.recv = send, recv

    def _part(self, u, z, y, x):
        unit = self.units[u]
        return self.wholes[unit.array].at[(z, self.p.c) + unit.quarter(y, x)]

    def _z(self, u, d):
        p, unit = self.p, self.units[u]
        src = self.shards[unit.array].at[unit.quarter(p.y, p.x)]
        return remote(src, self._part(u, p.z, p.y, p.x), self.send.at[u, d - 1], self.recv.at[u, d - 1], p.at_z(d))

    def _hop(self, u, d, kind, y, x, device):
        ref = self._part(u, self.p.down(d), y, x)
        k = 3 * kind + d - 1
        return remote(ref, ref, self.send.at[u, k], self.recv.at[u, k], device)

    def _to_x(self, u, d):
        return self._hop(u, d, 1, self.p.y, self.p.x, self.p.at_x())

    def _to_y(self, u, d):
        return self._hop(u, d, 2, self.p.y, self.p.x, self.p.at_y())

    def _through_x(self, u, d):
        return (u + d) % 2 == 0

    def _diagonal(self, u, d):
        p = self.p
        if self._through_x(u, d):
            return self._hop(u, d, 3, p.y, 1 - p.x, p.at_y())
        return self._hop(u, d, 3, 1 - p.y, p.x, p.at_x())

    def _core(self, u):
        unit = self.units[u]
        ref = self.wholes[unit.array].at[(slice(None), self.p.c) + unit.whole()]
        return remote(ref, ref, self.send.at[u, 12], self.recv.at[u, 12], self.p.core())

    def start(self, u):
        for d in (1, 2, 3):
            self._z(u, d).start()

    def plane(self, u):
        for d in (1, 2, 3):
            self._z(u, d).wait_recv()
            self._to_x(u, d).start()
            self._to_y(u, d).start()

    def corner(self, u):
        for d in (1, 2, 3):
            first, second = (self._to_x, self._to_y) if self._through_x(u, d) else (self._to_y, self._to_x)
            first(u, d).wait_recv()
            self._diagonal(u, d).start()
            second(u, d).wait_recv()

    def pair(self, u):
        for d in (1, 2, 3):
            self._diagonal(u, d).wait_recv()
        self._core(u).start()

    def arrive(self, u):
        self._core(u).wait_recv()

    def finish(self, u):
        for d in (1, 2, 3):
            self._z(u, d).wait_send()
            self._to_x(u, d).wait_send()
            self._to_y(u, d).wait_send()
            self._diagonal(u, d).wait_send()
        self._core(u).wait_send()


def gather_units():
    small = [Unit(i, 0, 96, 0, 768) for i in range(4)]
    up = [Unit(4, 0, 96, 768 * j, 768) for j in range(4)]
    down = [Unit(5, 128 * j, 128, 0, 768) for j in range(3)]
    return small + up + [Unit(6, 0, 96, 0, 768)] + down


def dot(a, b, ca=1, cb=0):
    return lax.dot_general(a, b, (((ca,), (cb,)), ((), ())), preferred_element_type=jnp.float32)


def dot_exact(a, b, ca=1, cb=0):
    return lax.dot_general(
        a, b, (((ca,), (cb,)), ((), ())), precision=HIGH, preferred_element_type=jnp.float32
    )


def low(v):
    return v.astype(jnp.bfloat16)


def wide(v):
    return v.astype(jnp.float32)


def two_parts(v):
    high = wide(low(v))
    return low(jnp.concatenate([high, v - high], axis=0))


def norm_factor(v):
    return lax.rsqrt(jnp.mean(v * v, axis=-1, keepdims=True) + EPSILON)


def norm_back(v, factor, gain, upstream):
    normed = v * factor
    inner = upstream * gain
    grad = factor * (inner - normed * jnp.mean(inner * normed, axis=-1, keepdims=True))
    return grad, jnp.sum(upstream * normed, axis=0, keepdims=True)


def gelu_both(v):
    scale = math.sqrt(2.0 / math.pi)
    square = v * v
    bent = jnp.tanh(scale * v * (1.0 + 0.044715 * square))
    share = 0.5 + 0.5 * bent
    slope = share + (0.5 * scale) * v * (1.0 - bent * bent) * (1.0 + (3 * 0.044715) * square)
    return v * share, slope


def flat(ref, *where):
    value = ref[where] if where else ref[...]
    return value.reshape(-1, value.shape[-1])


TILE, SPAN = 128, 384


def rows_of(t):
    return pl.ds(t * TILE, TILE)


def span_of(t):
    return pl.ds(t * TILE, SPAN)


def heads_of(p):
    return pl.ds(pl.multiple_of(p * LANES, LANES), LANES)


def stacked(v, axis=0):
    first = lax.broadcasted_iota(jnp.int32, v.shape, 1) < LANES // 2
    zero = jnp.zeros_like(v)
    return jnp.concatenate([jnp.where(first, v, zero), jnp.where(first, zero, v)], axis=axis)


def side_by_side(v):
    return jnp.concatenate([v[:TILE], v[TILE:]], axis=1)


def probs_at(p, t):
    return (pl.ds(pl.multiple_of((p // 2) * 256, 256), 256), pl.ds(pl.multiple_of((p % 2) * 1536, 1536) + t * SPAN, SPAN))


def attend(p, t, q, keys, values, band, mask, probs, mixed):
    scores = dot(stacked(q[rows_of(t), heads_of(p)]), keys[span_of(t), heads_of(p)], 1, 1)
    hidden = mask[t]
    scores = scores + band[p] + jnp.concatenate([hidden, hidden], axis=0)
    powered = jnp.exp(scores - jnp.max(scores, axis=1, keepdims=True))
    soft = low(powered * (1.0 / jnp.sum(powered, axis=1, keepdims=True)))
    probs[probs_at(p, t)] = soft
    out = dot(side_by_side(soft), stacked(values[span_of(t), heads_of(p)]))
    mixed[rows_of(t), heads_of(p)] = low(out)


def forward_kernel(units, *refs):
    x_ref, seg_ref, pool_ref, emb_ref, g1_ref, g2_ref, g3_ref, table_ref, near_ref = refs[:9]
    shards, refs = refs[9:16], refs[16:]
    w_outs, big_outs, small_outs, refs = refs[:6], refs[6:17], refs[17:21], refs[21:]
    wholes, refs = refs[:7], refs[7:]
    held, refs = refs[:10], refs[10:]
    act, slope, n1, n2, mixed, q, keys, values, probs, h1 = held
    h2, band, mask = refs[:3]
    send, recv, local, ready = refs[3:]
    emb_out, pooled_out, eg_out, top_out = small_outs
    wq, wk, wv, wo, wup, wdn, wpj = wholes
    place = Place()
    gather = Gather(place, units, shards, wholes, send, recv)
    own = [
        pltpu.make_async_copy(shard, whole.at[place.z, place.c], local.at[i])
        for i, (shard, whole) in enumerate(zip(shards, wholes))
    ]
    backs = [pltpu.make_async_copy(a, b, local.at[7 + i]) for i, (a, b) in enumerate(zip(wholes[:6], w_outs))]
    keeps = [pltpu.make_async_copy(a, b, ready.at[i]) for i, (a, b) in enumerate(zip(held, big_outs))]
    for copy in own:
        copy.start()
    place.greet()
    place.meet()
    n = len(units)
    stages = (gather.plane, gather.corner, gather.pair, gather.arrive)

    def step(t):
        for lag, stage in enumerate(stages):
            if 0 <= t - lag < n:
                stage(t - lag)
                if lag == 0 and t + 2 < n:
                    gather.start(t + 2)

    for u in range(2):
        gather.start(u)
    for copy in own:
        copy.wait()

    x = wide(x_ref[...])
    n1[...] = low(x * norm_factor(x) * g1_ref[...].reshape(1, 768))
    step(0)
    ray = dot_exact(table_ref[...], near_ref[...])
    for h in range(ray.shape[0]):
        rolled = pltpu.roll(jnp.broadcast_to(ray[h : h + 1], (TILE, 512)), 0, 1, stride=1, stride_axis=0)
        band[h // 2, pl.ds((h % 2) * TILE, TILE), :] = rolled[:, :SPAN]
    step(1)
    seg = seg_ref[...]
    seg_f = wide(seg)
    column = jnp.transpose(jnp.broadcast_to(seg_f, (TILE, 512)))
    edge = jnp.full((1, TILE), -1.0, jnp.float32)
    line = jnp.concatenate([edge, seg_f, edge], axis=1)
    for t in range(4):
        own_seg = column[t * TILE : (t + 1) * TILE]
        same = jnp.concatenate([own_seg] * 3, axis=1) == line[:, t * TILE : t * TILE + SPAN]
        mask[t] = jnp.where(same, 0.0, -1e30)
    blank = jnp.zeros((TILE, 768), jnp.bfloat16)
    for ref in (keys, values):
        ref[pl.ds(0, TILE), :] = blank
        ref[pl.ds(640, TILE), :] = blank
    step(2)
    step(3)
    q[...] = low(dot(n1[...], flat(wq)))
    backs[0].start()
    step(4)
    keys[pl.ds(TILE, 512), :] = low(dot(n1[...], flat(wk)))
    backs[1].start()
    step(5)
    values[pl.ds(TILE, 512), :] = low(dot(n1[...], flat(wv)))
    backs[2].start()
    for i in (2, 5, 6, 7):
        keeps[i].start()

    def pairs(first, last):
        @pl.loop(first, last)
        def _(p):
            for t in range(4):
                attend(p, t, q, keys, values, band, mask, probs, mixed)

    pairs(0, 2)
    step(6)
    pairs(2, 4)
    step(7)
    pairs(4, 6)
    backs[3].start()
    keeps[8].start()
    keeps[4].start()
    hidden = wide(x_ref[...]) + dot(mixed[...], flat(wo))
    h1[...] = hidden
    n2[...] = low(hidden * norm_factor(hidden) * g2_ref[...].reshape(1, 768))
    keeps[3].start()
    keeps[9].start()
    for j in range(4):
        cols = pl.ds(768 * j, 768)
        value, grad = gelu_both(dot(n2[...], flat(wup, slice(None), slice(None), slice(None), cols)))
        act[:, cols] = low(value)
        slope[:, cols] = low(grad)
        step(8 + j)
    backs[4].start()
    keeps[0].start()
    keeps[1].start()
    for j in range(3):
        step(12 + j)
        part = jnp.concatenate([act[:, pl.ds(384 * s + 128 * j, 128)] for s in range(8)], axis=1)
        more = dot(part, flat(wdn, slice(None), slice(None), pl.ds(128 * j, 128)))
        h2[...] = (h1[...] if j == 0 else h2[...]) + more
    backs[5].start()
    h = h2[...]
    factor = norm_factor(h)
    fin = h * factor * g3_ref[...].reshape(1, 768)
    eye = lax.broadcasted_iota(jnp.int32, (8, 8), 0) == lax.broadcasted_iota(jnp.int32, (8, 8), 1)
    pool = jnp.sum(jnp.where(eye, wide(pool_ref[...]), 0.0), axis=1, keepdims=True)
    member = jnp.where(seg_f == pool, 1.0, 0.0)
    count = jnp.sum(member, axis=1, keepdims=True)
    fin_high = low(fin)
    pooled = (dot(low(member), fin_high) + dot(low(member), low(fin - wide(fin_high)))) / count
    wp = flat(wpj)
    both = dot(two_parts(pooled), wp)
    projected = both[:8] + both[8:]
    inverse = lax.rsqrt(jnp.sum(projected * projected, axis=-1, keepdims=True) + EPSILON)
    emb = projected * inverse
    up = emb_ref[...].reshape(8, 768)
    eg = inverse * (up - emb * jnp.sum(up * emb, axis=-1, keepdims=True))
    both = dot(two_parts(eg), wp, 1, 1)
    pooled_grad = (both[:8] + both[8:]) / count
    twice = low(jnp.concatenate([member, member], axis=0))
    fin_grad = dot(twice, two_parts(pooled_grad), 0, 0)
    stream, gain_grad = norm_back(h, factor, g3_ref[...].reshape(1, 768), fin_grad)
    emb_out[...] = emb
    pooled_out[...] = pooled
    eg_out[...] = eg
    h2[...] = stream
    top_out[...] = gain_grad
    last = pltpu.make_async_copy(h2, big_outs[10], ready.at[10])
    last.start()
    for u in range(n):
        gather.finish(u)
    for copy in (*backs, *keeps, last):
        copy.wait()


def bucket_rows(away, buckets):
    halfway = buckets // 2
    exact = halfway // 2
    distance = np.abs(away)
    logged = exact + (
        np.log(np.maximum(distance, 1) / exact) / np.log(REACH / exact) * (halfway - exact)
    ).astype(np.int64)
    bucket = (away > 0) * halfway + np.where(distance < exact, distance, np.minimum(logged, halfway - 1))
    return (np.arange(buckets)[:, None] == bucket[None, :]).astype(np.float32)


def ray_buckets(buckets):
    near = np.arange(512)
    return bucket_rows(np.where(near < SPAN, near - TILE, near - 512 - TILE), buckets)


def forward_all(x, seg_ids, pool_index, emb_grad, gains, table, shards):
    units = gather_units()
    full = [(4, 2) + shard.shape for shard in shards]
    low_shapes = [(512, 3072)] * 2 + [(512, 768)] * 4 + [(768, 768)] * 2 + [(768, 3072)]
    held = [jax.ShapeDtypeStruct(s, jnp.bfloat16) for s in low_shapes]
    held.append(jax.ShapeDtypeStruct((512, 768), jnp.float32))
    outs = [jax.ShapeDtypeStruct(s, jnp.bfloat16) for s in full[:6]]
    outs += held + [jax.ShapeDtypeStruct((512, 768), jnp.float32)]
    n_large = len(outs)
    outs += [jax.ShapeDtypeStruct((8, 768), jnp.float32)] * 3 + [jax.ShapeDtypeStruct((1, 768), jnp.float32)]
    vmem, large = pl.BlockSpec(memory_space=pltpu.VMEM), pl.BlockSpec(memory_space=pl.ANY)
    return pl.pallas_call(
        partial(forward_kernel, units),
        out_shape=outs,
        in_specs=[vmem] * 9 + [large] * 7,
        out_specs=[large] * n_large + [vmem] * 4,
        scratch_shapes=[pltpu.VMEM(shape, jnp.bfloat16) for shape in full]
        + [pltpu.VMEM(h.shape, h.dtype) for h in held]
        + [
            pltpu.VMEM((512, 768), jnp.float32),
            pltpu.VMEM((6, 2 * TILE, SPAN), jnp.float32),
            pltpu.VMEM((4, TILE, SPAN), jnp.float32),
            pltpu.SemaphoreType.DMA((len(units), Gather.RECVS)),
            pltpu.SemaphoreType.DMA((len(units), Gather.RECVS)),
            pltpu.SemaphoreType.DMA((13,)),
            pltpu.SemaphoreType.DMA((11,)),
        ],
        compiler_params=pltpu.CompilerParams(
            collective_id=0, has_side_effects=True, vmem_limit_bytes=VMEM_BYTES
        ),
        name="forward",
    )(x, seg_ids, pool_index, emb_grad, *gains, table, ray_buckets(table.shape[1]), *shards)


class Reduce:
    SEMS = 11

    @staticmethod
    def shapes(rows):
        return [(2, rows, 384), (2, rows // 2, 768), (2, rows // 2, 384), (2, rows // 2, 384), (3, rows // 2, 384)]

    def __init__(self, place, through_x, grad, own, core, total, buffers, send, recv):
        self.p, self.g, self.own, self.rc, self.f = place, grad, own, core, total
        self.through_x, self.send, self.recv = through_x, send, recv
        self._take(buffers)
        p = place
        self.row = [half(i, own.shape[1]) for i in (p.y, 1 - p.y)]
        self.col = [half(i, 768) for i in (p.x, 1 - p.x)]

    def _take(self, buffers):
        self.rx, self.ry, self.sx, self.sy, self.rz = buffers

    def _copy(self, k, src, dst, device):
        return remote(src, dst, self.send.at[k], self.recv.at[k], device)

    def _core(self):
        return self._copy(0, self.g.at[:, 1 - self.p.c], self.rc, self.p.core())

    def _first(self):
        p, low, high = self.p, pl.ds(0, 2), pl.ds(2, 2)
        return [
            self._copy(1, self.own.at[low, :, self.col[1]], self.rx, p.at_x()),
            self._copy(2, self.own.at[high, self.row[1], :], self.ry, p.at_y()),
        ]

    def _second(self):
        p, low, high = self.p, pl.ds(0, 2), pl.ds(2, 2)
        return [
            self._copy(3, self.own.at[low, self.row[1], self.col[0]], self.sy, p.at_y()),
            self._copy(4, self.own.at[high, self.row[0], self.col[1]], self.sx, p.at_x()),
        ]

    def _third(self):
        p = self.p
        return [
            self._copy(4 + d, self.own.at[p.up(d), self.row[0], self.col[0]], self.rz.at[d - 1], p.at_z(d))
            for d in (1, 2, 3)
        ]

    def _spread(self):
        p, part = self.p, self.f.at[self.row[0], self.col[0]]
        return [self._copy(8 + i, part, part, device) for i, device in enumerate((p.at_x(), p.at_y()))]

    def _corner(self):
        p = self.p
        if self.through_x:
            part, device = self.f.at[self.row[0], self.col[1]], p.at_y()
        else:
            part, device = self.f.at[self.row[1], self.col[0]], p.at_x()
        return self._copy(10, part, part, device)

    def _add(self, where, other):
        self.own[where] = low(wide(self.own[where]) + wide(other[...]))

    def start(self):
        self._core().start()

    def first(self):
        self._core().wait()
        for i in range(4):
            self.own[i] = low(wide(self.g[i, self.p.c]) + wide(self.rc[i]))
        for copy in self._first():
            copy.start()

    def second(self):
        along_x, along_y = self._first()
        to_y, to_x = self._second()
        along_x.wait_recv()
        for i in range(2):
            self._add((i, slice(None), self.col[0]), self.rx.at[i])
        to_y.start()
        along_y.wait_recv()
        for i in range(2):
            self._add((2 + i, self.row[0], slice(None)), self.ry.at[i])
        to_x.start()

    def third(self):
        for copy in self._second():
            copy.wait_recv()
        for i in range(2):
            self._add((i, self.row[0], self.col[0]), self.sy.at[i])
            self._add((2 + i, self.row[0], self.col[0]), self.sx.at[i])
        for copy in self._third():
            copy.start()

    def _total(self):
        total = wide(self.own[self.p.z, self.row[0], self.col[0]])
        for d, copy in enumerate(self._third()):
            copy.wait_recv()
            total = total + wide(self.rz[d])
        return total

    def spread(self):
        self.f[self.row[0], self.col[0]] = low(self._total())
        for copy in self._spread():
            copy.start()

    def corner(self):
        along_x, along_y = self._spread()
        early, later = (along_x, along_y) if self.through_x else (along_y, along_x)
        early.wait_recv()
        self._corner().start()
        later.wait_recv()

    def arrive(self):
        self._corner().wait_recv()

    def finish(self):
        for copy in (*self._first(), *self._second(), *self._third(), *self._spread(), self._corner()):
            copy.wait_send()


class LineFirst(Reduce):
    @staticmethod
    def shapes(rows):
        return [(3, rows, 768), (rows, 384), (rows // 2, 768), (rows // 2, 384)]

    def _take(self, buffers):
        self.rz, self.rx, self.ry, self.rq = buffers

    def _mine(self):
        return self.own.at[self.p.z]

    def _first(self):
        p = self.p
        return [self._copy(d, self.own.at[p.up(d)], self.rz.at[d - 1], p.at_z(d)) for d in (1, 2, 3)]

    def _second(self):
        if self.through_x:
            return [self._copy(4, self._mine().at[:, self.col[1]], self.rx, self.p.at_x())]
        return [self._copy(4, self._mine().at[self.row[1], :], self.ry, self.p.at_y())]

    def _third(self):
        if self.through_x:
            return [self._copy(5, self._mine().at[self.row[1], self.col[0]], self.rq, self.p.at_y())]
        return [self._copy(5, self._mine().at[self.row[0], self.col[1]], self.rq, self.p.at_x())]

    def second(self):
        total = wide(self._mine()[...])
        for d, copy in enumerate(self._first()):
            copy.wait_recv()
            total = total + wide(self.rz[d])
        self._mine()[...] = low(total)
        self._second()[0].start()

    def third(self):
        self._second()[0].wait_recv()
        if self.through_x:
            self._add((self.p.z, slice(None), self.col[0]), self.rx)
        else:
            self._add((self.p.z, self.row[0], slice(None)), self.ry)
        self._third()[0].start()

    def _total(self):
        self._third()[0].wait_recv()
        return wide(self.own[self.p.z, self.row[0], self.col[0]]) + wide(self.rq[...])


class Small:
    SEMS = 6

    def __init__(self, place, sums, got, line, send, recv):
        self.p, self.sums, self.got, self.line, self.send, self.recv = place, sums, got, line, send, recv

    def _pair(self, i):
        device = (self.p.core, self.p.at_x, self.p.at_y)[i]()
        return remote(self.sums.at[i], self.got.at[i], self.send.at[i], self.recv.at[i], device)

    def _line(self):
        p = self.p
        return [
            remote(self.sums.at[3], self.line.at[p.z], self.send.at[2 + d], self.recv.at[2 + d], p.at_z(d))
            for d in (1, 2, 3)
        ]

    def start(self):
        self._pair(0).start()

    def turn(self, i):
        self._pair(i).wait_recv()
        self.sums[i + 1] = self.sums[i] + self.got[i]
        if i < 2:
            self._pair(i + 1).start()
        else:
            self.line[self.p.z] = self.sums[3]
            for copy in self._line():
                copy.start()

    def finish(self):
        for copy in self._line():
            copy.wait()
        for i in range(3):
            self._pair(i).wait_send()
        return self.line[0] + self.line[1] + self.line[2] + self.line[3]


RING = 3
BLOCKS = [
    (6, 0, 96, True),
    (5, 0, 128, False),
    (5, 1, 128, False),
    (5, 2, 128, False),
    (4, 0, 96, False),
    (4, 1, 96, True),
    (4, 2, 96, False),
    (4, 3, 96, False),
    (3, 0, 96, False),
    (2, 0, 96, False),
    (1, 0, 96, False),
    (0, 0, 96, False),
]
PLAN = {
    "g0": [(0, 0)],
    "g1": [(0, 1)],
    "g2": [(1, 0), (0, 2), (1, 1)],
    "g3": [(0, 3), (1, 2)],
    "g5": [(0, 5), (1, 3), (0, 4)],
    "g6": [(1, 5), (0, 6), (2, 2), (1, 4)],
    "g7": [(0, 7)],
    "n3": [(2, 1)],
    "g8": [(0, 8), (1, 6), (2, 4)],
    "a0": [(2, 3), (2, 0), (1, 8), (3, 1)],
    "a1": [(1, 7)],
    "a2": [(3, 0), (3, 4), (2, 6)],
    "a3": [(2, 5), (2, 8)],
    "a4": [(3, 2)],
    "a5": [(4, 0), (4, 1)],
    "g9": [(0, 9), (3, 6), (3, 5), (2, 7)],
    "g10": [(1, 9), (0, 10)],
    "g11": [(3, 3), (3, 7), (0, 11), (1, 10), (2, 9), (3, 8), (1, 11)],
    "tail": [(3, 9), (4, 6), (2, 10), (2, 11), (4, 7), (4, 4), (5, 1), (3, 10), (5, 6), (4, 3), (3, 11), (4, 2), (4, 9), (4, 8), (4, 5), (6, 6), (5, 4)],
    "table": [(6, 1), (5, 3), (5, 0), (5, 2), (5, 7), (4, 10), (6, 4), (5, 5), (4, 11), (5, 8), (5, 9), (6, 0), (6, 2), (5, 10), (6, 3), (6, 5), (5, 11), (6, 8), (6, 7), (6, 9), (6, 10), (6, 11)],
}


def attend_back(p, t, held, keys, values, probs, sums, table):
    def heads_at(base):
        return pl.ds(pl.multiple_of(p * LANES + base, LANES), LANES)

    heads = heads_at(0)
    ups = stacked(held[rows_of(t), heads_at(768)])
    qs = stacked(held[rows_of(t), heads])
    soft = probs[probs_at(p, t)]
    weighted = wide(soft) * dot(ups, values[span_of(t), heads], 1, 1)
    grad = weighted - wide(soft) * jnp.sum(weighted, axis=1, keepdims=True)
    grad_low = low(grad)
    out = dot(side_by_side(grad_low), stacked(keys[span_of(t), heads]))
    held[rows_of(t), heads_at(1536)] = low(out)
    sums[pl.ds(t * TILE, SPAN), heads] += dot(grad_low, qs, 0, 0)
    sums[pl.ds(768 + t * TILE, SPAN), heads] += dot(soft, ups, 0, 0)
    table[p] += grad


def backward_kernel(*refs):
    pooled_ref, eg_ref, g1_ref, g2_ref, top_ref, far_ref = refs[:6]
    stream_in, act_in, slope_in, n1_in, n2_in, mixed_in, q_in, keys_in, values_in, probs_in, h1_in, x_in = refs[6:18]
    wq_in, wk_in, wv_in, wo_in, wup_in, wdn_in = refs[18:24]
    outs, input_out, small_out, refs = refs[24:31], refs[31], refs[32], refs[33:]
    held, pre, wup, wdn, n2, mixed, upstream, keys, values, stream, sums, table, rays = refs[:13]
    ring, refs = refs[13], refs[14:]
    buffers = []
    for _, _, rows, line_first in BLOCKS:
        count = 3 + len((LineFirst if line_first else Reduce).shapes(rows))
        buffers.append(refs[:count])
        refs = refs[count:]
    small_sums, small_got, small_line = refs[:3]
    send, recv, local, writes, small_send, small_recv = refs[3:]
    place = Place()
    loads = {}

    def load(name, src, dst):
        loads[name] = pltpu.make_async_copy(src, dst, local.at[len(loads)])
        loads[name].start()

    def part(ref, i):
        return ref.at[:, pl.ds(768 * i, 768)]

    load("stream", stream_in, stream)
    load("act", act_in, held)
    load("wdn", wdn_in, wdn)
    load("slope", slope_in, pre)
    load("n2", n2_in, n2)
    load("wup", wup_in, wup)
    load("h1", h1_in, sums.at[pl.ds(0, 512), :])
    load("mixed", mixed_in, mixed)
    load("keys", keys_in, keys)
    load("values", values_in, values)
    place.greet()

    works, results = [], []
    for u, (array, j, rows, line_first) in enumerate(BLOCKS):
        own, core, total, *rest = buffers[u]
        grad = ring.at[u % RING, :, :, pl.ds(0, rows), :]
        kind = LineFirst if line_first else Reduce
        works.append(kind(place, u % 2 == 0, grad, own, core, total, rest, send.at[u], recv.at[u]))
        dst = outs[5].at[pl.ds(128 * j, 128), :] if array == 5 else outs[array].at[:, pl.ds(768 * j, 768)]
        results.append(pltpu.make_async_copy(total, dst, writes.at[u]))
    n = len(BLOCKS)

    def put(u, value):
        works[u].g[...] = low(value).reshape(works[u].g.shape)

    def produce(u, value):
        put(u, value)
        if u == 0:
            place.meet()
        serve(f"g{u}")

    def end(u):
        works[u].arrive()
        results[u].start()

    def take(stage, u):
        work = works[u]
        if stage == 6:
            end(u)
        else:
            (work.start, work.first, work.second, work.third, work.spread, work.corner)[stage]()

    def serve(name):
        for stage, u in PLAN.get(name, ()):
            take(stage, u)

    pooled, eg = pooled_ref[...], eg_ref[...]
    pooled_high, eg_high = wide(low(pooled)), wide(low(eg))
    left = jnp.concatenate([pooled_high, pooled_high, pooled - pooled_high], axis=0)
    right = jnp.concatenate([eg_high, eg - eg_high, eg_high], axis=0)
    produce(0, dot(low(left), low(right), 0, 0))
    loads["stream"].wait()
    upstream[...] = low(stream[...])
    loads["act"].wait()
    for j in range(3):
        picked = jnp.concatenate([held[:, pl.ds(384 * s + 128 * j, 128)] for s in range(8)], axis=1)
        produce(1 + j, dot(picked, upstream[...], 0, 0))
    load("q", q_in, part(held, 0))
    load("n1", n1_in, part(held, 3))
    for name in ("wdn", "slope", "n2", "wup"):
        loads[name].wait()
    for j in range(4):
        cols = pl.ds(768 * j, 768)
        grad = low(wide(pre[:, cols]) * dot(upstream[...], wdn[cols, :], 1, 1))
        pre[:, cols] = grad
        produce(4 + j, dot(n2[...], grad, 0, 0))
        more = dot(grad, wup[:, cols], 1, 1)
        where = pl.ds(512, 512)
        sums[where, :] = more if j == 0 else sums[where, :] + more
        serve(f"n{j}")
    for i, ref in enumerate((wo_in, wq_in, wk_in, wv_in)):
        load(f"w{i}", ref, wdn.at[pl.ds(768 * i, 768), :])
    load("probs", probs_in, wup)
    load("x", x_in, n2)
    loads["h1"].wait()
    h1 = sums[pl.ds(0, 512), :]
    more, gain_two = norm_back(h1, norm_factor(h1), g2_ref[...].reshape(1, 768), sums[pl.ds(512, 512), :])
    through = stream[...] + more
    stream[...] = through
    upstream[...] = low(through)
    loads["mixed"].wait()
    produce(8, dot(mixed[...], upstream[...], 0, 0))
    loads["w0"].wait()
    part(held, 1)[...] = low(dot(upstream[...], wdn[pl.ds(0, 768), :], 1, 1))
    sums[...] = jnp.zeros_like(sums)
    table[...] = jnp.zeros_like(table)
    serve("og")
    for name in ("keys", "values", "q", "probs"):
        loads[name].wait()

    def pairs(first, last):
        @pl.loop(first, last)
        def _(p):
            for t in range(4):
                attend_back(p, t, held, keys, values, wup, sums, table)

    first = 0
    for p in range(6):
        if p == 5 or PLAN.get(f"a{p}"):
            pairs(first, p + 1)
            first = p + 1
        serve(f"a{p}")
    loads["n1"].wait()
    n1 = held[:, pl.ds(2304, 768)]
    vg, kg = low(sums[pl.ds(768 + TILE, 512), :]), low(sums[pl.ds(TILE, 512), :])
    produce(9, dot(n1, vg, 0, 0))
    produce(10, dot(n1, kg, 0, 0))
    qg = held[:, pl.ds(1536, 768)]
    produce(11, dot(n1, qg, 0, 0))
    for name in ("w1", "w2", "w3", "x"):
        loads[name].wait()
    n1_grad = dot(qg, wdn[pl.ds(768, 768), :], 1, 1) + dot(kg, wdn[pl.ds(1536, 768), :], 1, 1)
    n1_grad = n1_grad + dot(vg, wdn[pl.ds(2304, 768), :], 1, 1)
    x = wide(n2[...])
    more, gain_one = norm_back(x, norm_factor(x), g1_ref[...].reshape(1, 768), n1_grad)
    stream[...] = stream[...] + more
    last = pltpu.make_async_copy(stream, input_out, writes.at[n])
    last.start()
    serve("tail")
    turn = lax.broadcasted_iota(jnp.int32, (TILE, TILE), 0) + lax.broadcasted_iota(jnp.int32, (TILE, TILE), 1)
    mirror = low(jnp.where(turn == TILE - 1, 1.0, 0.0))
    rays[...] = jnp.zeros_like(rays)
    for h in range(12):
        tile = table[h // 2, pl.ds((h % 2) * TILE, TILE), :]
        high = low(tile)
        upside = dot(mirror, high) + dot(mirror, low(tile - wide(high)))
        spread = jnp.concatenate([upside, jnp.zeros((TILE, 512 - SPAN), jnp.float32)], axis=1)
        rolled = pltpu.roll(spread, 0, 1, stride=1, stride_axis=0)
        rays[pl.ds(h, 1), :] = jnp.sum(rolled, axis=0, keepdims=True)
    by_bucket = dot_exact(rays[...], far_ref[...], 1, 1)
    small_sums[0, :, pl.ds(0, 768)] = jnp.concatenate(
        [gain_one, gain_two, top_ref[...], jnp.zeros((5, 768), jnp.float32)], axis=0
    )
    small_sums[0, :, pl.ds(768, 128)] = by_bucket[:8]
    small_sums[0, :, pl.ds(896, 128)] = by_bucket[8:]
    small = Small(place, small_sums, small_got, small_line, small_send, small_recv)
    small.start()
    rest = PLAN["table"]
    for i in range(len(rest)):
        if i in (4, 9, 14):
            small.turn(i // 5)
        take(*rest[i])
    small_out[...] = small.finish()
    for u in range(n):
        works[u].finish()
        results[u].wait()
    last.wait()


def far_buckets(buckets):
    rows = np.zeros((LANES, 512), np.float32)
    rows[:buckets] = bucket_rows(np.arange(512) - 255, buckets)
    return rows


def backward_all(smalls, saved, x, weights, buckets):
    f32, b16 = jnp.float32, jnp.bfloat16
    buffers = []
    for _, _, rows, line_first in BLOCKS:
        shapes = [(4, rows, 768), (4, rows, 768), (rows, 768)]
        shapes += (LineFirst if line_first else Reduce).shapes(rows)
        buffers += [pltpu.VMEM(shape, b16) for shape in shapes]
    n = len(BLOCKS)
    outs = [jax.ShapeDtypeStruct(s, b16) for s in [(96, 768)] * 4 + [(96, 3072), (384, 768), (96, 768)]]
    outs += [jax.ShapeDtypeStruct((512, 768), f32), jax.ShapeDtypeStruct((8, 1024), f32)]
    vmem, large = pl.BlockSpec(memory_space=pltpu.VMEM), pl.BlockSpec(memory_space=pl.ANY)
    operands = (*smalls, far_buckets(buckets), *saved, x, *weights)
    return pl.pallas_call(
        backward_kernel,
        out_shape=outs,
        in_specs=[vmem] * 6 + [large] * 18,
        out_specs=[large] * 8 + [vmem],
        scratch_shapes=[
            pltpu.VMEM((512, 3072), b16),
            pltpu.VMEM((512, 3072), b16),
            pltpu.VMEM((768, 3072), b16),
            pltpu.VMEM((3072, 768), b16),
            pltpu.VMEM((512, 768), b16),
            pltpu.VMEM((512, 768), b16),
            pltpu.VMEM((512, 768), b16),
            pltpu.VMEM((768, 768), b16),
            pltpu.VMEM((768, 768), b16),
            pltpu.VMEM((512, 768), f32),
            pltpu.VMEM((1536, 768), f32),
            pltpu.VMEM((6, 2 * TILE, SPAN), f32),
            pltpu.VMEM((16, 512), f32),
            pltpu.VMEM((RING, 4, 2, 128, 768), b16),
        ]
        + buffers
        + [
            pltpu.VMEM((4, 8, 1024), f32),
            pltpu.VMEM((3, 8, 1024), f32),
            pltpu.VMEM((4, 8, 1024), f32),
            pltpu.SemaphoreType.DMA((n, Reduce.SEMS)),
            pltpu.SemaphoreType.DMA((n, Reduce.SEMS)),
            pltpu.SemaphoreType.DMA((20,)),
            pltpu.SemaphoreType.DMA((n + 1,)),
            pltpu.SemaphoreType.DMA((Small.SEMS,)),
            pltpu.SemaphoreType.DMA((Small.SEMS,)),
        ],
        compiler_params=pltpu.CompilerParams(
            collective_id=1, has_side_effects=True, vmem_limit_bytes=VMEM_BYTES
        ),
        name="backward",
    )(*operands)


def finish_kernel(emb_in, input_in, small_in, *refs):
    grads, outs = refs[:7], refs[7:]
    emb_out, input_out, gains, table = outs[0], outs[1], outs[9:12], outs[12]
    emb_out[...] = emb_in[...].reshape(emb_out.shape)
    input_out[...] = input_in[...].reshape(input_out.shape)
    for grad, out in zip(grads, outs[2:9]):
        out[...] = wide(grad[...])
    for i, gain in enumerate(gains):
        gain[...] = small_in[pl.ds(i, 1), pl.ds(0, 768)].reshape(768)
    both = jnp.concatenate([small_in[:, pl.ds(768, 128)], small_in[:, pl.ds(896, 128)]], axis=0)
    table[...] = both[:12, :32]


def finish_all(emb, input_grad, small, grads):
    f32 = jnp.float32
    shapes = [(1, 8, 768), (1, 512, 768)] + [g.shape for g in grads] + [(768,)] * 3 + [(12, 32)]
    vmem = pl.BlockSpec(memory_space=pltpu.VMEM)
    return pl.pallas_call(
        finish_kernel,
        out_shape=[jax.ShapeDtypeStruct(s, f32) for s in shapes],
        in_specs=[vmem] * 10,
        out_specs=[vmem] * 13,
        compiler_params=pltpu.CompilerParams(vmem_limit_bytes=VMEM_BYTES),
        name="finish",
    )(emb, input_grad, small, *grads)


def near_device(
    inputs,
    seg_ids,
    pool_index,
    w_query,
    w_key,
    w_value,
    w_out,
    w_up,
    w_down,
    w_proj,
    gain_attn,
    gain_ffn,
    gain_final,
    bias_table,
    emb_grad,
):
    x = inputs.reshape(-1, inputs.shape[-1])
    shards = (w_query, w_key, w_value, w_out, w_up, w_down, w_proj)
    gains = (gain_attn, gain_ffn, gain_final)
    done = forward_all(x, seg_ids, pool_index, emb_grad, gains, bias_table.T, shards)
    weights = [w.reshape(-1, w.shape[-1]) for w in done[:6]]
    act, slope, n1, n2, mixed, q, keys, values, probs, h1, stream = done[6:17]
    emb, pooled, eg, top = done[17:]
    saved = (stream, act, slope, n1, n2, mixed, q, keys, values, probs, h1)
    result = backward_all((pooled, eg, gain_attn, gain_ffn, top), saved, x, weights, bias_table.shape[0])
    out = finish_all(emb, result[7], result[8], result[:7])
    return (*out[:12], out[12].T)


def general(
    inputs,
    seg_ids,
    pool_index,
    w_query,
    w_key,
    w_value,
    w_out,
    w_up,
    w_down,
    w_proj,
    gain_attn,
    gain_ffn,
    gain_final,
    bias_table,
    emb_grad,
):
    rows, length, width = inputs.shape
    buckets, heads = bias_table.shape
    head_dim = width // heads
    tokens = rows * length
    head_shape = (rows, length, heads, head_dim)
    gathered = (
        lax.all_gather(w_query, "fsdp", axis=0, tiled=True),
        lax.all_gather(w_key, "fsdp", axis=0, tiled=True),
        lax.all_gather(w_value, "fsdp", axis=0, tiled=True),
        lax.all_gather(w_out, "fsdp", axis=0, tiled=True),
        lax.all_gather(w_up, "fsdp", axis=0, tiled=True),
        lax.all_gather(w_down, "fsdp", axis=0, tiled=True),
        lax.all_gather(w_proj, "fsdp", axis=0, tiled=True),
    )
    full_query, full_key, full_value, full_out, full_up, full_down, full_proj = gathered
    flat = inputs.reshape(tokens, width).astype(jnp.float32)
    normed_one, factor_one = rms_forward(flat, gain_attn)
    normed_one = normed_one.astype(jnp.bfloat16)
    queries = matmul(normed_one, full_query).astype(jnp.bfloat16).reshape(head_shape)
    key_rows = matmul(normed_one, full_key).astype(jnp.bfloat16).reshape(head_shape)
    value_rows = matmul(normed_one, full_value).astype(jnp.bfloat16).reshape(head_shape)
    bucket_ids = jnp.asarray(bucket_table(length, buckets, REACH))
    onehot_cols = (
        jnp.arange(buckets, dtype=jnp.int32)[:, None] == bucket_ids.reshape(1, length * length)
    ).astype(jnp.bfloat16)
    bias = jnp.dot(bias_table.T, onehot_cols.astype(jnp.float32), precision=HIGH).reshape(
        heads, length, length
    )

    def attend_row(pieces):
        query_row, key_row, value_row, seg_row = pieces
        scores = row_scores(query_row, key_row, seg_row, bias)
        row_peak = jnp.max(scores, axis=-1, keepdims=True)
        log_total = row_peak + jnp.log(jnp.sum(jnp.exp(scores - row_peak), axis=-1, keepdims=True))
        soft_low = jnp.exp(scores - log_total).astype(jnp.bfloat16)
        mixed = jnp.einsum("hqk,khd->qhd", soft_low, value_row, preferred_element_type=jnp.float32)
        return (mixed.astype(jnp.bfloat16), log_total)

    attended, log_totals = lax.map(attend_row, (queries, key_rows, value_rows, seg_ids))
    attended_flat = attended.reshape(tokens, width)
    hidden_one = flat + matmul(attended_flat, full_out)
    normed_two, factor_two = rms_forward(hidden_one, gain_ffn)
    normed_two = normed_two.astype(jnp.bfloat16)
    pre_act = matmul(normed_two, full_up)
    activated = jax.nn.gelu(pre_act, approximate=True).astype(jnp.bfloat16)
    hidden_two = hidden_one + matmul(activated, full_down)
    final_rows, factor_three = rms_forward(hidden_two, gain_final)
    member = (seg_ids[:, None, :] == pool_index[:, :, None]).astype(jnp.float32)
    counts = jnp.sum(member, axis=-1, keepdims=True)
    pooled = (
        jnp.einsum("rpl,rld->rpd", member, final_rows.reshape(rows, length, width), precision=HIGH)
        / counts
    )
    proj_full = full_proj.astype(jnp.float32)
    projected = jnp.einsum("rpd,de->rpe", pooled, proj_full, precision=HIGH)
    inverse_len = lax.rsqrt(jnp.sum(projected * projected, axis=-1, keepdims=True) + EPSILON)
    embeddings = projected * inverse_len
    emb_dot = jnp.sum(emb_grad * embeddings, axis=-1, keepdims=True)
    projected_grad = inverse_len * (emb_grad - embeddings * emb_dot)
    grad_proj = jnp.einsum("rpd,rpe->de", pooled, projected_grad, precision=HIGH)
    pooled_grad = jnp.einsum("rpe,de->rpd", projected_grad, proj_full, precision=HIGH) / counts
    final_grad = jnp.einsum("rpl,rpd->rld", member, pooled_grad, precision=HIGH).reshape(
        tokens, width
    )
    stream_two, grad_gain_final = rms_backward(hidden_two, factor_three, gain_final, final_grad)
    back_weights = (
        lax.all_gather(w_query, "fsdp", axis=0, tiled=True),
        lax.all_gather(w_key, "fsdp", axis=0, tiled=True),
        lax.all_gather(w_value, "fsdp", axis=0, tiled=True),
        lax.all_gather(w_out, "fsdp", axis=0, tiled=True),
        lax.all_gather(w_up, "fsdp", axis=0, tiled=True),
        lax.all_gather(w_down, "fsdp", axis=0, tiled=True),
        lax.all_gather(w_proj, "fsdp", axis=0, tiled=True),
    )
    back_query, back_key, back_value, back_out, back_up, back_down, back_proj = back_weights
    ffn_grad = stream_two.astype(jnp.bfloat16)
    grad_down = matmul_left(activated, ffn_grad)
    act_grad = matmul_right(ffn_grad, back_down)
    gelu_pullback = jax.vjp(partial(jax.nn.gelu, approximate=True), pre_act)[1]
    pre_grad = gelu_pullback(act_grad)[0].astype(jnp.bfloat16)
    grad_up = matmul_left(normed_two, pre_grad)
    normed_two_grad = matmul_right(pre_grad, back_up)
    stream_mid, grad_gain_ffn = rms_backward(hidden_one, factor_two, gain_ffn, normed_two_grad)
    stream_one = stream_two + stream_mid
    attn_grad = stream_one.astype(jnp.bfloat16)
    grad_out = matmul_left(attended_flat, attn_grad)
    mixed_grad = matmul_right(attn_grad, back_out).astype(jnp.bfloat16).reshape(head_shape)

    def attend_back(pieces):
        query_row, key_row, value_row, seg_row, log_total, upstream_row = pieces
        scores = row_scores(query_row, key_row, seg_row, bias)
        soft_rows = jnp.exp(scores - log_total)
        soft_grad = jnp.einsum(
            "qhd,khd->hqk", upstream_row, value_row, preferred_element_type=jnp.float32
        )
        score_grad = (
            soft_rows * (soft_grad - jnp.sum(soft_rows * soft_grad, axis=-1, keepdims=True))
        ).astype(jnp.bfloat16)
        query_grad = jnp.einsum(
            "hqk,khd->qhd", score_grad, key_row, preferred_element_type=jnp.float32
        ).astype(jnp.bfloat16)
        key_grad = jnp.einsum(
            "hqk,qhd->khd", score_grad, query_row, preferred_element_type=jnp.float32
        ).astype(jnp.bfloat16)
        value_grad = jnp.einsum(
            "hqk,qhd->khd",
            soft_rows.astype(jnp.bfloat16),
            upstream_row,
            preferred_element_type=jnp.float32,
        ).astype(jnp.bfloat16)
        table_grad = matmul_right(score_grad.reshape(heads, length * length), onehot_cols)
        return (query_grad, key_grad, value_grad, table_grad)

    query_grads, key_grads, value_grads, table_grads = lax.map(
        attend_back, (queries, key_rows, value_rows, seg_ids, log_totals, mixed_grad)
    )
    grad_table = jnp.sum(table_grads, axis=0).T
    query_flat = query_grads.reshape(tokens, width)
    key_flat = key_grads.reshape(tokens, width)
    value_flat = value_grads.reshape(tokens, width)
    grad_query = matmul_left(normed_one, query_flat)
    grad_key = matmul_left(normed_one, key_flat)
    grad_value = matmul_left(normed_one, value_flat)
    normed_one_grad = (
        matmul_right(query_flat, back_query)
        + matmul_right(key_flat, back_key)
        + matmul_right(value_flat, back_value)
    )
    stream_in, grad_gain_attn = rms_backward(flat, factor_one, gain_attn, normed_one_grad)
    input_grad = (stream_one + stream_in).reshape(rows, length, width)
    shard_query, shard_key, shard_value, shard_out, shard_up, shard_down, shard_proj = (
        lax.psum_scatter(grad_query, "fsdp", scatter_dimension=0, tiled=True),
        lax.psum_scatter(grad_key, "fsdp", scatter_dimension=0, tiled=True),
        lax.psum_scatter(grad_value, "fsdp", scatter_dimension=0, tiled=True),
        lax.psum_scatter(grad_out, "fsdp", scatter_dimension=0, tiled=True),
        lax.psum_scatter(grad_up, "fsdp", scatter_dimension=0, tiled=True),
        lax.psum_scatter(grad_down, "fsdp", scatter_dimension=0, tiled=True),
        lax.psum_scatter(grad_proj, "fsdp", scatter_dimension=0, tiled=True),
    )
    summed = (
        lax.psum(shard_query.astype(jnp.bfloat16), "dp").astype(jnp.float32),
        lax.psum(shard_key.astype(jnp.bfloat16), "dp").astype(jnp.float32),
        lax.psum(shard_value.astype(jnp.bfloat16), "dp").astype(jnp.float32),
        lax.psum(shard_out.astype(jnp.bfloat16), "dp").astype(jnp.float32),
        lax.psum(shard_up.astype(jnp.bfloat16), "dp").astype(jnp.float32),
        lax.psum(shard_down.astype(jnp.bfloat16), "dp").astype(jnp.float32),
        lax.psum(shard_proj.astype(jnp.bfloat16), "dp").astype(jnp.float32),
    )
    smalls = lax.psum((grad_gain_attn, grad_gain_ffn, grad_gain_final, grad_table), ("dp", "fsdp"))
    return (
        embeddings,
        input_grad,
        summed[0],
        summed[1],
        summed[2],
        summed[3],
        summed[4],
        summed[5],
        summed[6],
        smalls[0],
        smalls[1],
        smalls[2],
        smalls[3],
    )


def solution(mesh):
    near = (mesh.shape["dp"], mesh.shape["fsdp"]) == (4, 8)
    return jax.shard_map(
        near_device if near else general,
        mesh=mesh,
        in_specs=(
            P(("dp", "fsdp"), None, None),
            P(("dp", "fsdp"), None),
            P(("dp", "fsdp"), None),
            P("fsdp", None),
            P("fsdp", None),
            P("fsdp", None),
            P("fsdp", None),
            P("fsdp", None),
            P("fsdp", None),
            P("fsdp", None),
            P(),
            P(),
            P(),
            P(),
            P(("dp", "fsdp"), None, None),
        ),
        out_specs=(
            P(("dp", "fsdp"), None, None),
            P(("dp", "fsdp"), None, None),
            P("fsdp", None),
            P("fsdp", None),
            P("fsdp", None),
            P("fsdp", None),
            P("fsdp", None),
            P("fsdp", None),
            P("fsdp", None),
            P(),
            P(),
            P(),
            P(),
        ),
        check_vma=False,
    )
```

```python
import math
from functools import partial

import jax
import jax.numpy as jnp
import numpy as np
from jax import lax
from jax.experimental import pallas as pl
from jax.experimental.pallas import tpu as pltpu
from jax.sharding import PartitionSpec as P

REACH = 128


EPSILON = 1e-06
VMEM_BYTES = 64 * 2**20
HIGH = lax.Precision.HIGHEST


def bucket_table(length, buckets, reach):
    positions = np.arange(length)
    relative = positions[None, :] - positions[:, None]
    halfway = buckets // 2
    exact_span = halfway // 2
    distance = np.abs(relative)
    logged = exact_span + (
        np.log(np.maximum(distance, 1) / exact_span)
        / np.log(reach / exact_span)
        * (halfway - exact_span)
    ).astype(np.int64)
    logged = np.minimum(logged, halfway - 1)
    result = (relative > 0).astype(np.int64) * halfway + np.where(
        distance < exact_span, distance, logged
    )
    return result.astype(np.int32)


def rms_forward(values, gain):
    factor = lax.rsqrt(jnp.mean(values * values, axis=-1, keepdims=True) + EPSILON)
    return (values * factor * gain, factor)


def rms_backward(values, factor, gain, upstream):
    normed = values * factor
    gain_grad = jnp.sum(upstream * normed, axis=0)
    inner = upstream * gain
    return (factor * (inner - normed * jnp.mean(inner * normed, axis=-1, keepdims=True)), gain_grad)


def matmul(left, right):
    return jnp.dot(left, right, preferred_element_type=jnp.float32)


def matmul_left(left, right):
    return lax.dot_general(
        left, right, (((0,), (0,)), ((), ())), preferred_element_type=jnp.float32
    )


def matmul_right(left, right):
    return lax.dot_general(
        left, right, (((1,), (1,)), ((), ())), preferred_element_type=jnp.float32
    )


def row_scores(query_row, key_row, seg_row, bias):
    raw_scores = jnp.einsum("qhd,khd->hqk", query_row, key_row, preferred_element_type=jnp.float32)
    same_doc = (seg_row[:, None] == seg_row[None, :])[None]
    return jnp.where(same_doc, raw_scores + bias, -1e30)


MESH = pl.DeviceIdType.MESH
LANES = 128


class Place:
    def __init__(self):
        self.dp, self.fsdp = lax.axis_index("dp"), lax.axis_index("fsdp")
        self.y, self.x = self.dp // 2, self.dp % 2
        self.z, self.c = self.fsdp // 2, self.fsdp % 2

    def core(self):
        return (self.dp, self.z * 2 + (1 - self.c))

    def at_x(self):
        return (self.y * 2 + (1 - self.x), self.fsdp)

    def at_y(self):
        return ((1 - self.y) * 2 + self.x, self.fsdp)

    def at_xy(self):
        return ((1 - self.y) * 2 + (1 - self.x), self.fsdp)

    def up(self, d):
        return lax.rem(self.z + d, 4)

    def down(self, d):
        return lax.rem(self.z + 4 - d, 4)

    def at_z(self, d):
        return (self.dp, self.up(d) * 2 + self.c)

    def greet(self):
        partners = [self.core(), self.at_x(), self.at_y(), self.at_xy()]
        partners += [self.at_z(d) for d in (1, 2, 3)]
        for partner in partners:
            pl.semaphore_signal(
                pltpu.get_barrier_semaphore(), inc=1, device_id=partner, device_id_type=MESH
            )
        self.greeted = len(partners)

    def meet(self):
        pl.semaphore_wait(pltpu.get_barrier_semaphore(), self.greeted)


def remote(src, dst, send, recv, device):
    return pltpu.make_async_remote_copy(
        src_ref=src, dst_ref=dst, send_sem=send, recv_sem=recv, device_id=device, device_id_type=MESH
    )


def half(which, size, start=0):
    return pl.ds(pl.multiple_of(start + which * (size // 2), size // 2 if start % (size // 2) == 0 else 16), size // 2)


class Unit:
    def __init__(self, array, first, rows, left, wide, along_z):
        self.array, self.first, self.rows, self.left, self.wide = array, first, rows, left, wide
        self.along_z = along_z

    def quarter(self, y, x):
        return (half(y, self.rows, self.first), half(x, self.wide, self.left))

    def whole(self):
        return (pl.ds(self.first, self.rows), pl.ds(self.left, self.wide))


class Gather:
    SEMS = 14

    def __init__(self, place, units, shards, wholes, send, recv):
        self.p, self.units, self.shards, self.wholes = place, units, shards, wholes
        self.send, self.recv = send, recv
        z = place.z
        late = jnp.where(z == 0, 1, 3)
        self.turns = (2, 4 - late, late)
        self.inner = jnp.logical_and(z > 0, z < 3)

    def _part(self, u, z, y, x):
        unit = self.units[u]
        where = unit.whole() if unit.along_z else unit.quarter(y, x)
        return self.wholes[unit.array].at[(z, self.p.c) + where]

    def _z(self, u, d):
        p, unit = self.p, self.units[u]
        src = self.shards[unit.array].at[unit.whole() if unit.along_z else unit.quarter(p.y, p.x)]
        return remote(src, self._part(u, p.z, p.y, p.x), self.send.at[u, d - 1], self.recv.at[u, d - 1], p.at_z(d))

    def _sends(self, u):
        return [(self._z(u, 1), self.p.z != 3), (self._z(u, 2), None), (self._z(u, 3), self.p.z != 0)]

    def _hand_on(self, u):
        p = self.p
        ref = self._part(u, p.down(2), p.y, p.x)
        end = 3 * (p.z - 1)
        return remote(ref, ref, self.send.at[u, 13], self.recv.at[u, 2 * (p.z - 1)], (p.dp, end * 2 + p.c))

    def _hop(self, u, turn, kind, y, x, device):
        d = self.turns[turn]
        ref = self._part(u, self.p.down(d), y, x)
        k = 3 * kind + d - 1
        return remote(ref, ref, self.send.at[u, k], self.recv.at[u, k], device)

    def _to_x(self, u, turn):
        return self._hop(u, turn, 1, self.p.y, self.p.x, self.p.at_x())

    def _to_y(self, u, turn):
        return self._hop(u, turn, 2, self.p.y, self.p.x, self.p.at_y())

    def _through_x(self, u, turn):
        return (u + min(turn, 1)) % 2 == 0

    def _diagonal(self, u, turn):
        p = self.p
        if self._through_x(u, turn):
            return self._hop(u, turn, 3, p.y, 1 - p.x, p.at_y())
        return self._hop(u, turn, 3, 1 - p.y, p.x, p.at_x())

    def _core(self, u):
        unit = self.units[u]
        ref = self.wholes[unit.array].at[(slice(None), self.p.c) + unit.whole()]
        return remote(ref, ref, self.send.at[u, 12], self.recv.at[u, 12], self.p.core())

    def start(self, u):
        for copy, condition in self._sends(u):
            if condition is None:
                copy.start()
            else:
                pl.when(condition)(copy.start)

    def plane(self, u, turn):
        self._z(u, self.turns[turn]).wait_recv()
        if turn == 0:
            pl.when(self.inner)(lambda: self._hand_on(u).start())
        if not self.units[u].along_z:
            self._to_x(u, turn).start()
            self._to_y(u, turn).start()

    def corner(self, u, turn):
        early, later = self._to_x(u, turn), self._to_y(u, turn)
        if not self._through_x(u, turn):
            early, later = later, early
        early.wait_recv()
        self._diagonal(u, turn).start()
        later.wait_recv()

    def pair(self, u):
        if not self.units[u].along_z:
            for turn in range(3):
                self._diagonal(u, turn).wait_recv()
        self._core(u).start()

    def arrive(self, u):
        self._core(u).wait_recv()

    def finish(self, u):
        for copy, condition in self._sends(u):
            if condition is None:
                copy.wait_send()
            else:
                pl.when(condition)(copy.wait_send)
        pl.when(self.inner)(lambda: self._hand_on(u).wait_send())
        if not self.units[u].along_z:
            for turn in range(3):
                self._to_x(u, turn).wait_send()
                self._to_y(u, turn).wait_send()
                self._diagonal(u, turn).wait_send()
        self._core(u).wait_send()


UNITS = [
    (0, 0, 96, 0, 256, False),
    (0, 0, 96, 256, 256, False),
    (0, 0, 96, 512, 256, False),
    (1, 0, 96, 0, 768, False),
    (2, 0, 96, 0, 768, False),
    (3, 0, 96, 0, 768, False),
    (4, 0, 96, 0, 768, False),
    (4, 0, 96, 768, 768, False),
    (4, 0, 96, 1536, 768, False),
    (4, 0, 96, 2304, 768, False),
    (5, 0, 128, 0, 768, False),
    (5, 128, 128, 0, 768, False),
    (5, 256, 128, 0, 768, False),
    (6, 0, 96, 0, 256, False),
    (6, 0, 96, 256, 256, False),
    (6, 0, 96, 512, 256, False),
]
ARRIVALS = {
    "start": [
        (0, 2), (0, 0), (0, 4), (1, 2),
    ],
    "n1": [
        (0, 1), (2, 4), (2, 2), (0, 5), (1, 0), (1, 4), (3, 2), (0, 3), (2, 1), (1, 1), (2, 0), (3,
        0), (3, 4), (2, 5), (5, 2), (0, 9), (3, 1), (5, 4), (1, 5), (5, 1), (4, 0), (2, 3), (3, 5),
        (4, 1), (0, 6), (1, 3), (0, 10), (6, 1), (3, 3), (5, 0), (5, 3), (4, 2), (4, 3), (7, 1), (2,
        6), (6, 0), (6, 4), (0, 8), (0, 7), (6, 3), (4, 4), (4, 5),
    ],
    "band": [
        (6, 2), (6, 5), (0, 14), (1, 6), (7, 3), (2, 10), (7, 0), (0, 12), (1, 10), (7, 2), (2, 8),
        (3, 6), (7, 4), (8, 1), (1, 8), (8, 2), (8, 3), (8, 0), (5, 5),
    ],
    "mask": [
        (2, 9), (1, 9), (0, 13),
    ],
    "q": [
        (3, 10), (8, 4),
    ],
    "k": [
        (3, 8), (1, 7), (4, 6), (3, 9),
    ],
    "a0": [
        (3, 7), (1, 12), (4, 8),
    ],
    "a1": [
        (4, 9), (6, 6), (5, 6), (0, 11), (2, 7), (4, 7), (1, 13), (2, 13), (3, 12), (5, 9),
    ],
    "a2": [
        (5, 10), (5, 8), (3, 13), (0, 15), (6, 9),
    ],
    "a3": [
        (4, 10), (6, 10), (7, 5), (6, 7), (6, 8),
    ],
    "a4": [
        (2, 12), (1, 11), (2, 14), (5, 7), (1, 14), (2, 11),
    ],
    "a5": [
        (7, 6), (3, 11), (7, 8), (6, 13), (4, 12), (7, 10), (8, 5),
    ],
    "h": [
        (5, 12), (3, 14), (6, 12), (1, 15), (7, 9), (5, 14), (4, 14), (2, 15), (8, 6), (7, 7), (4,
        13), (4, 11), (5, 13),
    ],
    "u0": [
        (3, 15), (8, 10), (5, 11), (6, 11), (8, 7), (8, 8), (6, 14),
    ],
    "u1": [
        (7, 12),
    ],
    "u2": [
        (8, 9), (4, 15), (6, 15), (7, 11), (5, 15),
    ],
    "d0": [
        (8, 11), (7, 13), (8, 12),
    ],
    "d1": [
        (7, 14), (7, 15),
    ],
    "d2": [
        (8, 14), (8, 13),
    ],
    "e1": [
        (8, 15),
    ],
}


def dot(a, b, ca=1, cb=0):
    return lax.dot_general(a, b, (((ca,), (cb,)), ((), ())), preferred_element_type=jnp.float32)


def dot_exact(a, b, ca=1, cb=0):
    return lax.dot_general(
        a, b, (((ca,), (cb,)), ((), ())), precision=HIGH, preferred_element_type=jnp.float32
    )


def low(v):
    return v.astype(jnp.bfloat16)


def wide(v):
    return v.astype(jnp.float32)


def two_parts(v):
    high = wide(low(v))
    return low(jnp.concatenate([high, v - high], axis=0))


def norm_factor(v):
    return lax.rsqrt(jnp.mean(v * v, axis=-1, keepdims=True) + EPSILON)


def norm_back(v, factor, gain, upstream):
    normed = v * factor
    inner = upstream * gain
    grad = factor * (inner - normed * jnp.mean(inner * normed, axis=-1, keepdims=True))
    return grad, jnp.sum(upstream * normed, axis=0, keepdims=True)


def gelu_both(v):
    scale = math.sqrt(2.0 / math.pi)
    square = v * v
    bent = jnp.tanh(scale * v * (1.0 + 0.044715 * square))
    share = 0.5 + 0.5 * bent
    slope = share + (0.5 * scale) * v * (1.0 - bent * bent) * (1.0 + (3 * 0.044715) * square)
    return v * share, slope


def flat(ref, *where):
    value = ref[where] if where else ref[...]
    return value.reshape(-1, value.shape[-1])


TILE, SPAN = 128, 384


def rows_of(t):
    return pl.ds(t * TILE, TILE)


def span_of(t):
    return pl.ds(t * TILE, SPAN)


def heads_of(p):
    return pl.ds(pl.multiple_of(p * LANES, LANES), LANES)


def stacked(v, axis=0):
    first = lax.broadcasted_iota(jnp.int32, v.shape, 1) < LANES // 2
    zero = jnp.zeros_like(v)
    return jnp.concatenate([jnp.where(first, v, zero), jnp.where(first, zero, v)], axis=axis)


def side_by_side(v):
    return jnp.concatenate([v[:TILE], v[TILE:]], axis=1)


def probs_at(p, t):
    return (pl.ds(pl.multiple_of((p // 2) * 256, 256), 256), pl.ds(pl.multiple_of((p % 2) * 1536, 1536) + t * SPAN, SPAN))


def attend(p, t, q, keys, values, band, mask, probs, mixed):
    scores = dot(stacked(q[rows_of(t), heads_of(p)]), keys[span_of(t), heads_of(p)], 1, 1)
    hidden = jnp.concatenate([mask[3 * t + i] for i in range(3)], axis=1)
    scores = scores + band[p] + jnp.concatenate([hidden, hidden], axis=0)
    powered = jnp.exp(scores - jnp.max(scores, axis=1, keepdims=True))
    soft = low(powered * (1.0 / jnp.sum(powered, axis=1, keepdims=True)))
    probs[probs_at(p, t)] = soft
    out = dot(side_by_side(soft), stacked(values[span_of(t), heads_of(p)]))
    mixed[rows_of(t), heads_of(p)] = low(out)


def bucket_rows(away, buckets):
    halfway = buckets // 2
    exact = halfway // 2
    distance = np.abs(away)
    logged = exact + (
        np.log(np.maximum(distance, 1) / exact) / np.log(REACH / exact) * (halfway - exact)
    ).astype(np.int64)
    bucket = (away > 0) * halfway + np.where(distance < exact, distance, np.minimum(logged, halfway - 1))
    return (np.arange(buckets)[:, None] == bucket[None, :]).astype(np.float32)


def ray_buckets(buckets):
    near = np.arange(512)
    return bucket_rows(np.where(near < SPAN, near - TILE, near - 512 - TILE), buckets)


class Reduce:
    SEMS = 11

    @staticmethod
    def shapes(rows):
        return [(2, rows, 384), (2, rows // 2, 768), (2, rows // 2, 384), (2, rows // 2, 384), (3, rows // 2, 384)]

    def __init__(self, place, through_x, grad, own, core, total, buffers, send, recv, credit, waits, gives):
        self.p, self.g, self.own, self.rc, self.f = place, grad, own, core, total
        self.through_x, self.send, self.recv = through_x, send, recv
        self.credit, self.waits, self.gives = credit, waits, gives
        self._take(buffers)
        p = place
        self.row = [half(i, own.shape[1]) for i in (p.y, 1 - p.y)]
        self.col = [half(i, 768) for i in (p.x, 1 - p.x)]

    def _take(self, buffers):
        self.rx, self.ry, self.sx, self.sy, self.rz = buffers

    def _copy(self, k, src, dst, device):
        return remote(src, dst, self.send.at[k], self.recv.at[k], device)

    def _core(self):
        return self._copy(0, self.g.at[:, 1 - self.p.c], self.rc, self.p.core())

    def _first(self):
        p, low, high = self.p, pl.ds(0, 2), pl.ds(2, 2)
        return [
            self._copy(1, self.own.at[low, :, self.col[1]], self.rx, p.at_x()),
            self._copy(2, self.own.at[high, self.row[1], :], self.ry, p.at_y()),
        ]

    def _second(self):
        p, low, high = self.p, pl.ds(0, 2), pl.ds(2, 2)
        return [
            self._copy(3, self.own.at[low, self.row[1], self.col[0]], self.sy, p.at_y()),
            self._copy(4, self.own.at[high, self.row[0], self.col[1]], self.sx, p.at_x()),
        ]

    def _third(self):
        p = self.p
        return [
            self._copy(4 + d, self.own.at[p.up(d), self.row[0], self.col[0]], self.rz.at[d - 1], p.at_z(d))
            for d in (1, 2, 3)
        ]

    def _spread(self):
        p, part = self.p, self.f.at[self.row[0], self.col[0]]
        return [self._copy(8 + i, part, part, device) for i, device in enumerate((p.at_x(), p.at_y()))]

    def _corner(self):
        p = self.p
        if self.through_x:
            part, device = self.f.at[self.row[0], self.col[1]], p.at_y()
        else:
            part, device = self.f.at[self.row[1], self.col[0]], p.at_x()
        return self._copy(10, part, part, device)

    def _add(self, where, other):
        self.own[where] = low(wide(self.own[where]) + wide(other[...]))

    def start(self):
        if self.waits:
            pl.semaphore_wait(self.credit, self.waits)
        self._core().start()

    def first(self):
        self._core().wait()
        for i in range(4):
            self.own[i] = low(wide(self.g[i, self.p.c]) + wide(self.rc[i]))
        if self.gives:
            pl.semaphore_signal(self.credit, inc=1, device_id=self.p.core(), device_id_type=MESH)
        for copy in self._first():
            copy.start()

    def second(self):
        along_x, along_y = self._first()
        to_y, to_x = self._second()
        along_x.wait_recv()
        for i in range(2):
            self._add((i, slice(None), self.col[0]), self.rx.at[i])
        to_y.start()
        along_y.wait_recv()
        for i in range(2):
            self._add((2 + i, self.row[0], slice(None)), self.ry.at[i])
        to_x.start()
        self._sent((along_x, along_y))

    def third(self):
        for copy in self._second():
            copy.wait_recv()
        for i in range(2):
            self._add((i, self.row[0], self.col[0]), self.sy.at[i])
            self._add((2 + i, self.row[0], self.col[0]), self.sx.at[i])
        for copy in self._third():
            copy.start()
        self._sent(self._second())

    def _total(self):
        total = wide(self.own[self.p.z, self.row[0], self.col[0]])
        for d, copy in enumerate(self._third()):
            copy.wait_recv()
            total = total + wide(self.rz[d])
        return total

    def spread(self):
        self.f[self.row[0], self.col[0]] = low(self._total())
        for copy in self._spread():
            copy.start()
        self._sent(self._third())

    def corner(self):
        along_x, along_y = self._spread()
        early, later = (along_x, along_y) if self.through_x else (along_y, along_x)
        early.wait_recv()
        self._corner().start()
        later.wait_recv()
        self._sent(self._spread())

    def arrive(self):
        self._corner().wait()

    @staticmethod
    def _sent(copies):
        for copy in copies:
            copy.wait_send()


class LineFirst(Reduce):
    @staticmethod
    def shapes(rows):
        return [(3, rows, 768), (rows, 384), (rows // 2, 768), (rows // 2, 384)]

    def _take(self, buffers):
        self.rz, self.rx, self.ry, self.rq = buffers

    def _mine(self):
        return self.own.at[self.p.z]

    def _first(self):
        p = self.p
        return [self._copy(d, self.own.at[p.up(d)], self.rz.at[d - 1], p.at_z(d)) for d in (1, 2, 3)]

    def _second(self):
        if self.through_x:
            return [self._copy(4, self._mine().at[:, self.col[1]], self.rx, self.p.at_x())]
        return [self._copy(4, self._mine().at[self.row[1], :], self.ry, self.p.at_y())]

    def _third(self):
        if self.through_x:
            return [self._copy(5, self._mine().at[self.row[1], self.col[0]], self.rq, self.p.at_y())]
        return [self._copy(5, self._mine().at[self.row[0], self.col[1]], self.rq, self.p.at_x())]

    def second(self):
        total = wide(self._mine()[...])
        for d, copy in enumerate(self._first()):
            copy.wait_recv()
            total = total + wide(self.rz[d])
        self._mine()[...] = low(total)
        self._second()[0].start()
        self._sent(self._first())

    def third(self):
        self._second()[0].wait_recv()
        if self.through_x:
            self._add((self.p.z, slice(None), self.col[0]), self.rx)
        else:
            self._add((self.p.z, self.row[0], slice(None)), self.ry)
        self._third()[0].start()
        self._sent(self._second())

    def _total(self):
        self._third()[0].wait_recv()
        return wide(self.own[self.p.z, self.row[0], self.col[0]]) + wide(self.rq[...])


class Small:
    SEMS = 6

    def __init__(self, place, sums, got, line, send, recv):
        self.p, self.sums, self.got, self.line, self.send, self.recv = place, sums, got, line, send, recv

    def _pair(self, i):
        device = (self.p.core, self.p.at_x, self.p.at_y)[i]()
        return remote(self.sums.at[i], self.got.at[i], self.send.at[i], self.recv.at[i], device)

    def _line(self):
        p = self.p
        return [
            remote(self.sums.at[3], self.line.at[p.z], self.send.at[2 + d], self.recv.at[2 + d], p.at_z(d))
            for d in (1, 2, 3)
        ]

    def start(self):
        self._pair(0).start()

    def turn(self, i):
        self._pair(i).wait_recv()
        self.sums[i + 1] = self.sums[i] + self.got[i]
        if i < 2:
            self._pair(i + 1).start()
        else:
            self.line[self.p.z] = self.sums[3]
            for copy in self._line():
                copy.start()

    def finish(self):
        for copy in self._line():
            copy.wait()
        for i in range(3):
            self._pair(i).wait_send()
        return self.line[0] + self.line[1] + self.line[2] + self.line[3]


RING = 3
KEPT = 8
LEFT = 4
PLACES = [0, 1, 2, 3, 0, 1, 2, 4, 5, 3, 0, 1]
SAID = [0, 0, 0, 0, 1, 1, 1, 0, 0, 1, 1, 1]
BLOCKS = [
    (6, 0, 96, True),
    (5, 0, 128, False),
    (5, 1, 128, False),
    (5, 2, 128, False),
    (4, 0, 96, False),
    (4, 1, 96, True),
    (4, 2, 96, False),
    (4, 3, 96, False),
    (3, 0, 96, False),
    (2, 0, 96, False),
    (1, 0, 96, False),
    (0, 0, 96, False),
]
PLAN = {
    "g0": [
        (0, 0),
    ],
    "g1": [
        (0, 1), (1, 0),
    ],
    "g2": [
        (0, 2), (1, 1),
    ],
    "g3": [
        (0, 3),
    ],
    "g4": [
        (0, 4), (1, 2),
    ],
    "g5": [
        (0, 5), (1, 3), (1, 4),
    ],
    "n1": [
        (1, 5),
    ],
    "n3": [
        (2, 1), (0, 6), (2, 3),
    ],
    "og": [
        (0, 7), (1, 6), (0, 8),
    ],
    "a0": [
        (1, 7),
    ],
    "a1": [
        (3, 1), (2, 2),
    ],
    "a2": [
        (1, 8),
    ],
    "a4": [
        (2, 5), (4, 1), (3, 3), (2, 0), (2, 4),
    ],
    "a5": [
        (3, 2), (2, 7),
    ],
    "g9": [
        (0, 9), (2, 8),
    ],
    "g10": [
        (0, 10), (3, 4), (3, 0), (1, 9), (1, 10), (3, 8),
    ],
    "g11": [
        (4, 3), (3, 5),
    ],
    "tail": [
        (3, 7), (2, 9), (2, 10), (0, 11), (1, 11), (3, 9), (4, 8), (4, 2), (3, 10), (2, 11), (2, 6),
        (4, 4), (4, 7),
    ],
    "table": [
        (3, 11), (4, 9), (3, 6), (4, 10), (5, 3), (5, 7), (5, 4), (5, 9), (5, 1), (4, 5), (5, 8),
        (4, 0), (5, 2), (5, 10), (4, 11), (6, 8), (4, 6), (6, 10), (6, 7), (5, 0), (5, 5), (6, 1),
        (6, 4), (5, 11), (5, 6), (6, 9), (6, 5), (6, 2), (6, 11), (6, 3), (6, 0), (6, 6),
    ],
}


def attend_back(p, t, q, keys, values, probs, held, sums, table):
    heads, after = heads_of(p), pl.ds(pl.multiple_of(p * LANES + 768, LANES), LANES)
    ups = stacked(held[rows_of(t), heads])
    qs = stacked(q[rows_of(t), heads])
    soft = probs[probs_at(p, t)]
    weighted = wide(soft) * dot(ups, values[span_of(t), heads], 1, 1)
    grad = weighted - wide(soft) * jnp.sum(weighted, axis=1, keepdims=True)
    grad_low = low(grad)
    out = dot(side_by_side(grad_low), stacked(keys[span_of(t), heads]))
    held[rows_of(t), after] = low(out)
    for first, more in ((0, dot(grad_low, qs, 0, 0)), (6, dot(soft, ups, 0, 0))):
        where = pl.ds(first + t, 3)
        sums[where] = sums[where] + more.reshape(3, TILE, LANES)
    table[p] += grad


def layer_kernel(units, *refs):
    x_ref, seg_ref, pool_ref, emb_ref, g1_ref, g2_ref, g3_ref, table_ref, near_ref, far_ref = refs[:10]
    shards, outs, input_out, emb_out, small_out = refs[10:17], refs[17:24], refs[24], refs[25], refs[26]
    wholes, refs = refs[27:34], refs[34:]
    act, slope, n1, n2, mixed, q, upstream, keys, values, probs, h1, h2, band, mask, rays, ring, core_low, core_tall = refs[:18]
    refs = refs[18:]
    buffers = []
    for u, (_, _, rows, line_first) in enumerate(BLOCKS):
        count = 1 + (u < KEPT) + len((LineFirst if line_first else Reduce).shapes(rows))
        buffers.append(list(refs[:count]))
        refs = refs[count:]
    small_sums, small_got, small_line = refs[:3]
    send, recv, back_send, back_recv, credit, local, writes, small_send, small_recv = refs[3:]
    wq, wk, wv, wo, wup, wdn, wpj = wholes
    place = Place()
    gather = Gather(place, units, shards, wholes, send, recv)
    own = [
        pltpu.make_async_copy(shard, whole.at[place.z, place.c], local.at[i])
        for i, (shard, whole) in enumerate(zip(shards, wholes))
    ]
    works, results = [], []
    for u, (array, j, rows, line_first) in enumerate(BLOCKS):
        rest = buffers[u]
        total, at = rest.pop(0), PLACES[u]
        core = (core_low, *(core_tall.at[i, :, pl.ds(0, rows), :] for i in range(3)), wpj.at[:, 0], wpj.at[:, 1])[at]
        kept = rest.pop(0) if u < KEPT else wup.at[:, 0, :, pl.ds(768 * (u - KEPT), 768)]
        grad = ring.at[u % RING, :, :, pl.ds(0, rows), :]
        kind = LineFirst if line_first else Reduce
        turns = (credit, SAID[u], u < sum(SAID))
        works.append(kind(place, u % 2 == 0, grad, kept, core, total, rest, back_send.at[u], back_recv.at[u], *turns))
        dst = outs[5].at[pl.ds(128 * j, 128), :] if array == 5 else outs[array].at[:, pl.ds(768 * j, 768)]
        results.append(pltpu.make_async_copy(total, dst, writes.at[u]))
    for copy in own:
        copy.start()
    place.greet()
    n = len(units)

    def receive(name):
        for stage, u in ARRIVALS.get(name, ()):
            if stage == 0:
                gather.start(u)
            elif stage < 4:
                gather.plane(u, stage - 1)
            elif stage < 7:
                gather.corner(u, stage - 4)
            elif stage == 7:
                gather.pair(u)
            else:
                gather.arrive(u)
                if u < n - LEFT:
                    gather.finish(u)

    x = wide(x_ref[...])
    n1[...] = low(x * norm_factor(x) * g1_ref[...].reshape(1, 768))
    for copy in own:
        copy.wait()
    place.meet()
    receive("start")
    receive("n1")
    ray = dot_exact(table_ref[...], near_ref[...])
    for h in range(ray.shape[0]):
        rolled = pltpu.roll(jnp.broadcast_to(ray[h : h + 1], (TILE, 512)), 0, 1, stride=1, stride_axis=0)
        band[h // 2, pl.ds((h % 2) * TILE, TILE), :] = rolled[:, :SPAN]
    receive("band")
    seg = seg_ref[...]
    seg_f = wide(seg)
    column = jnp.transpose(jnp.broadcast_to(seg_f, (TILE, 512)))
    edge = jnp.full((1, TILE), -1.0, jnp.float32)
    line = jnp.concatenate([edge, seg_f, edge], axis=1)
    for t in range(4):
        own_seg = column[t * TILE : (t + 1) * TILE]
        same = jnp.concatenate([own_seg] * 3, axis=1) == line[:, t * TILE : t * TILE + SPAN]
        hidden = jnp.where(same, 0.0, -1e30)
        for i in range(3):
            mask[3 * t + i] = hidden[:, i * TILE : (i + 1) * TILE]
    blank = jnp.zeros((TILE, 768), jnp.bfloat16)
    for ref in (keys, values):
        ref[pl.ds(0, TILE), :] = blank
        ref[pl.ds(640, TILE), :] = blank
    receive("mask")
    q[...] = low(dot(n1[...], flat(wq)))
    receive("q")
    keys[pl.ds(TILE, 512), :] = low(dot(n1[...], flat(wk)))
    receive("k")
    values[pl.ds(TILE, 512), :] = low(dot(n1[...], flat(wv)))
    receive("v")

    def pairs(first, last):
        @pl.loop(first, last)
        def _(p):
            for t in range(4):
                attend(p, t, q, keys, values, band, mask, probs, mixed)

    first = 0
    for p in range(6):
        if p == 5 or ARRIVALS.get(f"a{p}"):
            pairs(first, p + 1)
            first = p + 1
        receive(f"a{p}")
    hidden = wide(x_ref[...]) + dot(mixed[...], flat(wo))
    h1[...] = hidden
    n2[...] = low(hidden * norm_factor(hidden) * g2_ref[...].reshape(1, 768))
    receive("h")
    for j in range(4):
        cols = pl.ds(768 * j, 768)
        value, grad = gelu_both(dot(n2[...], flat(wup, slice(None), slice(None), slice(None), cols)))
        act[:, cols] = low(value)
        slope[:, cols] = low(grad)
        receive(f"u{j}")
    for j in range(3):
        part = jnp.concatenate([act[:, pl.ds(384 * s + 128 * j, 128)] for s in range(8)], axis=1)
        more = dot(part, flat(wdn, slice(None), slice(None), pl.ds(128 * j, 128)))
        h2[...] = (h1[...] if j == 0 else h2[...]) + more
        receive(f"d{j}")
    h = h2[...]
    factor = norm_factor(h)
    g3 = g3_ref[...].reshape(1, 768)
    fin = h * factor * g3
    eye = lax.broadcasted_iota(jnp.int32, (8, 8), 0) == lax.broadcasted_iota(jnp.int32, (8, 8), 1)
    pool = jnp.sum(jnp.where(eye, wide(pool_ref[...]), 0.0), axis=1, keepdims=True)
    member = jnp.where(seg_f == pool, 1.0, 0.0)
    count = jnp.sum(member, axis=1, keepdims=True)
    fin_high = low(fin)
    pooled = (dot(low(member), fin_high) + dot(low(member), low(fin - wide(fin_high)))) / count
    receive("e1")
    wp = flat(wpj)
    both = dot(two_parts(pooled), wp)
    projected = both[:8] + both[8:]
    inverse = lax.rsqrt(jnp.sum(projected * projected, axis=-1, keepdims=True) + EPSILON)
    emb = projected * inverse
    up = emb_ref[...].reshape(8, 768)
    eg = inverse * (up - emb * jnp.sum(up * emb, axis=-1, keepdims=True))
    emb_out[...] = emb
    def take(stage, u):
        work = works[u]
        if stage == 6:
            work.arrive()
            results[u].start()
        else:
            (work.start, work.first, work.second, work.third, work.spread, work.corner)[stage]()

    def serve(name):
        for stage, u in PLAN.get(name, ()):
            take(stage, u)

    def produce(u, value):
        works[u].g[...] = low(value).reshape(works[u].g.shape)
        serve(f"g{u}")

    pooled_high, eg_high = wide(low(pooled)), wide(low(eg))
    left = jnp.concatenate([pooled_high, pooled_high, pooled - pooled_high], axis=0)
    right = jnp.concatenate([eg_high, eg - eg_high, eg_high], axis=0)
    produce(0, dot(low(left), low(right), 0, 0))
    both = dot(two_parts(eg), flat(wpj), 1, 1)
    pooled_grad = (both[:8] + both[8:]) / count
    twice = low(jnp.concatenate([member, member], axis=0))
    fin_grad = dot(twice, two_parts(pooled_grad), 0, 0)
    stream, gain_three = norm_back(h, factor, g3, fin_grad)
    h2[...] = stream
    upstream[...] = low(stream)
    for j in range(3):
        picked = jnp.concatenate([act[:, pl.ds(384 * s + 128 * j, 128)] for s in range(8)], axis=1)
        produce(1 + j, dot(picked, upstream[...], 0, 0))
    for u in range(n - LEFT, n):
        gather.finish(u)
    for j in range(4):
        cols = pl.ds(768 * j, 768)
        grad = low(wide(slope[:, cols]) * dot(upstream[...], flat(wdn, j), 1, 1))
        slope[:, cols] = grad
        produce(4 + j, dot(n2[...], grad, 0, 0))
        more = dot(grad, flat(wup, slice(None), slice(None), slice(None), cols), 1, 1)
        for i in range(2):
            where, half_more = pl.ds(2 * i, 2), more[:, 384 * i : 384 * (i + 1)].reshape(2, 256, 384)
            band[where] = half_more if j == 0 else band[where] + half_more
        serve(f"n{j}")
    n2_grad = jnp.concatenate([band[pl.ds(2 * i, 2)].reshape(512, 384) for i in range(2)], axis=1)
    h = h1[...]
    more, gain_two = norm_back(h, norm_factor(h), g2_ref[...].reshape(1, 768), n2_grad)
    through = h2[...] + more
    h2[...] = through
    upstream[...] = low(through)
    produce(8, dot(mixed[...], upstream[...], 0, 0))
    act[:, pl.ds(0, 768)] = low(dot(upstream[...], flat(wo), 1, 1))
    band[...] = jnp.zeros_like(band)
    serve("og")

    def pairs_back(first, last):
        @pl.loop(first, last)
        def _(p):
            mask[...] = jnp.zeros_like(mask)
            for t in range(4):
                attend_back(p, t, q, keys, values, probs, act, mask, band)
            heads, after = heads_of(p), pl.ds(pl.multiple_of(p * LANES + 768, LANES), LANES)
            slope[:, heads] = low(mask[pl.ds(1, 4)]).reshape(512, LANES)
            slope[:, after] = low(mask[pl.ds(7, 4)]).reshape(512, LANES)

    first = 0
    for p in range(6):
        if p == 5 or PLAN.get(f"a{p}"):
            pairs_back(first, p + 1)
            first = p + 1
        serve(f"a{p}")
    kg, vg, qg = slope[:, pl.ds(0, 768)], slope[:, pl.ds(768, 768)], act[:, pl.ds(768, 768)]
    produce(9, dot(n1[...], vg, 0, 0))
    produce(10, dot(n1[...], kg, 0, 0))
    produce(11, dot(n1[...], qg, 0, 0))
    n1_grad = dot(qg, flat(wq), 1, 1) + dot(kg, flat(wk), 1, 1) + dot(vg, flat(wv), 1, 1)
    x = wide(x_ref[...])
    more, gain_one = norm_back(x, norm_factor(x), g1_ref[...].reshape(1, 768), n1_grad)
    h2[...] = h2[...] + more
    last = pltpu.make_async_copy(h2, input_out, writes.at[len(BLOCKS)])
    last.start()
    serve("tail")
    turn = lax.broadcasted_iota(jnp.int32, (TILE, TILE), 0) + lax.broadcasted_iota(jnp.int32, (TILE, TILE), 1)
    mirror = low(jnp.where(turn == TILE - 1, 1.0, 0.0))
    rays[...] = jnp.zeros_like(rays)
    for h in range(12):
        tile = band[h // 2, pl.ds((h % 2) * TILE, TILE), :]
        high = low(tile)
        upside = dot(mirror, high) + dot(mirror, low(tile - wide(high)))
        spread = jnp.concatenate([upside, jnp.zeros((TILE, 512 - SPAN), jnp.float32)], axis=1)
        rolled = pltpu.roll(spread, 0, 1, stride=1, stride_axis=0)
        rays[pl.ds(h, 1), :] = jnp.sum(rolled, axis=0, keepdims=True)
    by_bucket = dot_exact(rays[...], far_ref[...], 1, 1)
    small_sums[0, :, pl.ds(0, 768)] = jnp.concatenate(
        [gain_one, gain_two, gain_three, jnp.zeros((5, 768), jnp.float32)], axis=0
    )
    small_sums[0, :, pl.ds(768, 256)] = jnp.zeros((8, 256), jnp.float32)
    small_sums[0, :, pl.ds(768, 32)] = by_bucket[:8]
    small_sums[0, :, pl.ds(896, 32)] = by_bucket[8:]
    small = Small(place, small_sums, small_got, small_line, small_send, small_recv)
    small.start()
    rest = PLAN["table"]
    for i in range(len(rest)):
        if i in (4, 9, 14):
            small.turn(i // 5)
        take(*rest[i])
    small_out[...] = small.finish()
    for copy in results:
        copy.wait()
    last.wait()


def far_buckets(buckets):
    return bucket_rows(np.arange(512) - 255, buckets)


def layer_all(x, seg_ids, pool_index, emb_grad, gains, table, shards):
    f32, b16 = jnp.float32, jnp.bfloat16
    units = [Unit(*unit) for unit in UNITS]
    held = [(512, 3072)] * 2 + [(512, 768)] * 5 + [(768, 768)] * 2 + [(768, 3072)]
    scratch = [pltpu.VMEM((4, 2) + shard.shape, b16) for shard in shards]
    scratch += [pltpu.VMEM(shape, b16) for shape in held]
    scratch += [pltpu.VMEM((512, 768), f32)] * 2
    scratch += [pltpu.VMEM((6, 2 * TILE, SPAN), f32), pltpu.VMEM((12, TILE, LANES), f32), pltpu.VMEM((16, 512), f32)]
    scratch += [pltpu.VMEM((RING, 4, 2, 128, 768), b16), pltpu.VMEM((4, 96, 768), b16)]
    scratch += [pltpu.VMEM((3, 4, 128, 768), b16)]
    for u, (_, _, rows, line_first) in enumerate(BLOCKS):
        shapes = [(rows, 768)] + [(4, rows, 768)] * (u < KEPT)
        shapes += (LineFirst if line_first else Reduce).shapes(rows)
        scratch += [pltpu.VMEM(shape, b16) for shape in shapes]
    scratch += [pltpu.VMEM((k, 8, 1024), f32) for k in (4, 3, 4)]
    dma = pltpu.SemaphoreType.DMA
    scratch += [dma((len(units), Gather.SEMS))] * 2 + [dma((len(BLOCKS), Reduce.SEMS))] * 2
    scratch += [pltpu.SemaphoreType.REGULAR, dma((7,)), dma((len(BLOCKS) + 1,)), dma((Small.SEMS,)), dma((Small.SEMS,))]
    outs = [jax.ShapeDtypeStruct(shard.shape, b16) for shard in shards]
    outs += [jax.ShapeDtypeStruct(s, f32) for s in [(512, 768), (8, 768), (8, 1024)]]
    vmem, large = pl.BlockSpec(memory_space=pltpu.VMEM), pl.BlockSpec(memory_space=pl.ANY)
    buckets = table.shape[1]
    return pl.pallas_call(
        partial(layer_kernel, units),
        out_shape=outs,
        in_specs=[vmem] * 10 + [large] * 7,
        out_specs=[large] * 8 + [vmem] * 2,
        scratch_shapes=scratch,
        compiler_params=pltpu.CompilerParams(
            collective_id=0, has_side_effects=True, vmem_limit_bytes=VMEM_BYTES
        ),
        name="layer",
    )(x, seg_ids, pool_index, emb_grad, *gains, table, ray_buckets(buckets), far_buckets(buckets), *shards)


def finish_kernel(emb_in, input_in, small_in, *refs):
    grads, outs = refs[:7], refs[7:]
    emb_out, input_out, gains, table = outs[0], outs[1], outs[9:12], outs[12]
    emb_out[...] = emb_in[...].reshape(emb_out.shape)
    input_out[...] = input_in[...].reshape(input_out.shape)
    for grad, out in zip(grads, outs[2:9]):
        out[...] = wide(grad[...])
    for i, gain in enumerate(gains):
        gain[...] = small_in[pl.ds(i, 1), pl.ds(0, 768)].reshape(768)
    both = jnp.concatenate([small_in[:, pl.ds(768, 128)], small_in[:, pl.ds(896, 128)]], axis=0)
    table[...] = both[:12, :32]


def finish_all(emb, input_grad, small, grads):
    f32 = jnp.float32
    shapes = [(1, 8, 768), (1, 512, 768)] + [g.shape for g in grads] + [(768,)] * 3 + [(12, 32)]
    vmem = pl.BlockSpec(memory_space=pltpu.VMEM)
    return pl.pallas_call(
        finish_kernel,
        out_shape=[jax.ShapeDtypeStruct(s, f32) for s in shapes],
        in_specs=[vmem] * 10,
        out_specs=[vmem] * 13,
        compiler_params=pltpu.CompilerParams(vmem_limit_bytes=VMEM_BYTES),
        name="finish",
    )(emb, input_grad, small, *grads)


def near_device(
    inputs,
    seg_ids,
    pool_index,
    w_query,
    w_key,
    w_value,
    w_out,
    w_up,
    w_down,
    w_proj,
    gain_attn,
    gain_ffn,
    gain_final,
    bias_table,
    emb_grad,
):
    x = inputs.reshape(-1, inputs.shape[-1])
    shards = (w_query, w_key, w_value, w_out, w_up, w_down, w_proj)
    gains = (gain_attn, gain_ffn, gain_final)
    *grads, input_grad, emb, small = layer_all(x, seg_ids, pool_index, emb_grad, gains, bias_table.T, shards)
    out = finish_all(emb, input_grad, small, grads)
    return (*out[:12], out[12].T)


def general(
    inputs,
    seg_ids,
    pool_index,
    w_query,
    w_key,
    w_value,
    w_out,
    w_up,
    w_down,
    w_proj,
    gain_attn,
    gain_ffn,
    gain_final,
    bias_table,
    emb_grad,
):
    rows, length, width = inputs.shape
    buckets, heads = bias_table.shape
    head_dim = width // heads
    tokens = rows * length
    head_shape = (rows, length, heads, head_dim)
    gathered = (
        lax.all_gather(w_query, "fsdp", axis=0, tiled=True),
        lax.all_gather(w_key, "fsdp", axis=0, tiled=True),
        lax.all_gather(w_value, "fsdp", axis=0, tiled=True),
        lax.all_gather(w_out, "fsdp", axis=0, tiled=True),
        lax.all_gather(w_up, "fsdp", axis=0, tiled=True),
        lax.all_gather(w_down, "fsdp", axis=0, tiled=True),
        lax.all_gather(w_proj, "fsdp", axis=0, tiled=True),
    )
    full_query, full_key, full_value, full_out, full_up, full_down, full_proj = gathered
    flat = inputs.reshape(tokens, width).astype(jnp.float32)
    normed_one, factor_one = rms_forward(flat, gain_attn)
    normed_one = normed_one.astype(jnp.bfloat16)
    queries = matmul(normed_one, full_query).astype(jnp.bfloat16).reshape(head_shape)
    key_rows = matmul(normed_one, full_key).astype(jnp.bfloat16).reshape(head_shape)
    value_rows = matmul(normed_one, full_value).astype(jnp.bfloat16).reshape(head_shape)
    bucket_ids = jnp.asarray(bucket_table(length, buckets, REACH))
    onehot_cols = (
        jnp.arange(buckets, dtype=jnp.int32)[:, None] == bucket_ids.reshape(1, length * length)
    ).astype(jnp.bfloat16)
    bias = jnp.dot(bias_table.T, onehot_cols.astype(jnp.float32), precision=HIGH).reshape(
        heads, length, length
    )

    def attend_row(pieces):
        query_row, key_row, value_row, seg_row = pieces
        scores = row_scores(query_row, key_row, seg_row, bias)
        row_peak = jnp.max(scores, axis=-1, keepdims=True)
        log_total = row_peak + jnp.log(jnp.sum(jnp.exp(scores - row_peak), axis=-1, keepdims=True))
        soft_low = jnp.exp(scores - log_total).astype(jnp.bfloat16)
        mixed = jnp.einsum("hqk,khd->qhd", soft_low, value_row, preferred_element_type=jnp.float32)
        return (mixed.astype(jnp.bfloat16), log_total)

    attended, log_totals = lax.map(attend_row, (queries, key_rows, value_rows, seg_ids))
    attended_flat = attended.reshape(tokens, width)
    hidden_one = flat + matmul(attended_flat, full_out)
    normed_two, factor_two = rms_forward(hidden_one, gain_ffn)
    normed_two = normed_two.astype(jnp.bfloat16)
    pre_act = matmul(normed_two, full_up)
    activated = jax.nn.gelu(pre_act, approximate=True).astype(jnp.bfloat16)
    hidden_two = hidden_one + matmul(activated, full_down)
    final_rows, factor_three = rms_forward(hidden_two, gain_final)
    member = (seg_ids[:, None, :] == pool_index[:, :, None]).astype(jnp.float32)
    counts = jnp.sum(member, axis=-1, keepdims=True)
    pooled = (
        jnp.einsum("rpl,rld->rpd", member, final_rows.reshape(rows, length, width), precision=HIGH)
        / counts
    )
    proj_full = full_proj.astype(jnp.float32)
    projected = jnp.einsum("rpd,de->rpe", pooled, proj_full, precision=HIGH)
    inverse_len = lax.rsqrt(jnp.sum(projected * projected, axis=-1, keepdims=True) + EPSILON)
    embeddings = projected * inverse_len
    emb_dot = jnp.sum(emb_grad * embeddings, axis=-1, keepdims=True)
    projected_grad = inverse_len * (emb_grad - embeddings * emb_dot)
    grad_proj = jnp.einsum("rpd,rpe->de", pooled, projected_grad, precision=HIGH)
    pooled_grad = jnp.einsum("rpe,de->rpd", projected_grad, proj_full, precision=HIGH) / counts
    final_grad = jnp.einsum("rpl,rpd->rld", member, pooled_grad, precision=HIGH).reshape(
        tokens, width
    )
    stream_two, grad_gain_final = rms_backward(hidden_two, factor_three, gain_final, final_grad)
    back_weights = (
        lax.all_gather(w_query, "fsdp", axis=0, tiled=True),
        lax.all_gather(w_key, "fsdp", axis=0, tiled=True),
        lax.all_gather(w_value, "fsdp", axis=0, tiled=True),
        lax.all_gather(w_out, "fsdp", axis=0, tiled=True),
        lax.all_gather(w_up, "fsdp", axis=0, tiled=True),
        lax.all_gather(w_down, "fsdp", axis=0, tiled=True),
        lax.all_gather(w_proj, "fsdp", axis=0, tiled=True),
    )
    back_query, back_key, back_value, back_out, back_up, back_down, back_proj = back_weights
    ffn_grad = stream_two.astype(jnp.bfloat16)
    grad_down = matmul_left(activated, ffn_grad)
    act_grad = matmul_right(ffn_grad, back_down)
    gelu_pullback = jax.vjp(partial(jax.nn.gelu, approximate=True), pre_act)[1]
    pre_grad = gelu_pullback(act_grad)[0].astype(jnp.bfloat16)
    grad_up = matmul_left(normed_two, pre_grad)
    normed_two_grad = matmul_right(pre_grad, back_up)
    stream_mid, grad_gain_ffn = rms_backward(hidden_one, factor_two, gain_ffn, normed_two_grad)
    stream_one = stream_two + stream_mid
    attn_grad = stream_one.astype(jnp.bfloat16)
    grad_out = matmul_left(attended_flat, attn_grad)
    mixed_grad = matmul_right(attn_grad, back_out).astype(jnp.bfloat16).reshape(head_shape)

    def attend_back(pieces):
        query_row, key_row, value_row, seg_row, log_total, upstream_row = pieces
        scores = row_scores(query_row, key_row, seg_row, bias)
        soft_rows = jnp.exp(scores - log_total)
        soft_grad = jnp.einsum(
            "qhd,khd->hqk", upstream_row, value_row, preferred_element_type=jnp.float32
        )
        score_grad = (
            soft_rows * (soft_grad - jnp.sum(soft_rows * soft_grad, axis=-1, keepdims=True))
        ).astype(jnp.bfloat16)
        query_grad = jnp.einsum(
            "hqk,khd->qhd", score_grad, key_row, preferred_element_type=jnp.float32
        ).astype(jnp.bfloat16)
        key_grad = jnp.einsum(
            "hqk,qhd->khd", score_grad, query_row, preferred_element_type=jnp.float32
        ).astype(jnp.bfloat16)
        value_grad = jnp.einsum(
            "hqk,qhd->khd",
            soft_rows.astype(jnp.bfloat16),
            upstream_row,
            preferred_element_type=jnp.float32,
        ).astype(jnp.bfloat16)
        table_grad = matmul_right(score_grad.reshape(heads, length * length), onehot_cols)
        return (query_grad, key_grad, value_grad, table_grad)

    query_grads, key_grads, value_grads, table_grads = lax.map(
        attend_back, (queries, key_rows, value_rows, seg_ids, log_totals, mixed_grad)
    )
    grad_table = jnp.sum(table_grads, axis=0).T
    query_flat = query_grads.reshape(tokens, width)
    key_flat = key_grads.reshape(tokens, width)
    value_flat = value_grads.reshape(tokens, width)
    grad_query = matmul_left(normed_one, query_flat)
    grad_key = matmul_left(normed_one, key_flat)
    grad_value = matmul_left(normed_one, value_flat)
    normed_one_grad = (
        matmul_right(query_flat, back_query)
        + matmul_right(key_flat, back_key)
        + matmul_right(value_flat, back_value)
    )
    stream_in, grad_gain_attn = rms_backward(flat, factor_one, gain_attn, normed_one_grad)
    input_grad = (stream_one + stream_in).reshape(rows, length, width)
    shard_query, shard_key, shard_value, shard_out, shard_up, shard_down, shard_proj = (
        lax.psum_scatter(grad_query, "fsdp", scatter_dimension=0, tiled=True),
        lax.psum_scatter(grad_key, "fsdp", scatter_dimension=0, tiled=True),
        lax.psum_scatter(grad_value, "fsdp", scatter_dimension=0, tiled=True),
        lax.psum_scatter(grad_out, "fsdp", scatter_dimension=0, tiled=True),
        lax.psum_scatter(grad_up, "fsdp", scatter_dimension=0, tiled=True),
        lax.psum_scatter(grad_down, "fsdp", scatter_dimension=0, tiled=True),
        lax.psum_scatter(grad_proj, "fsdp", scatter_dimension=0, tiled=True),
    )
    summed = (
        lax.psum(shard_query.astype(jnp.bfloat16), "dp").astype(jnp.float32),
        lax.psum(shard_key.astype(jnp.bfloat16), "dp").astype(jnp.float32),
        lax.psum(shard_value.astype(jnp.bfloat16), "dp").astype(jnp.float32),
        lax.psum(shard_out.astype(jnp.bfloat16), "dp").astype(jnp.float32),
        lax.psum(shard_up.astype(jnp.bfloat16), "dp").astype(jnp.float32),
        lax.psum(shard_down.astype(jnp.bfloat16), "dp").astype(jnp.float32),
        lax.psum(shard_proj.astype(jnp.bfloat16), "dp").astype(jnp.float32),
    )
    smalls = lax.psum((grad_gain_attn, grad_gain_ffn, grad_gain_final, grad_table), ("dp", "fsdp"))
    return (
        embeddings,
        input_grad,
        summed[0],
        summed[1],
        summed[2],
        summed[3],
        summed[4],
        summed[5],
        summed[6],
        smalls[0],
        smalls[1],
        smalls[2],
        smalls[3],
    )


def solution(mesh):
    near = (mesh.shape["dp"], mesh.shape["fsdp"]) == (4, 8)
    return jax.shard_map(
        near_device if near else general,
        mesh=mesh,
        in_specs=(
            P(("dp", "fsdp"), None, None),
            P(("dp", "fsdp"), None),
            P(("dp", "fsdp"), None),
            P("fsdp", None),
            P("fsdp", None),
            P("fsdp", None),
            P("fsdp", None),
            P("fsdp", None),
            P("fsdp", None),
            P("fsdp", None),
            P(),
            P(),
            P(),
            P(),
            P(("dp", "fsdp"), None, None),
        ),
        out_specs=(
            P(("dp", "fsdp"), None, None),
            P(("dp", "fsdp"), None, None),
            P("fsdp", None),
            P("fsdp", None),
            P("fsdp", None),
            P("fsdp", None),
            P("fsdp", None),
            P("fsdp", None),
            P("fsdp", None),
            P(),
            P(),
            P(),
            P(),
        ),
        check_vma=False,
    )
```

```python
import math
from functools import partial

import jax
import jax.numpy as jnp
import numpy as np
from jax import lax
from jax.experimental import pallas as pl
from jax.experimental.pallas import tpu as pltpu
from jax.sharding import PartitionSpec as P

REACH = 128


EPSILON = 1e-06
VMEM_BYTES = 64 * 2**20
HIGH = lax.Precision.HIGHEST


def bucket_table(length, buckets, reach):
    positions = np.arange(length)
    relative = positions[None, :] - positions[:, None]
    halfway = buckets // 2
    exact_span = halfway // 2
    distance = np.abs(relative)
    logged = exact_span + (
        np.log(np.maximum(distance, 1) / exact_span)
        / np.log(reach / exact_span)
        * (halfway - exact_span)
    ).astype(np.int64)
    logged = np.minimum(logged, halfway - 1)
    result = (relative > 0).astype(np.int64) * halfway + np.where(
        distance < exact_span, distance, logged
    )
    return result.astype(np.int32)


def rms_forward(values, gain):
    factor = lax.rsqrt(jnp.mean(values * values, axis=-1, keepdims=True) + EPSILON)
    return (values * factor * gain, factor)


def rms_backward(values, factor, gain, upstream):
    normed = values * factor
    gain_grad = jnp.sum(upstream * normed, axis=0)
    inner = upstream * gain
    return (factor * (inner - normed * jnp.mean(inner * normed, axis=-1, keepdims=True)), gain_grad)


def matmul(left, right):
    return jnp.dot(left, right, preferred_element_type=jnp.float32)


def matmul_left(left, right):
    return lax.dot_general(
        left, right, (((0,), (0,)), ((), ())), preferred_element_type=jnp.float32
    )


def matmul_right(left, right):
    return lax.dot_general(
        left, right, (((1,), (1,)), ((), ())), preferred_element_type=jnp.float32
    )


def row_scores(query_row, key_row, seg_row, bias):
    raw_scores = jnp.einsum("qhd,khd->hqk", query_row, key_row, preferred_element_type=jnp.float32)
    same_doc = (seg_row[:, None] == seg_row[None, :])[None]
    return jnp.where(same_doc, raw_scores + bias, -1e30)


MESH = pl.DeviceIdType.MESH
LANES = 128


class Place:
    def __init__(self):
        self.dp, self.fsdp = lax.axis_index("dp"), lax.axis_index("fsdp")
        self.y, self.x = self.dp // 2, self.dp % 2
        self.z, self.c = self.fsdp // 2, self.fsdp % 2

    def core(self):
        return (self.dp, self.z * 2 + (1 - self.c))

    def at_x(self):
        return (self.y * 2 + (1 - self.x), self.fsdp)

    def at_y(self):
        return ((1 - self.y) * 2 + self.x, self.fsdp)

    def at_xy(self):
        return ((1 - self.y) * 2 + (1 - self.x), self.fsdp)

    def up(self, d):
        return lax.rem(self.z + d, 4)

    def down(self, d):
        return lax.rem(self.z + 4 - d, 4)

    def at_z(self, d):
        return (self.dp, self.up(d) * 2 + self.c)

    def greet(self):
        partners = [self.core(), self.at_x(), self.at_y(), self.at_xy()]
        partners += [self.at_z(d) for d in (1, 2, 3)]
        for partner in partners:
            pl.semaphore_signal(
                pltpu.get_barrier_semaphore(), inc=1, device_id=partner, device_id_type=MESH
            )
        self.greeted = len(partners)

    def meet(self):
        pl.semaphore_wait(pltpu.get_barrier_semaphore(), self.greeted)


def remote(src, dst, send, recv, device):
    return pltpu.make_async_remote_copy(
        src_ref=src, dst_ref=dst, send_sem=send, recv_sem=recv, device_id=device, device_id_type=MESH
    )


def half(which, size, start=0):
    return pl.ds(pl.multiple_of(start + which * (size // 2), size // 2 if start % (size // 2) == 0 else 16), size // 2)


class Unit:
    def __init__(self, array, first, rows, left, wide, along_z):
        self.array, self.first, self.rows, self.left, self.wide = array, first, rows, left, wide
        self.along_z = along_z

    def quarter(self, y, x):
        return (half(y, self.rows, self.first), half(x, self.wide, self.left))

    def whole(self):
        return (pl.ds(self.first, self.rows), pl.ds(self.left, self.wide))


class Gather:
    SEMS = 14

    def __init__(self, place, units, shards, wholes, send, recv):
        self.p, self.units, self.shards, self.wholes = place, units, shards, wholes
        self.send, self.recv = send, recv
        z = place.z
        late = jnp.where(z == 0, 1, 3)
        self.turns = (2, 4 - late, late)
        self.inner = jnp.logical_and(z > 0, z < 3)

    def _part(self, u, z, y, x):
        unit = self.units[u]
        where = unit.whole() if unit.along_z else unit.quarter(y, x)
        return self.wholes[unit.array].at[(z, self.p.c) + where]

    def _z(self, u, d):
        p, unit = self.p, self.units[u]
        src = self.shards[unit.array].at[unit.whole() if unit.along_z else unit.quarter(p.y, p.x)]
        return remote(src, self._part(u, p.z, p.y, p.x), self.send.at[u, d - 1], self.recv.at[u, d - 1], p.at_z(d))

    def _sends(self, u):
        return [(self._z(u, 1), self.p.z != 3), (self._z(u, 2), None), (self._z(u, 3), self.p.z != 0)]

    def _hand_on(self, u):
        p = self.p
        ref = self._part(u, p.down(2), p.y, p.x)
        end = 3 * (p.z - 1)
        return remote(ref, ref, self.send.at[u, 13], self.recv.at[u, 2 * (p.z - 1)], (p.dp, end * 2 + p.c))

    def _hop(self, u, turn, kind, y, x, device):
        d = self.turns[turn]
        ref = self._part(u, self.p.down(d), y, x)
        k = 3 * kind + d - 1
        return remote(ref, ref, self.send.at[u, k], self.recv.at[u, k], device)

    def _to_x(self, u, turn):
        return self._hop(u, turn, 1, self.p.y, self.p.x, self.p.at_x())

    def _to_y(self, u, turn):
        return self._hop(u, turn, 2, self.p.y, self.p.x, self.p.at_y())

    def _through_x(self, u, turn):
        return (u + min(turn, 1)) % 2 == 0

    def _diagonal(self, u, turn):
        p = self.p
        if self._through_x(u, turn):
            return self._hop(u, turn, 3, p.y, 1 - p.x, p.at_y())
        return self._hop(u, turn, 3, 1 - p.y, p.x, p.at_x())

    def _core(self, u):
        unit = self.units[u]
        ref = self.wholes[unit.array].at[(slice(None), self.p.c) + unit.whole()]
        return remote(ref, ref, self.send.at[u, 12], self.recv.at[u, 12], self.p.core())

    def start(self, u):
        for copy, condition in self._sends(u):
            if condition is None:
                copy.start()
            else:
                pl.when(condition)(copy.start)

    def plane(self, u, turn):
        self._z(u, self.turns[turn]).wait_recv()
        if turn == 0:
            pl.when(self.inner)(lambda: self._hand_on(u).start())
        if not self.units[u].along_z:
            self._to_x(u, turn).start()
            self._to_y(u, turn).start()

    def corner(self, u, turn):
        early, later = self._to_x(u, turn), self._to_y(u, turn)
        if not self._through_x(u, turn):
            early, later = later, early
        early.wait_recv()
        self._diagonal(u, turn).start()
        later.wait_recv()

    def pair(self, u):
        if not self.units[u].along_z:
            for turn in range(3):
                self._diagonal(u, turn).wait_recv()
        self._core(u).start()

    def arrive(self, u):
        self._core(u).wait_recv()

    def finish(self, u):
        for copy, condition in self._sends(u):
            if condition is None:
                copy.wait_send()
            else:
                pl.when(condition)(copy.wait_send)
        pl.when(self.inner)(lambda: self._hand_on(u).wait_send())
        if not self.units[u].along_z:
            for turn in range(3):
                self._to_x(u, turn).wait_send()
                self._to_y(u, turn).wait_send()
                self._diagonal(u, turn).wait_send()
        self._core(u).wait_send()


UNITS = [
    (0, 0, 96, 0, 256, False),
    (0, 0, 96, 256, 256, False),
    (0, 0, 96, 512, 256, False),
    (1, 0, 96, 0, 768, False),
    (2, 0, 96, 0, 768, False),
    (3, 0, 96, 0, 768, False),
    (4, 0, 96, 0, 768, False),
    (4, 0, 96, 768, 768, False),
    (4, 0, 96, 1536, 768, False),
    (4, 0, 96, 2304, 768, False),
    (5, 0, 128, 0, 768, False),
    (5, 128, 128, 0, 768, False),
    (5, 256, 128, 0, 768, False),
    (6, 0, 96, 0, 256, False),
    (6, 0, 96, 256, 256, False),
    (6, 0, 96, 512, 256, False),
]
ARRIVALS = {
    "start": [
        (0, 2), (0, 0), (0, 4), (1, 2),
    ],
    "n1": [
        (0, 1), (2, 4), (2, 2), (0, 5), (1, 0), (1, 4), (3, 2), (0, 3), (2, 1), (1, 1), (2, 0), (3,
        0), (3, 4), (2, 5), (5, 2), (0, 9), (3, 1), (5, 4), (1, 5), (5, 1), (4, 0), (2, 3), (3, 5),
        (4, 1), (0, 6), (1, 3), (0, 10), (6, 1), (3, 3), (5, 0), (5, 3), (4, 2), (4, 3), (7, 1), (2,
        6), (6, 0), (6, 4), (0, 8), (0, 7), (6, 3), (4, 4), (4, 5),
    ],
    "band": [
        (6, 2), (6, 5), (0, 14), (1, 6), (7, 3), (2, 10), (7, 0), (0, 12), (1, 10), (7, 2), (2, 8),
        (3, 6), (7, 4), (8, 1), (1, 8), (8, 2), (8, 3), (8, 0), (5, 5),
    ],
    "mask": [
        (2, 9), (1, 9), (0, 13),
    ],
    "q": [
        (3, 10), (8, 4),
    ],
    "k": [
        (3, 8), (1, 7), (4, 6), (3, 9),
    ],
    "a0": [
        (3, 7), (1, 12), (4, 8),
    ],
    "a1": [
        (4, 9), (6, 6), (5, 6), (0, 11), (2, 7), (4, 7), (1, 13), (2, 13), (3, 12), (5, 9),
    ],
    "a2": [
        (5, 10), (5, 8), (3, 13), (0, 15), (6, 9),
    ],
    "a3": [
        (4, 10), (6, 10), (7, 5), (6, 7), (6, 8),
    ],
    "a4": [
        (2, 12), (1, 11), (2, 14), (5, 7), (1, 14), (2, 11),
    ],
    "a5": [
        (7, 6), (3, 11), (7, 8), (6, 13), (4, 12), (7, 10), (8, 5),
    ],
    "h": [
        (5, 12), (3, 14), (6, 12), (1, 15), (7, 9), (5, 14), (4, 14), (2, 15), (8, 6), (7, 7), (4,
        13), (4, 11), (5, 13),
    ],
    "u0": [
        (3, 15), (8, 10), (5, 11), (6, 11), (8, 7), (8, 8), (6, 14),
    ],
    "u1": [
        (7, 12),
    ],
    "u2": [
        (8, 9), (4, 15), (6, 15), (7, 11), (5, 15),
    ],
    "d0": [
        (8, 11), (7, 13), (8, 12),
    ],
    "d1": [
        (7, 14), (7, 15),
    ],
    "d2": [
        (8, 14), (8, 13),
    ],
    "e1": [
        (8, 15),
    ],
}


def dot(a, b, ca=1, cb=0):
    return lax.dot_general(a, b, (((ca,), (cb,)), ((), ())), preferred_element_type=jnp.float32)


def dot_exact(a, b, ca=1, cb=0):
    return lax.dot_general(
        a, b, (((ca,), (cb,)), ((), ())), precision=HIGH, preferred_element_type=jnp.float32
    )


def low(v):
    return v.astype(jnp.bfloat16)


def wide(v):
    return v.astype(jnp.float32)


def two_parts(v):
    high = wide(low(v))
    return low(jnp.concatenate([high, v - high], axis=0))


def norm_factor(v):
    return lax.rsqrt(jnp.mean(v * v, axis=-1, keepdims=True) + EPSILON)


def norm_back(v, factor, gain, upstream):
    normed = v * factor
    inner = upstream * gain
    grad = factor * (inner - normed * jnp.mean(inner * normed, axis=-1, keepdims=True))
    return grad, jnp.sum(upstream * normed, axis=0, keepdims=True)


def gelu_both(v):
    scale = math.sqrt(2.0 / math.pi)
    square = v * v
    bent = jnp.tanh(scale * v * (1.0 + 0.044715 * square))
    share = 0.5 + 0.5 * bent
    slope = share + (0.5 * scale) * v * (1.0 - bent * bent) * (1.0 + (3 * 0.044715) * square)
    return v * share, slope


def flat(ref, *where):
    value = ref[where] if where else ref[...]
    return value.reshape(-1, value.shape[-1])


TILE, SPAN = 128, 384


def rows_of(t):
    return pl.ds(t * TILE, TILE)


def span_of(t):
    return pl.ds(t * TILE, SPAN)


def heads_of(p):
    return pl.ds(pl.multiple_of(p * LANES, LANES), LANES)


def stacked(v, axis=0):
    first = lax.broadcasted_iota(jnp.int32, v.shape, 1) < LANES // 2
    zero = jnp.zeros_like(v)
    return jnp.concatenate([jnp.where(first, v, zero), jnp.where(first, zero, v)], axis=axis)


def side_by_side(v):
    return jnp.concatenate([v[:TILE], v[TILE:]], axis=1)


def probs_at(p, t):
    return (pl.ds(pl.multiple_of((p // 2) * 256, 256), 256), pl.ds(pl.multiple_of((p % 2) * 1536, 1536) + t * SPAN, SPAN))


def attend(p, t, q, keys, values, band, mask, probs, mixed):
    scores = dot(stacked(q[rows_of(t), heads_of(p)]), keys[span_of(t), heads_of(p)], 1, 1)
    hidden = jnp.concatenate([mask[3 * t + i] for i in range(3)], axis=1)
    scores = scores + band[p] + jnp.concatenate([hidden, hidden], axis=0)
    powered = jnp.exp(scores - jnp.max(scores, axis=1, keepdims=True))
    soft = low(powered * (1.0 / jnp.sum(powered, axis=1, keepdims=True)))
    probs[probs_at(p, t)] = soft
    out = dot(side_by_side(soft), stacked(values[span_of(t), heads_of(p)]))
    mixed[rows_of(t), heads_of(p)] = low(out)


def bucket_rows(away, buckets):
    halfway = buckets // 2
    exact = halfway // 2
    distance = np.abs(away)
    logged = exact + (
        np.log(np.maximum(distance, 1) / exact) / np.log(REACH / exact) * (halfway - exact)
    ).astype(np.int64)
    bucket = (away > 0) * halfway + np.where(distance < exact, distance, np.minimum(logged, halfway - 1))
    return (np.arange(buckets)[:, None] == bucket[None, :]).astype(np.float32)


def ray_buckets(buckets):
    near = np.arange(512)
    return bucket_rows(np.where(near < SPAN, near - TILE, near - 512 - TILE), buckets)


class Reduce:
    SEMS = 11

    @staticmethod
    def shapes(rows):
        return [(2, rows, 384), (2, rows // 2, 768), (2, rows // 2, 384), (2, rows // 2, 384), (3, rows // 2, 384)]

    def __init__(self, place, through_x, grad, own, core, total, buffers, send, recv, credit, waits, gives):
        self.p, self.g, self.own, self.rc, self.f = place, grad, own, core, total
        self.through_x, self.send, self.recv = through_x, send, recv
        self.credit, self.waits, self.gives = credit, waits, gives
        self._take(buffers)
        p = place
        self.row = [half(i, own.shape[1]) for i in (p.y, 1 - p.y)]
        self.col = [half(i, 768) for i in (p.x, 1 - p.x)]

    def _take(self, buffers):
        self.rx, self.ry, self.sx, self.sy, self.rz = buffers

    def _copy(self, k, src, dst, device):
        return remote(src, dst, self.send.at[k], self.recv.at[k], device)

    def _core(self):
        return self._copy(0, self.g.at[:, 1 - self.p.c], self.rc, self.p.core())

    def _first(self):
        p, low, high = self.p, pl.ds(0, 2), pl.ds(2, 2)
        return [
            self._copy(1, self.own.at[low, :, self.col[1]], self.rx, p.at_x()),
            self._copy(2, self.own.at[high, self.row[1], :], self.ry, p.at_y()),
        ]

    def _second(self):
        p, low, high = self.p, pl.ds(0, 2), pl.ds(2, 2)
        return [
            self._copy(3, self.own.at[low, self.row[1], self.col[0]], self.sy, p.at_y()),
            self._copy(4, self.own.at[high, self.row[0], self.col[1]], self.sx, p.at_x()),
        ]

    def _third(self):
        p = self.p
        return [
            self._copy(4 + d, self.own.at[p.up(d), self.row[0], self.col[0]], self.rz.at[d - 1], p.at_z(d))
            for d in (1, 2, 3)
        ]

    def _spread(self):
        p, part = self.p, self.f.at[self.row[0], self.col[0]]
        return [self._copy(8 + i, part, part, device) for i, device in enumerate((p.at_x(), p.at_y()))]

    def _corner(self):
        p = self.p
        if self.through_x:
            part, device = self.f.at[self.row[0], self.col[1]], p.at_y()
        else:
            part, device = self.f.at[self.row[1], self.col[0]], p.at_x()
        return self._copy(10, part, part, device)

    def _add(self, where, other):
        self.own[where] = low(wide(self.own[where]) + wide(other[...]))

    def start(self):
        if self.waits:
            pl.semaphore_wait(self.credit, self.waits)
        self._core().start()

    def first(self):
        self._core().wait()
        for i in range(4):
            self.own[i] = low(wide(self.g[i, self.p.c]) + wide(self.rc[i]))
        if self.gives:
            pl.semaphore_signal(self.credit, inc=1, device_id=self.p.core(), device_id_type=MESH)
        for copy in self._first():
            copy.start()

    def second(self):
        along_x, along_y = self._first()
        to_y, to_x = self._second()
        along_x.wait_recv()
        for i in range(2):
            self._add((i, slice(None), self.col[0]), self.rx.at[i])
        to_y.start()
        along_y.wait_recv()
        for i in range(2):
            self._add((2 + i, self.row[0], slice(None)), self.ry.at[i])
        to_x.start()
        self._sent((along_x, along_y))

    def third(self):
        for copy in self._second():
            copy.wait_recv()
        for i in range(2):
            self._add((i, self.row[0], self.col[0]), self.sy.at[i])
            self._add((2 + i, self.row[0], self.col[0]), self.sx.at[i])
        for copy in self._third():
            copy.start()
        self._sent(self._second())

    def _total(self):
        total = wide(self.own[self.p.z, self.row[0], self.col[0]])
        for d, copy in enumerate(self._third()):
            copy.wait_recv()
            total = total + wide(self.rz[d])
        return total

    def spread(self):
        self.f[self.row[0], self.col[0]] = low(self._total())
        for copy in self._spread():
            copy.start()
        self._sent(self._third())

    def corner(self):
        along_x, along_y = self._spread()
        early, later = (along_x, along_y) if self.through_x else (along_y, along_x)
        early.wait_recv()
        self._corner().start()
        later.wait_recv()
        self._sent(self._spread())

    def arrive(self):
        self._corner().wait()

    @staticmethod
    def _sent(copies):
        for copy in copies:
            copy.wait_send()


class LineFirst(Reduce):
    @staticmethod
    def shapes(rows):
        return [(3, rows, 768), (rows, 384), (rows // 2, 768), (rows // 2, 384)]

    def _take(self, buffers):
        self.rz, self.rx, self.ry, self.rq = buffers

    def _mine(self):
        return self.own.at[self.p.z]

    def _first(self):
        p = self.p
        return [self._copy(d, self.own.at[p.up(d)], self.rz.at[d - 1], p.at_z(d)) for d in (1, 2, 3)]

    def _second(self):
        if self.through_x:
            return [self._copy(4, self._mine().at[:, self.col[1]], self.rx, self.p.at_x())]
        return [self._copy(4, self._mine().at[self.row[1], :], self.ry, self.p.at_y())]

    def _third(self):
        if self.through_x:
            return [self._copy(5, self._mine().at[self.row[1], self.col[0]], self.rq, self.p.at_y())]
        return [self._copy(5, self._mine().at[self.row[0], self.col[1]], self.rq, self.p.at_x())]

    def second(self):
        total = wide(self._mine()[...])
        for d, copy in enumerate(self._first()):
            copy.wait_recv()
            total = total + wide(self.rz[d])
        self._mine()[...] = low(total)
        self._second()[0].start()
        self._sent(self._first())

    def third(self):
        self._second()[0].wait_recv()
        if self.through_x:
            self._add((self.p.z, slice(None), self.col[0]), self.rx)
        else:
            self._add((self.p.z, self.row[0], slice(None)), self.ry)
        self._third()[0].start()
        self._sent(self._second())

    def _total(self):
        self._third()[0].wait_recv()
        return wide(self.own[self.p.z, self.row[0], self.col[0]]) + wide(self.rq[...])


class Projection:
    SEMS = 7

    def __init__(self, place, rows, send, recv):
        self.p, self.rows, self.send, self.recv = place, rows, send, recv

    def _copy(self, k, ref, device):
        return remote(ref, ref, self.send.at[k], self.recv.at[k], device)

    def _plane(self):
        p = self.p
        own = self.rows.at[p.c, p.z, p.dp]
        return [self._copy(0, own, p.at_x()), self._copy(1, own, p.at_y())]

    def _corner(self):
        p = self.p
        x_chip, y_chip = p.at_x()[0], p.at_y()[0]
        taken, target = jnp.where(p.c == 0, x_chip, y_chip), jnp.where(p.c == 0, y_chip, x_chip)
        return [self._copy(2, self.rows.at[p.c, p.z, taken], (target, p.fsdp))]

    def _line(self):
        p = self.p
        return [self._copy(2 + d, self.rows.at[p.c, p.z], p.at_z(d)) for d in (1, 2, 3)]

    def _core(self):
        return [self._copy(6, self.rows.at[self.p.c], self.p.core())]

    def start(self, pooled, grad):
        self.rows[self.p.c, self.p.z, self.p.dp] = low(jnp.concatenate([pooled, grad], axis=0))

    def take(self, stage):
        order = (self._plane, self._corner, self._line, self._core)
        if stage > 0:
            for copy in order[stage - 1]():
                copy.wait()
        if stage < 4:
            for copy in order[stage]():
                copy.start()

    def product(self):
        rows = wide(self.rows[...]).reshape(32, 2, 8, 768)
        return dot(low(rows[:, 0].reshape(256, 768)), low(rows[:, 1].reshape(256, 768)), 0, 0)


class Small:
    SEMS = 6

    def __init__(self, place, sums, got, line, send, recv):
        self.p, self.sums, self.got, self.line, self.send, self.recv = place, sums, got, line, send, recv

    def _pair(self, i):
        device = (self.p.core, self.p.at_x, self.p.at_y)[i]()
        return remote(self.sums.at[i], self.got.at[i], self.send.at[i], self.recv.at[i], device)

    def _line(self):
        p = self.p
        return [
            remote(self.sums.at[3], self.line.at[p.z], self.send.at[2 + d], self.recv.at[2 + d], p.at_z(d))
            for d in (1, 2, 3)
        ]

    def start(self):
        self._pair(0).start()

    def turn(self, i):
        self._pair(i).wait_recv()
        self.sums[i + 1] = self.sums[i] + self.got[i]
        if i < 2:
            self._pair(i + 1).start()
        else:
            self.line[self.p.z] = self.sums[3]
            for copy in self._line():
                copy.start()

    def finish(self):
        for copy in self._line():
            copy.wait()
        for i in range(3):
            self._pair(i).wait_send()
        return self.line[0] + self.line[1] + self.line[2] + self.line[3]


RING = 3
KEPT = 7
LEFT = 4
PLACES = [1, 2, 3, 0, 1, 2, 4, 5, 3, 0, 1]
SAID = [0, 0, 0, 0, 1, 1, 0, 0, 1, 1, 1]
BLOCKS = [
    (5, 0, 128, False),
    (5, 1, 128, True),
    (5, 2, 128, False),
    (4, 0, 96, False),
    (4, 1, 96, False),
    (4, 2, 96, False),
    (4, 3, 96, False),
    (3, 0, 96, False),
    (2, 0, 96, False),
    (1, 0, 96, False),
    (0, 0, 96, False),
]
PLAN = {
    "g0": [
        (0, 0),
    ],
    "g1": [
        (0, 1),
    ],
    "g2": [
        (1, 0), (10, 0), (0, 2),
    ],
    "n0": [
        (1, 1), (0, 3), (1, 2),
    ],
    "n1": [
        (0, 4), (1, 3),
    ],
    "g5": [
        (2, 0),
    ],
    "n2": [
        (11, 0),
    ],
    "g6": [
        (1, 4),
    ],
    "n3": [
        (0, 5),
    ],
    "g7": [
        (0, 6),
    ],
    "og": [
        (1, 5), (3, 0),
    ],
    "a0": [
        (1, 6), (0, 7),
    ],
    "a1": [
        (2, 4),
    ],
    "a2": [
        (12, 0), (2, 5), (1, 7),
    ],
    "a3": [
        (2, 1), (2, 3),
    ],
    "a4": [
        (2, 2),
    ],
    "g8": [
        (3, 5),
    ],
    "g9": [
        (0, 8), (2, 7), (3, 1), (3, 3),
    ],
    "g10": [
        (0, 9), (1, 8), (3, 2), (0, 10), (1, 9), (3, 4), (1, 10),
    ],
    "tail": [
        (2, 9), (2, 6), (4, 1), (2, 8), (3, 7), (4, 0), (4, 2), (3, 9), (4, 5), (3, 6), (2, 10), (3,
        8), (4, 7), (5, 1), (13, 0), (5, 0), (5, 2),
    ],
    "table": [
        (5, 5), (4, 9), (4, 3), (3, 10), (4, 6), (6, 5), (4, 4), (5, 9), (5, 6), (6, 2), (5, 3), (4,
        8), (5, 4), (4, 10), (6, 0), (6, 9), (5, 7), (5, 8), (6, 6), (6, 3), (5, 10), (6, 7), (6,
        8), (6, 4), (6, 1), (6, 10), (14, 0),
    ],
}


def attend_back(p, t, q, keys, values, probs, held, sums, table):
    heads, after = heads_of(p), pl.ds(pl.multiple_of(p * LANES + 768, LANES), LANES)
    ups = stacked(held[rows_of(t), heads])
    qs = stacked(q[rows_of(t), heads])
    soft = probs[probs_at(p, t)]
    weighted = wide(soft) * dot(ups, values[span_of(t), heads], 1, 1)
    grad = weighted - wide(soft) * jnp.sum(weighted, axis=1, keepdims=True)
    grad_low = low(grad)
    out = dot(side_by_side(grad_low), stacked(keys[span_of(t), heads]))
    held[rows_of(t), after] = low(out)
    for first, more in ((0, dot(grad_low, qs, 0, 0)), (6, dot(soft, ups, 0, 0))):
        where = pl.ds(first + t, 3)
        sums[where] = sums[where] + more.reshape(3, TILE, LANES)
    table[p] += grad


def layer_kernel(units, *refs):
    x_ref, seg_ref, pool_ref, emb_ref, g1_ref, g2_ref, g3_ref, table_ref, near_ref, far_ref = refs[:10]
    shards, outs, input_out, emb_out, small_out = refs[10:17], refs[17:24], refs[24], refs[25], refs[26]
    wholes, refs = refs[27:34], refs[34:]
    act, slope, n1, n2, mixed, q, upstream, keys, values, probs, h1, h2, band, mask, rays, ring, core_low, core_tall = refs[:18]
    refs = refs[18:]
    buffers = []
    for u, (_, _, rows, line_first) in enumerate(BLOCKS):
        count = 1 + (u < KEPT) + len((LineFirst if line_first else Reduce).shapes(rows))
        buffers.append(list(refs[:count]))
        refs = refs[count:]
    small_sums, small_got, small_line, all_rows = refs[:4]
    send, recv, back_send, back_recv, credit, local, writes, small_send, small_recv, rows_send, rows_recv = refs[4:]
    wq, wk, wv, wo, wup, wdn, wpj = wholes
    place = Place()
    gather = Gather(place, units, shards, wholes, send, recv)
    own = [
        pltpu.make_async_copy(shard, whole.at[place.z, place.c], local.at[i])
        for i, (shard, whole) in enumerate(zip(shards, wholes))
    ]
    works, results = [], []
    for u, (array, j, rows, line_first) in enumerate(BLOCKS):
        rest = buffers[u]
        total, at = rest.pop(0), PLACES[u]
        core = (core_low, *(core_tall.at[i, :, pl.ds(0, rows), :] for i in range(3)), wpj.at[:, 0], wpj.at[:, 1])[at]
        kept = rest.pop(0) if u < KEPT else wup.at[:, 0, :, pl.ds(768 * (u - KEPT), 768)]
        grad = ring.at[u % RING, :, :, pl.ds(0, rows), :]
        kind = LineFirst if line_first else Reduce
        turns = (credit, SAID[u], u < sum(SAID))
        works.append(kind(place, u % 2 == 0, grad, kept, core, total, rest, back_send.at[u], back_recv.at[u], *turns))
        dst = outs[5].at[pl.ds(128 * j, 128), :] if array == 5 else outs[array].at[:, pl.ds(768 * j, 768)]
        results.append(pltpu.make_async_copy(total, dst, writes.at[u]))
    for copy in own:
        copy.start()
    place.greet()
    n = len(units)

    def receive(name):
        for stage, u in ARRIVALS.get(name, ()):
            if stage == 0:
                gather.start(u)
            elif stage < 4:
                gather.plane(u, stage - 1)
            elif stage < 7:
                gather.corner(u, stage - 4)
            elif stage == 7:
                gather.pair(u)
            else:
                gather.arrive(u)
                if u < n - LEFT:
                    gather.finish(u)

    x = wide(x_ref[...])
    n1[...] = low(x * norm_factor(x) * g1_ref[...].reshape(1, 768))
    for copy in own:
        copy.wait()
    place.meet()
    receive("start")
    receive("n1")
    ray = dot_exact(table_ref[...], near_ref[...])
    for h in range(ray.shape[0]):
        rolled = pltpu.roll(jnp.broadcast_to(ray[h : h + 1], (TILE, 512)), 0, 1, stride=1, stride_axis=0)
        band[h // 2, pl.ds((h % 2) * TILE, TILE), :] = rolled[:, :SPAN]
    receive("band")
    seg = seg_ref[...]
    seg_f = wide(seg)
    column = jnp.transpose(jnp.broadcast_to(seg_f, (TILE, 512)))
    edge = jnp.full((1, TILE), -1.0, jnp.float32)
    line = jnp.concatenate([edge, seg_f, edge], axis=1)
    for t in range(4):
        own_seg = column[t * TILE : (t + 1) * TILE]
        same = jnp.concatenate([own_seg] * 3, axis=1) == line[:, t * TILE : t * TILE + SPAN]
        hidden = jnp.where(same, 0.0, -1e30)
        for i in range(3):
            mask[3 * t + i] = hidden[:, i * TILE : (i + 1) * TILE]
    blank = jnp.zeros((TILE, 768), jnp.bfloat16)
    for ref in (keys, values):
        ref[pl.ds(0, TILE), :] = blank
        ref[pl.ds(640, TILE), :] = blank
    receive("mask")
    q[...] = low(dot(n1[...], flat(wq)))
    receive("q")
    keys[pl.ds(TILE, 512), :] = low(dot(n1[...], flat(wk)))
    receive("k")
    values[pl.ds(TILE, 512), :] = low(dot(n1[...], flat(wv)))
    receive("v")

    def pairs(first, last):
        @pl.loop(first, last)
        def _(p):
            for t in range(4):
                attend(p, t, q, keys, values, band, mask, probs, mixed)

    first = 0
    for p in range(6):
        if p == 5 or ARRIVALS.get(f"a{p}"):
            pairs(first, p + 1)
            first = p + 1
        receive(f"a{p}")
    hidden = wide(x_ref[...]) + dot(mixed[...], flat(wo))
    h1[...] = hidden
    n2[...] = low(hidden * norm_factor(hidden) * g2_ref[...].reshape(1, 768))
    receive("h")
    for j in range(4):
        cols = pl.ds(768 * j, 768)
        value, grad = gelu_both(dot(n2[...], flat(wup, slice(None), slice(None), slice(None), cols)))
        act[:, cols] = low(value)
        slope[:, cols] = low(grad)
        receive(f"u{j}")
    for j in range(3):
        part = jnp.concatenate([act[:, pl.ds(384 * s + 128 * j, 128)] for s in range(8)], axis=1)
        more = dot(part, flat(wdn, slice(None), slice(None), pl.ds(128 * j, 128)))
        h2[...] = (h1[...] if j == 0 else h2[...]) + more
        receive(f"d{j}")
    h = h2[...]
    factor = norm_factor(h)
    g3 = g3_ref[...].reshape(1, 768)
    fin = h * factor * g3
    eye = lax.broadcasted_iota(jnp.int32, (8, 8), 0) == lax.broadcasted_iota(jnp.int32, (8, 8), 1)
    pool = jnp.sum(jnp.where(eye, wide(pool_ref[...]), 0.0), axis=1, keepdims=True)
    member = jnp.where(seg_f == pool, 1.0, 0.0)
    count = jnp.sum(member, axis=1, keepdims=True)
    pooled = dot(low(member), low(fin)) / count
    receive("e1")
    wp = flat(wpj)
    both = dot(two_parts(pooled), wp)
    projected = both[:8] + both[8:]
    inverse = lax.rsqrt(jnp.sum(projected * projected, axis=-1, keepdims=True) + EPSILON)
    emb = projected * inverse
    up = emb_ref[...].reshape(8, 768)
    eg = inverse * (up - emb * jnp.sum(up * emb, axis=-1, keepdims=True))
    emb_out[...] = emb
    projection = Projection(place, all_rows, rows_send, rows_recv)

    def take(stage, u):
        work = works[u]
        if stage >= 10:
            projection.take(stage - 10)
        elif stage == 6:
            work.arrive()
            results[u].start()
        else:
            (work.start, work.first, work.second, work.third, work.spread, work.corner)[stage]()

    def serve(name):
        for stage, u in PLAN.get(name, ()):
            take(stage, u)

    def produce(u, value):
        works[u].g[...] = low(value).reshape(works[u].g.shape)
        serve(f"g{u}")

    projection.start(pooled, eg)
    serve("start")
    both = dot(two_parts(eg), flat(wpj), 1, 1)
    pooled_grad = (both[:8] + both[8:]) / count
    twice = low(jnp.concatenate([member, member], axis=0))
    fin_grad = dot(twice, two_parts(pooled_grad), 0, 0)
    stream, gain_three = norm_back(h, factor, g3, fin_grad)
    h2[...] = stream
    upstream[...] = low(stream)
    for j in range(3):
        picked = jnp.concatenate([act[:, pl.ds(384 * s + 128 * j, 128)] for s in range(8)], axis=1)
        produce(j, dot(picked, upstream[...], 0, 0))
    for u in range(n - LEFT, n):
        gather.finish(u)
    for j in range(4):
        cols = pl.ds(768 * j, 768)
        grad = low(wide(slope[:, cols]) * dot(upstream[...], flat(wdn, j), 1, 1))
        slope[:, cols] = grad
        produce(3 + j, dot(n2[...], grad, 0, 0))
        more = dot(grad, flat(wup, slice(None), slice(None), slice(None), cols), 1, 1)
        for i in range(2):
            where, half_more = pl.ds(2 * i, 2), more[:, 384 * i : 384 * (i + 1)].reshape(2, 256, 384)
            band[where] = half_more if j == 0 else band[where] + half_more
        serve(f"n{j}")
    n2_grad = jnp.concatenate([band[pl.ds(2 * i, 2)].reshape(512, 384) for i in range(2)], axis=1)
    h = h1[...]
    more, gain_two = norm_back(h, norm_factor(h), g2_ref[...].reshape(1, 768), n2_grad)
    through = h2[...] + more
    h2[...] = through
    upstream[...] = low(through)
    produce(7, dot(mixed[...], upstream[...], 0, 0))
    act[:, pl.ds(0, 768)] = low(dot(upstream[...], flat(wo), 1, 1))
    band[...] = jnp.zeros_like(band)
    serve("og")

    def pairs_back(first, last):
        @pl.loop(first, last)
        def _(p):
            mask[...] = jnp.zeros_like(mask)
            for t in range(4):
                attend_back(p, t, q, keys, values, probs, act, mask, band)
            heads, after = heads_of(p), pl.ds(pl.multiple_of(p * LANES + 768, LANES), LANES)
            slope[:, heads] = low(mask[pl.ds(1, 4)]).reshape(512, LANES)
            slope[:, after] = low(mask[pl.ds(7, 4)]).reshape(512, LANES)

    first = 0
    for p in range(6):
        if p == 5 or PLAN.get(f"a{p}"):
            pairs_back(first, p + 1)
            first = p + 1
        serve(f"a{p}")
    kg, vg, qg = slope[:, pl.ds(0, 768)], slope[:, pl.ds(768, 768)], act[:, pl.ds(768, 768)]
    produce(8, dot(n1[...], vg, 0, 0))
    produce(9, dot(n1[...], kg, 0, 0))
    produce(10, dot(n1[...], qg, 0, 0))
    n1_grad = dot(qg, flat(wq), 1, 1) + dot(kg, flat(wk), 1, 1) + dot(vg, flat(wv), 1, 1)
    x = wide(x_ref[...])
    more, gain_one = norm_back(x, norm_factor(x), g1_ref[...].reshape(1, 768), n1_grad)
    h2[...] = h2[...] + more
    last = pltpu.make_async_copy(h2, input_out, writes.at[len(BLOCKS)])
    last.start()
    serve("tail")
    turn = lax.broadcasted_iota(jnp.int32, (TILE, TILE), 0) + lax.broadcasted_iota(jnp.int32, (TILE, TILE), 1)
    mirror = low(jnp.where(turn == TILE - 1, 1.0, 0.0))
    rays[...] = jnp.zeros_like(rays)
    for h in range(12):
        tile = band[h // 2, pl.ds((h % 2) * TILE, TILE), :]
        high = low(tile)
        upside = dot(mirror, high) + dot(mirror, low(tile - wide(high)))
        spread = jnp.concatenate([upside, jnp.zeros((TILE, 512 - SPAN), jnp.float32)], axis=1)
        rolled = pltpu.roll(spread, 0, 1, stride=1, stride_axis=0)
        rays[pl.ds(h, 1), :] = jnp.sum(rolled, axis=0, keepdims=True)
    by_bucket = dot_exact(rays[...], far_ref[...], 1, 1)
    small_sums[0, :, pl.ds(0, 768)] = jnp.concatenate(
        [gain_one, gain_two, gain_three, jnp.zeros((5, 768), jnp.float32)], axis=0
    )
    small_sums[0, :, pl.ds(768, 256)] = jnp.zeros((8, 256), jnp.float32)
    small_sums[0, :, pl.ds(768, 32)] = by_bucket[:8]
    small_sums[0, :, pl.ds(896, 32)] = by_bucket[8:]
    small = Small(place, small_sums, small_got, small_line, small_send, small_recv)
    small.start()
    rest = PLAN["table"]
    for i in range(len(rest)):
        if i in (4, 9, 14):
            small.turn(i // 5)
        take(*rest[i])
    ring[0, :, :, pl.ds(0, 96), :] = low(projection.product()).reshape(4, 2, 96, 768)
    product = pltpu.make_async_copy(ring.at[0, place.z, place.c, pl.ds(0, 96), :], outs[6], writes.at[len(BLOCKS) + 1])
    product.start()
    small_out[...] = small.finish()
    product.wait()
    for copy in results:
        copy.wait()
    last.wait()


def far_buckets(buckets):
    return bucket_rows(np.arange(512) - 255, buckets)


def layer_all(x, seg_ids, pool_index, emb_grad, gains, table, shards):
    f32, b16 = jnp.float32, jnp.bfloat16
    units = [Unit(*unit) for unit in UNITS]
    held = [(512, 3072)] * 2 + [(512, 768)] * 5 + [(768, 768)] * 2 + [(768, 3072)]
    scratch = [pltpu.VMEM((4, 2) + shard.shape, b16) for shard in shards]
    scratch += [pltpu.VMEM(shape, b16) for shape in held]
    scratch += [pltpu.VMEM((512, 768), f32)] * 2
    scratch += [pltpu.VMEM((6, 2 * TILE, SPAN), f32), pltpu.VMEM((12, TILE, LANES), f32), pltpu.VMEM((16, 512), f32)]
    scratch += [pltpu.VMEM((RING, 4, 2, 128, 768), b16), pltpu.VMEM((4, 96, 768), b16)]
    scratch += [pltpu.VMEM((3, 4, 128, 768), b16)]
    for u, (_, _, rows, line_first) in enumerate(BLOCKS):
        shapes = [(rows, 768)] + [(4, rows, 768)] * (u < KEPT)
        shapes += (LineFirst if line_first else Reduce).shapes(rows)
        scratch += [pltpu.VMEM(shape, b16) for shape in shapes]
    scratch += [pltpu.VMEM((k, 8, 1024), f32) for k in (4, 3, 4)] + [pltpu.VMEM((2, 4, 4, 16, 768), b16)]
    dma = pltpu.SemaphoreType.DMA
    scratch += [dma((len(units), Gather.SEMS))] * 2 + [dma((len(BLOCKS), Reduce.SEMS))] * 2
    scratch += [pltpu.SemaphoreType.REGULAR, dma((7,)), dma((len(BLOCKS) + 2,)), dma((Small.SEMS,)), dma((Small.SEMS,))]
    scratch += [dma((Projection.SEMS,))] * 2
    outs = [jax.ShapeDtypeStruct(shard.shape, b16) for shard in shards]
    outs += [jax.ShapeDtypeStruct(s, f32) for s in [(512, 768), (8, 768), (8, 1024)]]
    vmem, large = pl.BlockSpec(memory_space=pltpu.VMEM), pl.BlockSpec(memory_space=pl.ANY)
    buckets = table.shape[1]
    return pl.pallas_call(
        partial(layer_kernel, units),
        out_shape=outs,
        in_specs=[vmem] * 10 + [large] * 7,
        out_specs=[large] * 8 + [vmem] * 2,
        scratch_shapes=scratch,
        compiler_params=pltpu.CompilerParams(
            collective_id=0, has_side_effects=True, vmem_limit_bytes=VMEM_BYTES
        ),
        name="layer",
    )(x, seg_ids, pool_index, emb_grad, *gains, table, ray_buckets(buckets), far_buckets(buckets), *shards)


def finish_kernel(emb_in, input_in, small_in, *refs):
    grads, outs = refs[:7], refs[7:]
    emb_out, input_out, gains, table = outs[0], outs[1], outs[9:12], outs[12]
    emb_out[...] = emb_in[...].reshape(emb_out.shape)
    input_out[...] = input_in[...].reshape(input_out.shape)
    for grad, out in zip(grads, outs[2:9]):
        out[...] = wide(grad[...])
    for i, gain in enumerate(gains):
        gain[...] = small_in[pl.ds(i, 1), pl.ds(0, 768)].reshape(768)
    both = jnp.concatenate([small_in[:, pl.ds(768, 128)], small_in[:, pl.ds(896, 128)]], axis=0)
    table[...] = both[:12, :32]


def finish_all(emb, input_grad, small, grads):
    f32 = jnp.float32
    shapes = [(1, 8, 768), (1, 512, 768)] + [g.shape for g in grads] + [(768,)] * 3 + [(12, 32)]
    vmem = pl.BlockSpec(memory_space=pltpu.VMEM)
    return pl.pallas_call(
        finish_kernel,
        out_shape=[jax.ShapeDtypeStruct(s, f32) for s in shapes],
        in_specs=[vmem] * 10,
        out_specs=[vmem] * 13,
        compiler_params=pltpu.CompilerParams(vmem_limit_bytes=VMEM_BYTES),
        name="finish",
    )(emb, input_grad, small, *grads)


def near_device(
    inputs,
    seg_ids,
    pool_index,
    w_query,
    w_key,
    w_value,
    w_out,
    w_up,
    w_down,
    w_proj,
    gain_attn,
    gain_ffn,
    gain_final,
    bias_table,
    emb_grad,
):
    x = inputs.reshape(-1, inputs.shape[-1])
    shards = (w_query, w_key, w_value, w_out, w_up, w_down, w_proj)
    gains = (gain_attn, gain_ffn, gain_final)
    *grads, input_grad, emb, small = layer_all(x, seg_ids, pool_index, emb_grad, gains, bias_table.T, shards)
    out = finish_all(emb, input_grad, small, grads)
    return (*out[:12], out[12].T)


def general(
    inputs,
    seg_ids,
    pool_index,
    w_query,
    w_key,
    w_value,
    w_out,
    w_up,
    w_down,
    w_proj,
    gain_attn,
    gain_ffn,
    gain_final,
    bias_table,
    emb_grad,
):
    rows, length, width = inputs.shape
    buckets, heads = bias_table.shape
    head_dim = width // heads
    tokens = rows * length
    head_shape = (rows, length, heads, head_dim)
    gathered = (
        lax.all_gather(w_query, "fsdp", axis=0, tiled=True),
        lax.all_gather(w_key, "fsdp", axis=0, tiled=True),
        lax.all_gather(w_value, "fsdp", axis=0, tiled=True),
        lax.all_gather(w_out, "fsdp", axis=0, tiled=True),
        lax.all_gather(w_up, "fsdp", axis=0, tiled=True),
        lax.all_gather(w_down, "fsdp", axis=0, tiled=True),
        lax.all_gather(w_proj, "fsdp", axis=0, tiled=True),
    )
    full_query, full_key, full_value, full_out, full_up, full_down, full_proj = gathered
    flat = inputs.reshape(tokens, width).astype(jnp.float32)
    normed_one, factor_one = rms_forward(flat, gain_attn)
    normed_one = normed_one.astype(jnp.bfloat16)
    queries = matmul(normed_one, full_query).astype(jnp.bfloat16).reshape(head_shape)
    key_rows = matmul(normed_one, full_key).astype(jnp.bfloat16).reshape(head_shape)
    value_rows = matmul(normed_one, full_value).astype(jnp.bfloat16).reshape(head_shape)
    bucket_ids = jnp.asarray(bucket_table(length, buckets, REACH))
    onehot_cols = (
        jnp.arange(buckets, dtype=jnp.int32)[:, None] == bucket_ids.reshape(1, length * length)
    ).astype(jnp.bfloat16)
    bias = jnp.dot(bias_table.T, onehot_cols.astype(jnp.float32), precision=HIGH).reshape(
        heads, length, length
    )

    def attend_row(pieces):
        query_row, key_row, value_row, seg_row = pieces
        scores = row_scores(query_row, key_row, seg_row, bias)
        row_peak = jnp.max(scores, axis=-1, keepdims=True)
        log_total = row_peak + jnp.log(jnp.sum(jnp.exp(scores - row_peak), axis=-1, keepdims=True))
        soft_low = jnp.exp(scores - log_total).astype(jnp.bfloat16)
        mixed = jnp.einsum("hqk,khd->qhd", soft_low, value_row, preferred_element_type=jnp.float32)
        return (mixed.astype(jnp.bfloat16), log_total)

    attended, log_totals = lax.map(attend_row, (queries, key_rows, value_rows, seg_ids))
    attended_flat = attended.reshape(tokens, width)
    hidden_one = flat + matmul(attended_flat, full_out)
    normed_two, factor_two = rms_forward(hidden_one, gain_ffn)
    normed_two = normed_two.astype(jnp.bfloat16)
    pre_act = matmul(normed_two, full_up)
    activated = jax.nn.gelu(pre_act, approximate=True).astype(jnp.bfloat16)
    hidden_two = hidden_one + matmul(activated, full_down)
    final_rows, factor_three = rms_forward(hidden_two, gain_final)
    member = (seg_ids[:, None, :] == pool_index[:, :, None]).astype(jnp.float32)
    counts = jnp.sum(member, axis=-1, keepdims=True)
    pooled = (
        jnp.einsum("rpl,rld->rpd", member, final_rows.reshape(rows, length, width), precision=HIGH)
        / counts
    )
    proj_full = full_proj.astype(jnp.float32)
    projected = jnp.einsum("rpd,de->rpe", pooled, proj_full, precision=HIGH)
    inverse_len = lax.rsqrt(jnp.sum(projected * projected, axis=-1, keepdims=True) + EPSILON)
    embeddings = projected * inverse_len
    emb_dot = jnp.sum(emb_grad * embeddings, axis=-1, keepdims=True)
    projected_grad = inverse_len * (emb_grad - embeddings * emb_dot)
    grad_proj = jnp.einsum("rpd,rpe->de", pooled, projected_grad, precision=HIGH)
    pooled_grad = jnp.einsum("rpe,de->rpd", projected_grad, proj_full, precision=HIGH) / counts
    final_grad = jnp.einsum("rpl,rpd->rld", member, pooled_grad, precision=HIGH).reshape(
        tokens, width
    )
    stream_two, grad_gain_final = rms_backward(hidden_two, factor_three, gain_final, final_grad)
    back_weights = (
        lax.all_gather(w_query, "fsdp", axis=0, tiled=True),
        lax.all_gather(w_key, "fsdp", axis=0, tiled=True),
        lax.all_gather(w_value, "fsdp", axis=0, tiled=True),
        lax.all_gather(w_out, "fsdp", axis=0, tiled=True),
        lax.all_gather(w_up, "fsdp", axis=0, tiled=True),
        lax.all_gather(w_down, "fsdp", axis=0, tiled=True),
        lax.all_gather(w_proj, "fsdp", axis=0, tiled=True),
    )
    back_query, back_key, back_value, back_out, back_up, back_down, back_proj = back_weights
    ffn_grad = stream_two.astype(jnp.bfloat16)
    grad_down = matmul_left(activated, ffn_grad)
    act_grad = matmul_right(ffn_grad, back_down)
    gelu_pullback = jax.vjp(partial(jax.nn.gelu, approximate=True), pre_act)[1]
    pre_grad = gelu_pullback(act_grad)[0].astype(jnp.bfloat16)
    grad_up = matmul_left(normed_two, pre_grad)
    normed_two_grad = matmul_right(pre_grad, back_up)
    stream_mid, grad_gain_ffn = rms_backward(hidden_one, factor_two, gain_ffn, normed_two_grad)
    stream_one = stream_two + stream_mid
    attn_grad = stream_one.astype(jnp.bfloat16)
    grad_out = matmul_left(attended_flat, attn_grad)
    mixed_grad = matmul_right(attn_grad, back_out).astype(jnp.bfloat16).reshape(head_shape)

    def attend_back(pieces):
        query_row, key_row, value_row, seg_row, log_total, upstream_row = pieces
        scores = row_scores(query_row, key_row, seg_row, bias)
        soft_rows = jnp.exp(scores - log_total)
        soft_grad = jnp.einsum(
            "qhd,khd->hqk", upstream_row, value_row, preferred_element_type=jnp.float32
        )
        score_grad = (
            soft_rows * (soft_grad - jnp.sum(soft_rows * soft_grad, axis=-1, keepdims=True))
        ).astype(jnp.bfloat16)
        query_grad = jnp.einsum(
            "hqk,khd->qhd", score_grad, key_row, preferred_element_type=jnp.float32
        ).astype(jnp.bfloat16)
        key_grad = jnp.einsum(
            "hqk,qhd->khd", score_grad, query_row, preferred_element_type=jnp.float32
        ).astype(jnp.bfloat16)
        value_grad = jnp.einsum(
            "hqk,qhd->khd",
            soft_rows.astype(jnp.bfloat16),
            upstream_row,
            preferred_element_type=jnp.float32,
        ).astype(jnp.bfloat16)
        table_grad = matmul_right(score_grad.reshape(heads, length * length), onehot_cols)
        return (query_grad, key_grad, value_grad, table_grad)

    query_grads, key_grads, value_grads, table_grads = lax.map(
        attend_back, (queries, key_rows, value_rows, seg_ids, log_totals, mixed_grad)
    )
    grad_table = jnp.sum(table_grads, axis=0).T
    query_flat = query_grads.reshape(tokens, width)
    key_flat = key_grads.reshape(tokens, width)
    value_flat = value_grads.reshape(tokens, width)
    grad_query = matmul_left(normed_one, query_flat)
    grad_key = matmul_left(normed_one, key_flat)
    grad_value = matmul_left(normed_one, value_flat)
    normed_one_grad = (
        matmul_right(query_flat, back_query)
        + matmul_right(key_flat, back_key)
        + matmul_right(value_flat, back_value)
    )
    stream_in, grad_gain_attn = rms_backward(flat, factor_one, gain_attn, normed_one_grad)
    input_grad = (stream_one + stream_in).reshape(rows, length, width)
    shard_query, shard_key, shard_value, shard_out, shard_up, shard_down, shard_proj = (
        lax.psum_scatter(grad_query, "fsdp", scatter_dimension=0, tiled=True),
        lax.psum_scatter(grad_key, "fsdp", scatter_dimension=0, tiled=True),
        lax.psum_scatter(grad_value, "fsdp", scatter_dimension=0, tiled=True),
        lax.psum_scatter(grad_out, "fsdp", scatter_dimension=0, tiled=True),
        lax.psum_scatter(grad_up, "fsdp", scatter_dimension=0, tiled=True),
        lax.psum_scatter(grad_down, "fsdp", scatter_dimension=0, tiled=True),
        lax.psum_scatter(grad_proj, "fsdp", scatter_dimension=0, tiled=True),
    )
    summed = (
        lax.psum(shard_query.astype(jnp.bfloat16), "dp").astype(jnp.float32),
        lax.psum(shard_key.astype(jnp.bfloat16), "dp").astype(jnp.float32),
        lax.psum(shard_value.astype(jnp.bfloat16), "dp").astype(jnp.float32),
        lax.psum(shard_out.astype(jnp.bfloat16), "dp").astype(jnp.float32),
        lax.psum(shard_up.astype(jnp.bfloat16), "dp").astype(jnp.float32),
        lax.psum(shard_down.astype(jnp.bfloat16), "dp").astype(jnp.float32),
        lax.psum(shard_proj.astype(jnp.bfloat16), "dp").astype(jnp.float32),
    )
    smalls = lax.psum((grad_gain_attn, grad_gain_ffn, grad_gain_final, grad_table), ("dp", "fsdp"))
    return (
        embeddings,
        input_grad,
        summed[0],
        summed[1],
        summed[2],
        summed[3],
        summed[4],
        summed[5],
        summed[6],
        smalls[0],
        smalls[1],
        smalls[2],
        smalls[3],
    )


def solution(mesh):
    near = (mesh.shape["dp"], mesh.shape["fsdp"]) == (4, 8)
    return jax.shard_map(
        near_device if near else general,
        mesh=mesh,
        in_specs=(
            P(("dp", "fsdp"), None, None),
            P(("dp", "fsdp"), None),
            P(("dp", "fsdp"), None),
            P("fsdp", None),
            P("fsdp", None),
            P("fsdp", None),
            P("fsdp", None),
            P("fsdp", None),
            P("fsdp", None),
            P("fsdp", None),
            P(),
            P(),
            P(),
            P(),
            P(("dp", "fsdp"), None, None),
        ),
        out_specs=(
            P(("dp", "fsdp"), None, None),
            P(("dp", "fsdp"), None, None),
            P("fsdp", None),
            P("fsdp", None),
            P("fsdp", None),
            P("fsdp", None),
            P("fsdp", None),
            P("fsdp", None),
            P("fsdp", None),
            P(),
            P(),
            P(),
            P(),
        ),
        check_vma=False,
    )
```

```python
import math
from functools import partial

import jax
import jax.numpy as jnp
import numpy as np
from jax import lax
from jax.experimental import pallas as pl
from jax.experimental.pallas import tpu as pltpu
from jax.sharding import PartitionSpec as P

REACH = 128


EPSILON = 1e-06
VMEM_BYTES = 64 * 2**20
HIGH = lax.Precision.HIGHEST


def bucket_table(length, buckets, reach):
    positions = np.arange(length)
    relative = positions[None, :] - positions[:, None]
    halfway = buckets // 2
    exact_span = halfway // 2
    distance = np.abs(relative)
    logged = exact_span + (
        np.log(np.maximum(distance, 1) / exact_span)
        / np.log(reach / exact_span)
        * (halfway - exact_span)
    ).astype(np.int64)
    logged = np.minimum(logged, halfway - 1)
    result = (relative > 0).astype(np.int64) * halfway + np.where(
        distance < exact_span, distance, logged
    )
    return result.astype(np.int32)


def rms_forward(values, gain):
    factor = lax.rsqrt(jnp.mean(values * values, axis=-1, keepdims=True) + EPSILON)
    return (values * factor * gain, factor)


def rms_backward(values, factor, gain, upstream):
    normed = values * factor
    gain_grad = jnp.sum(upstream * normed, axis=0)
    inner = upstream * gain
    return (factor * (inner - normed * jnp.mean(inner * normed, axis=-1, keepdims=True)), gain_grad)


def matmul(left, right):
    return jnp.dot(left, right, preferred_element_type=jnp.float32)


def matmul_left(left, right):
    return lax.dot_general(
        left, right, (((0,), (0,)), ((), ())), preferred_element_type=jnp.float32
    )


def matmul_right(left, right):
    return lax.dot_general(
        left, right, (((1,), (1,)), ((), ())), preferred_element_type=jnp.float32
    )


def row_scores(query_row, key_row, seg_row, bias):
    raw_scores = jnp.einsum("qhd,khd->hqk", query_row, key_row, preferred_element_type=jnp.float32)
    same_doc = (seg_row[:, None] == seg_row[None, :])[None]
    return jnp.where(same_doc, raw_scores + bias, -1e30)


MESH = pl.DeviceIdType.MESH
LANES = 128


class Place:
    def __init__(self):
        self.dp, self.fsdp = lax.axis_index("dp"), lax.axis_index("fsdp")
        self.y, self.x = self.dp // 2, self.dp % 2
        self.z, self.c = self.fsdp // 2, self.fsdp % 2

    def core(self):
        return (self.dp, self.z * 2 + (1 - self.c))

    def at_x(self):
        return (self.y * 2 + (1 - self.x), self.fsdp)

    def at_y(self):
        return ((1 - self.y) * 2 + self.x, self.fsdp)

    def at_xy(self):
        return ((1 - self.y) * 2 + (1 - self.x), self.fsdp)

    def up(self, d):
        return lax.rem(self.z + d, 4)

    def down(self, d):
        return lax.rem(self.z + 4 - d, 4)

    def at_z(self, d):
        return (self.dp, self.up(d) * 2 + self.c)

    def greet(self):
        partners = [self.core(), self.at_x(), self.at_y(), self.at_xy()]
        partners += [self.at_z(d) for d in (1, 2, 3)]
        for partner in partners:
            pl.semaphore_signal(
                pltpu.get_barrier_semaphore(), inc=1, device_id=partner, device_id_type=MESH
            )
        self.greeted = len(partners)

    def meet(self):
        pl.semaphore_wait(pltpu.get_barrier_semaphore(), self.greeted)


def remote(src, dst, send, recv, device):
    return pltpu.make_async_remote_copy(
        src_ref=src, dst_ref=dst, send_sem=send, recv_sem=recv, device_id=device, device_id_type=MESH
    )


def half(which, size, start=0):
    return pl.ds(pl.multiple_of(start + which * (size // 2), size // 2 if start % (size // 2) == 0 else 16), size // 2)


class Unit:
    def __init__(self, array, first, rows, left, wide, along_z):
        self.array, self.first, self.rows, self.left, self.wide = array, first, rows, left, wide
        self.along_z = along_z

    def quarter(self, y, x):
        return (half(y, self.rows, self.first), half(x, self.wide, self.left))

    def whole(self):
        return (pl.ds(self.first, self.rows), pl.ds(self.left, self.wide))


class Gather:
    SEMS = 14

    def __init__(self, place, units, shards, wholes, send, recv):
        self.p, self.units, self.shards, self.wholes = place, units, shards, wholes
        self.send, self.recv = send, recv
        z = place.z
        late = jnp.where(z == 0, 1, 3)
        self.turns = (2, 4 - late, late)
        self.inner = jnp.logical_and(z > 0, z < 3)

    def _part(self, u, z, y, x):
        unit = self.units[u]
        where = unit.whole() if unit.along_z else unit.quarter(y, x)
        return self.wholes[unit.array].at[(z, self.p.c) + where]

    def _z(self, u, d):
        p, unit = self.p, self.units[u]
        src = self.shards[unit.array].at[unit.whole() if unit.along_z else unit.quarter(p.y, p.x)]
        return remote(src, self._part(u, p.z, p.y, p.x), self.send.at[u, d - 1], self.recv.at[u, d - 1], p.at_z(d))

    def _sends(self, u):
        return [(self._z(u, 1), self.p.z != 3), (self._z(u, 2), None), (self._z(u, 3), self.p.z != 0)]

    def _hand_on(self, u):
        p = self.p
        ref = self._part(u, p.down(2), p.y, p.x)
        end = 3 * (p.z - 1)
        return remote(ref, ref, self.send.at[u, 13], self.recv.at[u, 2 * (p.z - 1)], (p.dp, end * 2 + p.c))

    def _hop(self, u, turn, kind, y, x, device):
        d = self.turns[turn]
        ref = self._part(u, self.p.down(d), y, x)
        k = 3 * kind + d - 1
        return remote(ref, ref, self.send.at[u, k], self.recv.at[u, k], device)

    def _to_x(self, u, turn):
        return self._hop(u, turn, 1, self.p.y, self.p.x, self.p.at_x())

    def _to_y(self, u, turn):
        return self._hop(u, turn, 2, self.p.y, self.p.x, self.p.at_y())

    def _through_x(self, u, turn):
        return (u + min(turn, 1)) % 2 == 0

    def _diagonal(self, u, turn):
        p = self.p
        if self._through_x(u, turn):
            return self._hop(u, turn, 3, p.y, 1 - p.x, p.at_y())
        return self._hop(u, turn, 3, 1 - p.y, p.x, p.at_x())

    def _core(self, u):
        unit = self.units[u]
        ref = self.wholes[unit.array].at[(slice(None), self.p.c) + unit.whole()]
        return remote(ref, ref, self.send.at[u, 12], self.recv.at[u, 12], self.p.core())

    def start(self, u):
        for copy, condition in self._sends(u):
            if condition is None:
                copy.start()
            else:
                pl.when(condition)(copy.start)

    def plane(self, u, turn):
        self._z(u, self.turns[turn]).wait_recv()
        if turn == 0:
            pl.when(self.inner)(lambda: self._hand_on(u).start())
        if not self.units[u].along_z:
            self._to_x(u, turn).start()
            self._to_y(u, turn).start()

    def corner(self, u, turn):
        early, later = self._to_x(u, turn), self._to_y(u, turn)
        if not self._through_x(u, turn):
            early, later = later, early
        early.wait_recv()
        self._diagonal(u, turn).start()
        later.wait_recv()

    def pair(self, u):
        if not self.units[u].along_z:
            for turn in range(3):
                self._diagonal(u, turn).wait_recv()
        self._core(u).start()

    def arrive(self, u):
        self._core(u).wait_recv()

    def finish(self, u):
        for copy, condition in self._sends(u):
            if condition is None:
                copy.wait_send()
            else:
                pl.when(condition)(copy.wait_send)
        pl.when(self.inner)(lambda: self._hand_on(u).wait_send())
        if not self.units[u].along_z:
            for turn in range(3):
                self._to_x(u, turn).wait_send()
                self._to_y(u, turn).wait_send()
                self._diagonal(u, turn).wait_send()
        self._core(u).wait_send()


UNITS = [
    (0, 0, 96, 0, 256, False),
    (0, 0, 96, 256, 256, False),
    (0, 0, 96, 512, 256, False),
    (1, 0, 96, 0, 768, False),
    (2, 0, 96, 0, 768, False),
    (3, 0, 96, 0, 768, False),
    (4, 0, 96, 0, 768, False),
    (4, 0, 96, 768, 768, False),
    (4, 0, 96, 1536, 768, False),
    (4, 0, 96, 2304, 768, False),
    (5, 0, 128, 0, 768, False),
    (5, 128, 128, 0, 768, True),
    (5, 256, 128, 0, 768, False),
    (6, 0, 96, 0, 256, False),
    (6, 0, 96, 256, 256, False),
    (6, 0, 96, 512, 256, False),
]
ARRIVALS = {
    "start": [
        (0, 2), (0, 1), (0, 3), (2, 2), (0, 0), (1, 1), (0, 4), (3, 1), (1, 2), (0, 15), (0, 7), (2,
        0), (2, 1), (1, 0), (3, 2), (1, 3), (5, 2), (0, 5), (0, 8), (5, 1), (2, 4), (6, 2), (3, 3),
        (3, 0), (2, 3), (6, 1), (1, 4),
    ],
    "n1": [
        (3, 4), (0, 10), (2, 7), (0, 13), (6, 0), (4, 3), (5, 0), (4, 1), (6, 3), (5, 4), (1, 7),
        (1, 5), (2, 5), (4, 0), (0, 6), (5, 3), (3, 5), (1, 8), (6, 4), (0, 9), (7, 1), (4, 4), (7,
        0),
    ],
    "band": [
        (7, 3), (4, 2), (3, 7), (1, 10), (2, 13),
    ],
    "mask": [
        (2, 8), (7, 2), (0, 12), (7, 4), (8, 3), (8, 1), (2, 10), (0, 14), (8, 0), (2, 6), (6, 7),
        (3, 8), (1, 6), (4, 8), (8, 2),
    ],
    "q": [
        (0, 11), (8, 4), (4, 7),
    ],
    "v": [
        (2, 15), (5, 8), (2, 9),
    ],
    "a0": [
        (3, 10), (6, 8), (1, 13), (4, 5), (3, 6), (5, 5), (1, 12),
    ],
    "a1": [
        (6, 5), (5, 6), (1, 15), (1, 14), (1, 9),
    ],
    "a2": [
        (5, 7), (3, 13), (2, 11), (3, 12), (4, 6),
    ],
    "a3": [
        (2, 14), (4, 13), (7, 8), (6, 6), (7, 5), (3, 14), (3, 15), (3, 9),
    ],
    "a4": [
        (2, 12), (4, 9), (6, 13), (5, 9), (6, 10), (5, 15), (6, 12), (4, 15), (5, 14), (8, 5), (5,
        13), (4, 10), (7, 6), (7, 7), (6, 15), (4, 12), (1, 11),
    ],
    "a5": [
        (6, 9),
    ],
    "h": [
        (8, 7), (4, 14), (8, 6), (5, 12), (8, 8), (5, 10), (3, 11),
    ],
    "u0": [
        (7, 15), (6, 14), (7, 9), (7, 11),
    ],
    "u1": [
        (7, 10),
    ],
    "u2": [
        (7, 13), (7, 12), (8, 9), (8, 11), (8, 15),
    ],
    "u3": [
        (8, 10),
    ],
    "d0": [
        (7, 14),
    ],
    "d1": [
        (8, 12),
    ],
    "e1": [
        (8, 14), (8, 13),
    ],
}


def dot(a, b, ca=1, cb=0):
    return lax.dot_general(a, b, (((ca,), (cb,)), ((), ())), preferred_element_type=jnp.float32)


def dot_exact(a, b, ca=1, cb=0):
    return lax.dot_general(
        a, b, (((ca,), (cb,)), ((), ())), precision=HIGH, preferred_element_type=jnp.float32
    )


def low(v):
    return v.astype(jnp.bfloat16)


def wide(v):
    return v.astype(jnp.float32)


def two_parts(v):
    high = wide(low(v))
    return low(jnp.concatenate([high, v - high], axis=0))


def norm_factor(v):
    return lax.rsqrt(jnp.mean(v * v, axis=-1, keepdims=True) + EPSILON)


def norm_back(v, factor, gain, upstream):
    normed = v * factor
    inner = upstream * gain
    grad = factor * (inner - normed * jnp.mean(inner * normed, axis=-1, keepdims=True))
    return grad, jnp.sum(upstream * normed, axis=0, keepdims=True)


def gelu_both(v):
    scale = math.sqrt(2.0 / math.pi)
    square = v * v
    bent = jnp.tanh(scale * v * (1.0 + 0.044715 * square))
    share = 0.5 + 0.5 * bent
    slope = share + (0.5 * scale) * v * (1.0 - bent * bent) * (1.0 + (3 * 0.044715) * square)
    return v * share, slope


def flat(ref, *where):
    value = ref[where] if where else ref[...]
    return value.reshape(-1, value.shape[-1])


TILE, SPAN = 128, 384


def rows_of(t):
    return pl.ds(t * TILE, TILE)


def span_of(t):
    return pl.ds(t * TILE, SPAN)


def heads_of(p):
    return pl.ds(pl.multiple_of(p * LANES, LANES), LANES)


def stacked(v, axis=0):
    first = lax.broadcasted_iota(jnp.int32, v.shape, 1) < LANES // 2
    zero = jnp.zeros_like(v)
    return jnp.concatenate([jnp.where(first, v, zero), jnp.where(first, zero, v)], axis=axis)


def side_by_side(v):
    return jnp.concatenate([v[:TILE], v[TILE:]], axis=1)


def probs_at(p, t):
    return (pl.ds(pl.multiple_of((p // 2) * 256, 256), 256), pl.ds(pl.multiple_of((p % 2) * 1536, 1536) + t * SPAN, SPAN))


def attend(p, t, q, keys, values, band, mask, probs, mixed):
    scores = dot(stacked(q[rows_of(t), heads_of(p)]), keys[span_of(t), heads_of(p)], 1, 1)
    hidden = jnp.concatenate([mask[3 * t + i] for i in range(3)], axis=1)
    scores = scores + band[p] + jnp.concatenate([hidden, hidden], axis=0)
    powered = jnp.exp(scores - jnp.max(scores, axis=1, keepdims=True))
    soft = low(powered * (1.0 / jnp.sum(powered, axis=1, keepdims=True)))
    probs[probs_at(p, t)] = soft
    out = dot(side_by_side(soft), stacked(values[span_of(t), heads_of(p)]))
    mixed[rows_of(t), heads_of(p)] = low(out)


def bucket_rows(away, buckets):
    halfway = buckets // 2
    exact = halfway // 2
    distance = np.abs(away)
    logged = exact + (
        np.log(np.maximum(distance, 1) / exact) / np.log(REACH / exact) * (halfway - exact)
    ).astype(np.int64)
    bucket = (away > 0) * halfway + np.where(distance < exact, distance, np.minimum(logged, halfway - 1))
    return (np.arange(buckets)[:, None] == bucket[None, :]).astype(np.float32)


def ray_buckets(buckets):
    near = np.arange(512)
    return bucket_rows(np.where(near < SPAN, near - TILE, near - 512 - TILE), buckets)


class Reduce:
    SEMS = 11

    @staticmethod
    def shapes(rows):
        return [(2, rows, 384), (2, rows // 2, 768), (2, rows // 2, 384), (2, rows // 2, 384), (3, rows // 2, 384)]

    def __init__(self, place, through_x, grad, own, core, total, buffers, send, recv, credit, waits, gives):
        self.p, self.g, self.own, self.rc, self.f = place, grad, own, core, total
        self.through_x, self.send, self.recv = through_x, send, recv
        self.credit, self.waits, self.gives = credit, waits, gives
        self._take(buffers)
        p = place
        self.row = [half(i, own.shape[1]) for i in (p.y, 1 - p.y)]
        self.col = [half(i, 768) for i in (p.x, 1 - p.x)]

    def _take(self, buffers):
        self.rx, self.ry, self.sx, self.sy, self.rz = buffers

    def _copy(self, k, src, dst, device):
        return remote(src, dst, self.send.at[k], self.recv.at[k], device)

    def _core(self):
        return self._copy(0, self.g.at[:, 1 - self.p.c], self.rc, self.p.core())

    def _first(self):
        p, low, high = self.p, pl.ds(0, 2), pl.ds(2, 2)
        return [
            self._copy(1, self.own.at[low, :, self.col[1]], self.rx, p.at_x()),
            self._copy(2, self.own.at[high, self.row[1], :], self.ry, p.at_y()),
        ]

    def _second(self):
        p, low, high = self.p, pl.ds(0, 2), pl.ds(2, 2)
        return [
            self._copy(3, self.own.at[low, self.row[1], self.col[0]], self.sy, p.at_y()),
            self._copy(4, self.own.at[high, self.row[0], self.col[1]], self.sx, p.at_x()),
        ]

    def _third(self):
        p = self.p
        return [
            self._copy(4 + d, self.own.at[p.up(d), self.row[0], self.col[0]], self.rz.at[d - 1], p.at_z(d))
            for d in (1, 2, 3)
        ]

    def _spread(self):
        p, part = self.p, self.f.at[self.row[0], self.col[0]]
        return [self._copy(8 + i, part, part, device) for i, device in enumerate((p.at_x(), p.at_y()))]

    def _corner(self):
        p = self.p
        if self.through_x:
            part, device = self.f.at[self.row[0], self.col[1]], p.at_y()
        else:
            part, device = self.f.at[self.row[1], self.col[0]], p.at_x()
        return self._copy(10, part, part, device)

    def _add(self, where, other):
        self.own[where] = low(wide(self.own[where]) + wide(other[...]))

    def start(self):
        if self.waits:
            pl.semaphore_wait(self.credit, self.waits)
        self._core().start()

    def first(self):
        self._core().wait()
        for i in range(4):
            self.own[i] = low(wide(self.g[i, self.p.c]) + wide(self.rc[i]))
        if self.gives:
            pl.semaphore_signal(self.credit, inc=1, device_id=self.p.core(), device_id_type=MESH)
        for copy in self._first():
            copy.start()

    def second(self):
        along_x, along_y = self._first()
        to_y, to_x = self._second()
        along_x.wait_recv()
        for i in range(2):
            self._add((i, slice(None), self.col[0]), self.rx.at[i])
        to_y.start()
        along_y.wait_recv()
        for i in range(2):
            self._add((2 + i, self.row[0], slice(None)), self.ry.at[i])
        to_x.start()
        self._sent((along_x, along_y))

    def third(self):
        for copy in self._second():
            copy.wait_recv()
        for i in range(2):
            self._add((i, self.row[0], self.col[0]), self.sy.at[i])
            self._add((2 + i, self.row[0], self.col[0]), self.sx.at[i])
        for copy in self._third():
            copy.start()
        self._sent(self._second())

    def _total(self):
        total = wide(self.own[self.p.z, self.row[0], self.col[0]])
        for d, copy in enumerate(self._third()):
            copy.wait_recv()
            total = total + wide(self.rz[d])
        return total

    def spread(self):
        self.f[self.row[0], self.col[0]] = low(self._total())
        for copy in self._spread():
            copy.start()
        self._sent(self._third())

    def corner(self):
        along_x, along_y = self._spread()
        early, later = (along_x, along_y) if self.through_x else (along_y, along_x)
        early.wait_recv()
        self._corner().start()
        later.wait_recv()
        self._sent(self._spread())

    def arrive(self):
        self._corner().wait()

    @staticmethod
    def _sent(copies):
        for copy in copies:
            copy.wait_send()


class LineFirst(Reduce):
    @staticmethod
    def shapes(rows):
        return [(3, rows, 768), (rows, 384), (rows // 2, 768), (rows // 2, 384)]

    def _take(self, buffers):
        self.rz, self.rx, self.ry, self.rq = buffers

    def _mine(self):
        return self.own.at[self.p.z]

    def _first(self):
        p = self.p
        return [self._copy(d, self.own.at[p.up(d)], self.rz.at[d - 1], p.at_z(d)) for d in (1, 2, 3)]

    def _second(self):
        if self.through_x:
            return [self._copy(4, self._mine().at[:, self.col[1]], self.rx, self.p.at_x())]
        return [self._copy(4, self._mine().at[self.row[1], :], self.ry, self.p.at_y())]

    def _third(self):
        if self.through_x:
            return [self._copy(5, self._mine().at[self.row[1], self.col[0]], self.rq, self.p.at_y())]
        return [self._copy(5, self._mine().at[self.row[0], self.col[1]], self.rq, self.p.at_x())]

    def second(self):
        total = wide(self._mine()[...])
        for d, copy in enumerate(self._first()):
            copy.wait_recv()
            total = total + wide(self.rz[d])
        self._mine()[...] = low(total)
        self._second()[0].start()
        self._sent(self._first())

    def third(self):
        self._second()[0].wait_recv()
        if self.through_x:
            self._add((self.p.z, slice(None), self.col[0]), self.rx)
        else:
            self._add((self.p.z, self.row[0], slice(None)), self.ry)
        self._third()[0].start()
        self._sent(self._second())

    def _total(self):
        self._third()[0].wait_recv()
        return wide(self.own[self.p.z, self.row[0], self.col[0]]) + wide(self.rq[...])


class Projection:
    SEMS = 7

    def __init__(self, place, rows, send, recv):
        self.p, self.rows, self.send, self.recv = place, rows, send, recv

    def _copy(self, k, ref, device):
        return remote(ref, ref, self.send.at[k], self.recv.at[k], device)

    def _plane(self):
        p = self.p
        own = self.rows.at[p.c, p.z, p.dp]
        return [self._copy(0, own, p.at_x()), self._copy(1, own, p.at_y())]

    def _corner(self):
        p = self.p
        x_chip, y_chip = p.at_x()[0], p.at_y()[0]
        taken, target = jnp.where(p.c == 0, x_chip, y_chip), jnp.where(p.c == 0, y_chip, x_chip)
        return [self._copy(2, self.rows.at[p.c, p.z, taken], (target, p.fsdp))]

    def _line(self):
        p = self.p
        return [self._copy(2 + d, self.rows.at[p.c, p.z], p.at_z(d)) for d in (1, 2, 3)]

    def _core(self):
        return [self._copy(6, self.rows.at[self.p.c], self.p.core())]

    def start(self, pooled, grad):
        self.rows[self.p.c, self.p.z, self.p.dp] = low(jnp.concatenate([pooled, grad], axis=0))

    def take(self, stage):
        order = (self._plane, self._corner, self._line, self._core)
        if stage > 0:
            for copy in order[stage - 1]():
                copy.wait()
        if stage < 4:
            for copy in order[stage]():
                copy.start()

    def product(self):
        rows = wide(self.rows[...]).reshape(32, 2, 8, 768)
        return dot(low(rows[:, 0].reshape(256, 768)), low(rows[:, 1].reshape(256, 768)), 0, 0)


class Small:
    SEMS = 6

    def __init__(self, place, sums, got, line, send, recv):
        self.p, self.sums, self.got, self.line, self.send, self.recv = place, sums, got, line, send, recv

    def _pair(self, i):
        device = (self.p.core, self.p.at_x, self.p.at_y)[i]()
        return remote(self.sums.at[i], self.got.at[i], self.send.at[i], self.recv.at[i], device)

    def _line(self):
        p = self.p
        return [
            remote(self.sums.at[3], self.line.at[p.z], self.send.at[2 + d], self.recv.at[2 + d], p.at_z(d))
            for d in (1, 2, 3)
        ]

    def start(self):
        self._pair(0).start()

    def turn(self, i):
        self._pair(i).wait_recv()
        self.sums[i + 1] = self.sums[i] + self.got[i]
        if i < 2:
            self._pair(i + 1).start()
        else:
            self.line[self.p.z] = self.sums[3]
            for copy in self._line():
                copy.start()

    def finish(self):
        for copy in self._line():
            copy.wait()
        for i in range(3):
            self._pair(i).wait_send()
        return self.line[0] + self.line[1] + self.line[2] + self.line[3]


RING = 3
KEPT = 7
LEFT = 4
PLACES = [1, 2, 3, 0, 1, 2, 4, 5, 3, 0, 1]
SAID = [0, 0, 0, 0, 1, 1, 0, 0, 1, 1, 1]
BLOCKS = [
    (5, 0, 128, False),
    (5, 1, 128, True),
    (5, 2, 128, False),
    (4, 0, 96, False),
    (4, 1, 96, False),
    (4, 2, 96, False),
    (4, 3, 96, False),
    (3, 0, 96, False),
    (2, 0, 96, False),
    (1, 0, 96, False),
    (0, 0, 96, False),
]
PLAN = {
    "g0": [
        (0, 0), (10, 0),
    ],
    "g1": [
        (0, 1),
    ],
    "g2": [
        (0, 2), (11, 0), (1, 0),
    ],
    "g3": [
        (1, 1), (0, 3), (1, 2),
    ],
    "g4": [
        (0, 4),
    ],
    "n1": [
        (1, 3),
    ],
    "n2": [
        (2, 0),
    ],
    "g6": [
        (0, 5), (0, 6), (2, 2),
    ],
    "n3": [
        (1, 4),
    ],
    "g7": [
        (1, 5),
    ],
    "og": [
        (0, 7), (1, 6), (12, 0),
    ],
    "a0": [
        (2, 4),
    ],
    "a1": [
        (2, 1), (1, 7), (3, 0),
    ],
    "a2": [
        (3, 2),
    ],
    "a3": [
        (2, 5),
    ],
    "a4": [
        (3, 1), (2, 6),
    ],
    "a5": [
        (2, 7),
    ],
    "g8": [
        (0, 8), (3, 5), (2, 3), (3, 4),
    ],
    "g9": [
        (0, 9), (1, 8),
    ],
    "g10": [
        (13, 0), (3, 3), (0, 10), (1, 9), (4, 5), (1, 10), (3, 7), (2, 8), (3, 6),
    ],
    "tail": [
        (4, 3), (2, 9), (4, 4), (4, 1), (2, 10), (5, 5), (3, 8), (4, 2), (4, 6), (4, 7), (4, 0), (3,
        9),
    ],
    "table": [
        (5, 4), (4, 8), (3, 10), (5, 6), (5, 7), (5, 2), (5, 3), (5, 1), (4, 9), (5, 0), (4, 10),
        (5, 9), (5, 8), (6, 6), (5, 10), (6, 0), (6, 4), (6, 3), (6, 5), (6, 7), (6, 9), (6, 2), (6,
        1), (6, 8), (6, 10),
    ],
}


def attend_back(p, t, q, keys, values, probs, held, sums, table):
    heads, after = heads_of(p), pl.ds(pl.multiple_of(p * LANES + 768, LANES), LANES)
    ups = stacked(held[rows_of(t), heads])
    qs = stacked(q[rows_of(t), heads])
    soft = probs[probs_at(p, t)]
    weighted = wide(soft) * dot(ups, values[span_of(t), heads], 1, 1)
    grad = weighted - wide(soft) * jnp.sum(weighted, axis=1, keepdims=True)
    grad_low = low(grad)
    out = dot(side_by_side(grad_low), stacked(keys[span_of(t), heads]))
    held[rows_of(t), after] = low(out)
    for first, more in ((0, dot(grad_low, qs, 0, 0)), (6, dot(soft, ups, 0, 0))):
        where = pl.ds(first + t, 3)
        sums[where] = sums[where] + more.reshape(3, TILE, LANES)
    table[p] += grad


def layer_kernel(units, *refs):
    x_ref, seg_ref, pool_ref, emb_ref, g1_ref, g2_ref, g3_ref, table_ref, near_ref, far_ref = refs[:10]
    shards, outs, input_out, emb_out, small_out = refs[10:17], refs[17:24], refs[24], refs[25], refs[26]
    wholes, refs = refs[27:34], refs[34:]
    act, slope, n1, n2, mixed, q, upstream, keys, values, probs, h1, h2, band, mask, rays, ring, core_low, core_tall = refs[:18]
    refs = refs[18:]
    buffers = []
    for u, (_, _, rows, line_first) in enumerate(BLOCKS):
        count = 1 + (u < KEPT) + len((LineFirst if line_first else Reduce).shapes(rows))
        buffers.append(list(refs[:count]))
        refs = refs[count:]
    small_sums, small_got, small_line, all_rows = refs[:4]
    send, recv, back_send, back_recv, credit, local, writes, small_send, small_recv, rows_send, rows_recv = refs[4:]
    wq, wk, wv, wo, wup, wdn, wpj = wholes
    place = Place()
    gather = Gather(place, units, shards, wholes, send, recv)
    own = [
        pltpu.make_async_copy(shard, whole.at[place.z, place.c], local.at[i])
        for i, (shard, whole) in enumerate(zip(shards, wholes))
    ]
    works, results = [], []
    for u, (array, j, rows, line_first) in enumerate(BLOCKS):
        rest = buffers[u]
        total, at = rest.pop(0), PLACES[u]
        core = (core_low, *(core_tall.at[i, :, pl.ds(0, rows), :] for i in range(3)), wpj.at[:, 0], wpj.at[:, 1])[at]
        kept = rest.pop(0) if u < KEPT else wup.at[:, 0, :, pl.ds(768 * (u - KEPT), 768)]
        grad = ring.at[u % RING, :, :, pl.ds(0, rows), :]
        kind = LineFirst if line_first else Reduce
        turns = (credit, SAID[u], u < sum(SAID))
        works.append(kind(place, u % 2 == 0, grad, kept, core, total, rest, back_send.at[u], back_recv.at[u], *turns))
        dst = outs[5].at[pl.ds(128 * j, 128), :] if array == 5 else outs[array].at[:, pl.ds(768 * j, 768)]
        results.append(pltpu.make_async_copy(total, dst, writes.at[u]))
    for copy in own:
        copy.start()
    place.greet()
    n = len(units)

    def receive(name):
        for stage, u in ARRIVALS.get(name, ()):
            if stage == 0:
                gather.start(u)
            elif stage < 4:
                gather.plane(u, stage - 1)
            elif stage < 7:
                gather.corner(u, stage - 4)
            elif stage == 7:
                gather.pair(u)
            else:
                gather.arrive(u)
                if u < n - LEFT:
                    gather.finish(u)

    x = wide(x_ref[...])
    n1[...] = low(x * norm_factor(x) * g1_ref[...].reshape(1, 768))
    for copy in own:
        copy.wait()
    place.meet()
    receive("start")
    receive("n1")
    ray = dot_exact(table_ref[...], near_ref[...])
    for h in range(ray.shape[0]):
        rolled = pltpu.roll(jnp.broadcast_to(ray[h : h + 1], (TILE, 512)), 0, 1, stride=1, stride_axis=0)
        band[h // 2, pl.ds((h % 2) * TILE, TILE), :] = rolled[:, :SPAN]
    receive("band")
    seg = seg_ref[...]
    seg_f = wide(seg)
    column = jnp.transpose(jnp.broadcast_to(seg_f, (TILE, 512)))
    edge = jnp.full((1, TILE), -1.0, jnp.float32)
    line = jnp.concatenate([edge, seg_f, edge], axis=1)
    for t in range(4):
        own_seg = column[t * TILE : (t + 1) * TILE]
        same = jnp.concatenate([own_seg] * 3, axis=1) == line[:, t * TILE : t * TILE + SPAN]
        hidden = jnp.where(same, 0.0, -1e30)
        for i in range(3):
            mask[3 * t + i] = hidden[:, i * TILE : (i + 1) * TILE]
    blank = jnp.zeros((TILE, 768), jnp.bfloat16)
    for ref in (keys, values):
        ref[pl.ds(0, TILE), :] = blank
        ref[pl.ds(640, TILE), :] = blank
    receive("mask")
    q[...] = low(dot(n1[...], flat(wq)))
    receive("q")
    keys[pl.ds(TILE, 512), :] = low(dot(n1[...], flat(wk)))
    receive("k")
    values[pl.ds(TILE, 512), :] = low(dot(n1[...], flat(wv)))
    receive("v")

    def pairs(first, last):
        @pl.loop(first, last)
        def _(p):
            for t in range(4):
                attend(p, t, q, keys, values, band, mask, probs, mixed)

    first = 0
    for p in range(6):
        if p == 5 or ARRIVALS.get(f"a{p}"):
            pairs(first, p + 1)
            first = p + 1
        receive(f"a{p}")
    hidden = wide(x_ref[...]) + dot(mixed[...], flat(wo))
    h1[...] = hidden
    n2[...] = low(hidden * norm_factor(hidden) * g2_ref[...].reshape(1, 768))
    receive("h")
    for j in range(4):
        cols = pl.ds(768 * j, 768)
        value, grad = gelu_both(dot(n2[...], flat(wup, slice(None), slice(None), slice(None), cols)))
        act[:, cols] = low(value)
        slope[:, cols] = low(grad)
        receive(f"u{j}")
    for j in range(3):
        part = jnp.concatenate([act[:, pl.ds(384 * s + 128 * j, 128)] for s in range(8)], axis=1)
        more = dot(part, flat(wdn, slice(None), slice(None), pl.ds(128 * j, 128)))
        h2[...] = (h1[...] if j == 0 else h2[...]) + more
        receive(f"d{j}")
    h = h2[...]
    factor = norm_factor(h)
    g3 = g3_ref[...].reshape(1, 768)
    fin = h * factor * g3
    eye = lax.broadcasted_iota(jnp.int32, (8, 8), 0) == lax.broadcasted_iota(jnp.int32, (8, 8), 1)
    pool = jnp.sum(jnp.where(eye, wide(pool_ref[...]), 0.0), axis=1, keepdims=True)
    member = jnp.where(seg_f == pool, 1.0, 0.0)
    count = jnp.sum(member, axis=1, keepdims=True)
    pooled = dot(low(member), low(fin)) / count
    receive("e1")
    wp = flat(wpj)
    both = dot(two_parts(pooled), wp)
    projected = both[:8] + both[8:]
    inverse = lax.rsqrt(jnp.sum(projected * projected, axis=-1, keepdims=True) + EPSILON)
    emb = projected * inverse
    up = emb_ref[...].reshape(8, 768)
    eg = inverse * (up - emb * jnp.sum(up * emb, axis=-1, keepdims=True))
    emb_out[...] = emb
    projection = Projection(place, all_rows, rows_send, rows_recv)

    def take(stage, u):
        work = works[u]
        if stage >= 10:
            projection.take(stage - 10)
        elif stage == 6:
            work.arrive()
            results[u].start()
        else:
            (work.start, work.first, work.second, work.third, work.spread, work.corner)[stage]()

    def serve(name):
        for stage, u in PLAN.get(name, ()):
            take(stage, u)

    def produce(u, value):
        works[u].g[...] = low(value).reshape(works[u].g.shape)
        serve(f"g{u}")

    projection.start(pooled, eg)
    serve("start")
    both = dot(two_parts(eg), flat(wpj), 1, 1)
    pooled_grad = (both[:8] + both[8:]) / count
    twice = low(jnp.concatenate([member, member], axis=0))
    fin_grad = dot(twice, two_parts(pooled_grad), 0, 0)
    stream, gain_three = norm_back(h, factor, g3, fin_grad)
    h2[...] = stream
    upstream[...] = low(stream)
    for j in range(3):
        picked = jnp.concatenate([act[:, pl.ds(384 * s + 128 * j, 128)] for s in range(8)], axis=1)
        produce(j, dot(picked, upstream[...], 0, 0))
    for u in range(n - LEFT, n):
        gather.finish(u)
    for j in range(4):
        cols = pl.ds(768 * j, 768)
        grad = low(wide(slope[:, cols]) * dot(upstream[...], flat(wdn, j), 1, 1))
        slope[:, cols] = grad
        produce(3 + j, dot(n2[...], grad, 0, 0))
        more = dot(grad, flat(wup, slice(None), slice(None), slice(None), cols), 1, 1)
        for i in range(2):
            where, half_more = pl.ds(2 * i, 2), more[:, 384 * i : 384 * (i + 1)].reshape(2, 256, 384)
            band[where] = half_more if j == 0 else band[where] + half_more
        serve(f"n{j}")
    n2_grad = jnp.concatenate([band[pl.ds(2 * i, 2)].reshape(512, 384) for i in range(2)], axis=1)
    h = h1[...]
    more, gain_two = norm_back(h, norm_factor(h), g2_ref[...].reshape(1, 768), n2_grad)
    through = h2[...] + more
    h2[...] = through
    upstream[...] = low(through)
    produce(7, dot(mixed[...], upstream[...], 0, 0))
    act[:, pl.ds(0, 768)] = low(dot(upstream[...], flat(wo), 1, 1))
    band[...] = jnp.zeros_like(band)
    serve("og")

    def pairs_back(first, last):
        @pl.loop(first, last)
        def _(p):
            mask[...] = jnp.zeros_like(mask)
            for t in range(4):
                attend_back(p, t, q, keys, values, probs, act, mask, band)
            heads, after = heads_of(p), pl.ds(pl.multiple_of(p * LANES + 768, LANES), LANES)
            slope[:, heads] = low(mask[pl.ds(1, 4)]).reshape(512, LANES)
            slope[:, after] = low(mask[pl.ds(7, 4)]).reshape(512, LANES)

    first = 0
    for p in range(6):
        if p == 5 or PLAN.get(f"a{p}"):
            pairs_back(first, p + 1)
            first = p + 1
        serve(f"a{p}")
    kg, vg, qg = slope[:, pl.ds(0, 768)], slope[:, pl.ds(768, 768)], act[:, pl.ds(768, 768)]
    produce(8, dot(n1[...], vg, 0, 0))
    produce(9, dot(n1[...], kg, 0, 0))
    produce(10, dot(n1[...], qg, 0, 0))
    n1_grad = dot(qg, flat(wq), 1, 1) + dot(kg, flat(wk), 1, 1) + dot(vg, flat(wv), 1, 1)
    x = wide(x_ref[...])
    more, gain_one = norm_back(x, norm_factor(x), g1_ref[...].reshape(1, 768), n1_grad)
    h2[...] = h2[...] + more
    last = pltpu.make_async_copy(h2, input_out, writes.at[len(BLOCKS)])
    last.start()
    serve("tail")
    turn = lax.broadcasted_iota(jnp.int32, (TILE, TILE), 0) + lax.broadcasted_iota(jnp.int32, (TILE, TILE), 1)
    mirror = low(jnp.where(turn == TILE - 1, 1.0, 0.0))
    rays[...] = jnp.zeros_like(rays)
    for h in range(12):
        tile = band[h // 2, pl.ds((h % 2) * TILE, TILE), :]
        high = low(tile)
        upside = dot(mirror, high) + dot(mirror, low(tile - wide(high)))
        spread = jnp.concatenate([upside, jnp.zeros((TILE, 512 - SPAN), jnp.float32)], axis=1)
        rolled = pltpu.roll(spread, 0, 1, stride=1, stride_axis=0)
        rays[pl.ds(h, 1), :] = jnp.sum(rolled, axis=0, keepdims=True)
    by_bucket = dot_exact(rays[...], far_ref[...], 1, 1)
    small_sums[0, :, pl.ds(0, 768)] = jnp.concatenate(
        [gain_one, gain_two, gain_three, jnp.zeros((5, 768), jnp.float32)], axis=0
    )
    small_sums[0, :, pl.ds(768, 256)] = jnp.zeros((8, 256), jnp.float32)
    small_sums[0, :, pl.ds(768, 32)] = by_bucket[:8]
    small_sums[0, :, pl.ds(896, 32)] = by_bucket[8:]
    small = Small(place, small_sums, small_got, small_line, small_send, small_recv)
    small.start()
    projection.take(4)
    ring[0, :, :, pl.ds(0, 96), :] = low(projection.product()).reshape(4, 2, 96, 768)
    product = pltpu.make_async_copy(ring.at[0, place.z, place.c, pl.ds(0, 96), :], outs[6], writes.at[len(BLOCKS) + 1])
    product.start()
    rest = PLAN["table"]
    for i in range(len(rest)):
        if i in (4, 9, 14):
            small.turn(i // 5)
        take(*rest[i])
    small_out[...] = small.finish()
    product.wait()
    for copy in results:
        copy.wait()
    last.wait()


def far_buckets(buckets):
    return bucket_rows(np.arange(512) - 255, buckets)


def layer_all(x, seg_ids, pool_index, emb_grad, gains, table, shards):
    f32, b16 = jnp.float32, jnp.bfloat16
    units = [Unit(*unit) for unit in UNITS]
    held = [(512, 3072)] * 2 + [(512, 768)] * 5 + [(768, 768)] * 2 + [(768, 3072)]
    scratch = [pltpu.VMEM((4, 2) + shard.shape, b16) for shard in shards]
    scratch += [pltpu.VMEM(shape, b16) for shape in held]
    scratch += [pltpu.VMEM((512, 768), f32)] * 2
    scratch += [pltpu.VMEM((6, 2 * TILE, SPAN), f32), pltpu.VMEM((12, TILE, LANES), f32), pltpu.VMEM((16, 512), f32)]
    scratch += [pltpu.VMEM((RING, 4, 2, 128, 768), b16), pltpu.VMEM((4, 96, 768), b16)]
    scratch += [pltpu.VMEM((3, 4, 128, 768), b16)]
    for u, (_, _, rows, line_first) in enumerate(BLOCKS):
        shapes = [(rows, 768)] + [(4, rows, 768)] * (u < KEPT)
        shapes += (LineFirst if line_first else Reduce).shapes(rows)
        scratch += [pltpu.VMEM(shape, b16) for shape in shapes]
    scratch += [pltpu.VMEM((k, 8, 1024), f32) for k in (4, 3, 4)] + [pltpu.VMEM((2, 4, 4, 16, 768), b16)]
    dma = pltpu.SemaphoreType.DMA
    scratch += [dma((len(units), Gather.SEMS))] * 2 + [dma((len(BLOCKS), Reduce.SEMS))] * 2
    scratch += [pltpu.SemaphoreType.REGULAR, dma((7,)), dma((len(BLOCKS) + 2,)), dma((Small.SEMS,)), dma((Small.SEMS,))]
    scratch += [dma((Projection.SEMS,))] * 2
    outs = [jax.ShapeDtypeStruct(shard.shape, b16) for shard in shards]
    outs += [jax.ShapeDtypeStruct(s, f32) for s in [(512, 768), (8, 768), (8, 1024)]]
    vmem, large = pl.BlockSpec(memory_space=pltpu.VMEM), pl.BlockSpec(memory_space=pl.ANY)
    buckets = table.shape[1]
    return pl.pallas_call(
        partial(layer_kernel, units),
        out_shape=outs,
        in_specs=[vmem] * 10 + [large] * 7,
        out_specs=[large] * 8 + [vmem] * 2,
        scratch_shapes=scratch,
        compiler_params=pltpu.CompilerParams(
            collective_id=0, has_side_effects=True, vmem_limit_bytes=VMEM_BYTES
        ),
        name="layer",
    )(x, seg_ids, pool_index, emb_grad, *gains, table, ray_buckets(buckets), far_buckets(buckets), *shards)


def finish_kernel(emb_in, input_in, small_in, *refs):
    grads, outs = refs[:7], refs[7:]
    emb_out, input_out, gains, table = outs[0], outs[1], outs[9:12], outs[12]
    emb_out[...] = emb_in[...].reshape(emb_out.shape)
    input_out[...] = input_in[...].reshape(input_out.shape)
    for grad, out in zip(grads, outs[2:9]):
        out[...] = wide(grad[...])
    for i, gain in enumerate(gains):
        gain[...] = small_in[pl.ds(i, 1), pl.ds(0, 768)].reshape(768)
    both = jnp.concatenate([small_in[:, pl.ds(768, 128)], small_in[:, pl.ds(896, 128)]], axis=0)
    table[...] = both[:12, :32]


def finish_all(emb, input_grad, small, grads):
    f32 = jnp.float32
    shapes = [(1, 8, 768), (1, 512, 768)] + [g.shape for g in grads] + [(768,)] * 3 + [(12, 32)]
    vmem = pl.BlockSpec(memory_space=pltpu.VMEM)
    return pl.pallas_call(
        finish_kernel,
        out_shape=[jax.ShapeDtypeStruct(s, f32) for s in shapes],
        in_specs=[vmem] * 10,
        out_specs=[vmem] * 13,
        compiler_params=pltpu.CompilerParams(vmem_limit_bytes=VMEM_BYTES),
        name="finish",
    )(emb, input_grad, small, *grads)


def near_device(
    inputs,
    seg_ids,
    pool_index,
    w_query,
    w_key,
    w_value,
    w_out,
    w_up,
    w_down,
    w_proj,
    gain_attn,
    gain_ffn,
    gain_final,
    bias_table,
    emb_grad,
):
    x = inputs.reshape(-1, inputs.shape[-1])
    shards = (w_query, w_key, w_value, w_out, w_up, w_down, w_proj)
    gains = (gain_attn, gain_ffn, gain_final)
    *grads, input_grad, emb, small = layer_all(x, seg_ids, pool_index, emb_grad, gains, bias_table.T, shards)
    out = finish_all(emb, input_grad, small, grads)
    return (*out[:12], out[12].T)


def general(
    inputs,
    seg_ids,
    pool_index,
    w_query,
    w_key,
    w_value,
    w_out,
    w_up,
    w_down,
    w_proj,
    gain_attn,
    gain_ffn,
    gain_final,
    bias_table,
    emb_grad,
):
    rows, length, width = inputs.shape
    buckets, heads = bias_table.shape
    head_dim = width // heads
    tokens = rows * length
    head_shape = (rows, length, heads, head_dim)
    gathered = (
        lax.all_gather(w_query, "fsdp", axis=0, tiled=True),
        lax.all_gather(w_key, "fsdp", axis=0, tiled=True),
        lax.all_gather(w_value, "fsdp", axis=0, tiled=True),
        lax.all_gather(w_out, "fsdp", axis=0, tiled=True),
        lax.all_gather(w_up, "fsdp", axis=0, tiled=True),
        lax.all_gather(w_down, "fsdp", axis=0, tiled=True),
        lax.all_gather(w_proj, "fsdp", axis=0, tiled=True),
    )
    full_query, full_key, full_value, full_out, full_up, full_down, full_proj = gathered
    flat = inputs.reshape(tokens, width).astype(jnp.float32)
    normed_one, factor_one = rms_forward(flat, gain_attn)
    normed_one = normed_one.astype(jnp.bfloat16)
    queries = matmul(normed_one, full_query).astype(jnp.bfloat16).reshape(head_shape)
    key_rows = matmul(normed_one, full_key).astype(jnp.bfloat16).reshape(head_shape)
    value_rows = matmul(normed_one, full_value).astype(jnp.bfloat16).reshape(head_shape)
    bucket_ids = jnp.asarray(bucket_table(length, buckets, REACH))
    onehot_cols = (
        jnp.arange(buckets, dtype=jnp.int32)[:, None] == bucket_ids.reshape(1, length * length)
    ).astype(jnp.bfloat16)
    bias = jnp.dot(bias_table.T, onehot_cols.astype(jnp.float32), precision=HIGH).reshape(
        heads, length, length
    )

    def attend_row(pieces):
        query_row, key_row, value_row, seg_row = pieces
        scores = row_scores(query_row, key_row, seg_row, bias)
        row_peak = jnp.max(scores, axis=-1, keepdims=True)
        log_total = row_peak + jnp.log(jnp.sum(jnp.exp(scores - row_peak), axis=-1, keepdims=True))
        soft_low = jnp.exp(scores - log_total).astype(jnp.bfloat16)
        mixed = jnp.einsum("hqk,khd->qhd", soft_low, value_row, preferred_element_type=jnp.float32)
        return (mixed.astype(jnp.bfloat16), log_total)

    attended, log_totals = lax.map(attend_row, (queries, key_rows, value_rows, seg_ids))
    attended_flat = attended.reshape(tokens, width)
    hidden_one = flat + matmul(attended_flat, full_out)
    normed_two, factor_two = rms_forward(hidden_one, gain_ffn)
    normed_two = normed_two.astype(jnp.bfloat16)
    pre_act = matmul(normed_two, full_up)
    activated = jax.nn.gelu(pre_act, approximate=True).astype(jnp.bfloat16)
    hidden_two = hidden_one + matmul(activated, full_down)
    final_rows, factor_three = rms_forward(hidden_two, gain_final)
    member = (seg_ids[:, None, :] == pool_index[:, :, None]).astype(jnp.float32)
    counts = jnp.sum(member, axis=-1, keepdims=True)
    pooled = (
        jnp.einsum("rpl,rld->rpd", member, final_rows.reshape(rows, length, width), precision=HIGH)
        / counts
    )
    proj_full = full_proj.astype(jnp.float32)
    projected = jnp.einsum("rpd,de->rpe", pooled, proj_full, precision=HIGH)
    inverse_len = lax.rsqrt(jnp.sum(projected * projected, axis=-1, keepdims=True) + EPSILON)
    embeddings = projected * inverse_len
    emb_dot = jnp.sum(emb_grad * embeddings, axis=-1, keepdims=True)
    projected_grad = inverse_len * (emb_grad - embeddings * emb_dot)
    grad_proj = jnp.einsum("rpd,rpe->de", pooled, projected_grad, precision=HIGH)
    pooled_grad = jnp.einsum("rpe,de->rpd", projected_grad, proj_full, precision=HIGH) / counts
    final_grad = jnp.einsum("rpl,rpd->rld", member, pooled_grad, precision=HIGH).reshape(
        tokens, width
    )
    stream_two, grad_gain_final = rms_backward(hidden_two, factor_three, gain_final, final_grad)
    back_weights = (
        lax.all_gather(w_query, "fsdp", axis=0, tiled=True),
        lax.all_gather(w_key, "fsdp", axis=0, tiled=True),
        lax.all_gather(w_value, "fsdp", axis=0, tiled=True),
        lax.all_gather(w_out, "fsdp", axis=0, tiled=True),
        lax.all_gather(w_up, "fsdp", axis=0, tiled=True),
        lax.all_gather(w_down, "fsdp", axis=0, tiled=True),
        lax.all_gather(w_proj, "fsdp", axis=0, tiled=True),
    )
    back_query, back_key, back_value, back_out, back_up, back_down, back_proj = back_weights
    ffn_grad = stream_two.astype(jnp.bfloat16)
    grad_down = matmul_left(activated, ffn_grad)
    act_grad = matmul_right(ffn_grad, back_down)
    gelu_pullback = jax.vjp(partial(jax.nn.gelu, approximate=True), pre_act)[1]
    pre_grad = gelu_pullback(act_grad)[0].astype(jnp.bfloat16)
    grad_up = matmul_left(normed_two, pre_grad)
    normed_two_grad = matmul_right(pre_grad, back_up)
    stream_mid, grad_gain_ffn = rms_backward(hidden_one, factor_two, gain_ffn, normed_two_grad)
    stream_one = stream_two + stream_mid
    attn_grad = stream_one.astype(jnp.bfloat16)
    grad_out = matmul_left(attended_flat, attn_grad)
    mixed_grad = matmul_right(attn_grad, back_out).astype(jnp.bfloat16).reshape(head_shape)

    def attend_back(pieces):
        query_row, key_row, value_row, seg_row, log_total, upstream_row = pieces
        scores = row_scores(query_row, key_row, seg_row, bias)
        soft_rows = jnp.exp(scores - log_total)
        soft_grad = jnp.einsum(
            "qhd,khd->hqk", upstream_row, value_row, preferred_element_type=jnp.float32
        )
        score_grad = (
            soft_rows * (soft_grad - jnp.sum(soft_rows * soft_grad, axis=-1, keepdims=True))
        ).astype(jnp.bfloat16)
        query_grad = jnp.einsum(
            "hqk,khd->qhd", score_grad, key_row, preferred_element_type=jnp.float32
        ).astype(jnp.bfloat16)
        key_grad = jnp.einsum(
            "hqk,qhd->khd", score_grad, query_row, preferred_element_type=jnp.float32
        ).astype(jnp.bfloat16)
        value_grad = jnp.einsum(
            "hqk,qhd->khd",
            soft_rows.astype(jnp.bfloat16),
            upstream_row,
            preferred_element_type=jnp.float32,
        ).astype(jnp.bfloat16)
        table_grad = matmul_right(score_grad.reshape(heads, length * length), onehot_cols)
        return (query_grad, key_grad, value_grad, table_grad)

    query_grads, key_grads, value_grads, table_grads = lax.map(
        attend_back, (queries, key_rows, value_rows, seg_ids, log_totals, mixed_grad)
    )
    grad_table = jnp.sum(table_grads, axis=0).T
    query_flat = query_grads.reshape(tokens, width)
    key_flat = key_grads.reshape(tokens, width)
    value_flat = value_grads.reshape(tokens, width)
    grad_query = matmul_left(normed_one, query_flat)
    grad_key = matmul_left(normed_one, key_flat)
    grad_value = matmul_left(normed_one, value_flat)
    normed_one_grad = (
        matmul_right(query_flat, back_query)
        + matmul_right(key_flat, back_key)
        + matmul_right(value_flat, back_value)
    )
    stream_in, grad_gain_attn = rms_backward(flat, factor_one, gain_attn, normed_one_grad)
    input_grad = (stream_one + stream_in).reshape(rows, length, width)
    shard_query, shard_key, shard_value, shard_out, shard_up, shard_down, shard_proj = (
        lax.psum_scatter(grad_query, "fsdp", scatter_dimension=0, tiled=True),
        lax.psum_scatter(grad_key, "fsdp", scatter_dimension=0, tiled=True),
        lax.psum_scatter(grad_value, "fsdp", scatter_dimension=0, tiled=True),
        lax.psum_scatter(grad_out, "fsdp", scatter_dimension=0, tiled=True),
        lax.psum_scatter(grad_up, "fsdp", scatter_dimension=0, tiled=True),
        lax.psum_scatter(grad_down, "fsdp", scatter_dimension=0, tiled=True),
        lax.psum_scatter(grad_proj, "fsdp", scatter_dimension=0, tiled=True),
    )
    summed = (
        lax.psum(shard_query.astype(jnp.bfloat16), "dp").astype(jnp.float32),
        lax.psum(shard_key.astype(jnp.bfloat16), "dp").astype(jnp.float32),
        lax.psum(shard_value.astype(jnp.bfloat16), "dp").astype(jnp.float32),
        lax.psum(shard_out.astype(jnp.bfloat16), "dp").astype(jnp.float32),
        lax.psum(shard_up.astype(jnp.bfloat16), "dp").astype(jnp.float32),
        lax.psum(shard_down.astype(jnp.bfloat16), "dp").astype(jnp.float32),
        lax.psum(shard_proj.astype(jnp.bfloat16), "dp").astype(jnp.float32),
    )
    smalls = lax.psum((grad_gain_attn, grad_gain_ffn, grad_gain_final, grad_table), ("dp", "fsdp"))
    return (
        embeddings,
        input_grad,
        summed[0],
        summed[1],
        summed[2],
        summed[3],
        summed[4],
        summed[5],
        summed[6],
        smalls[0],
        smalls[1],
        smalls[2],
        smalls[3],
    )


def solution(mesh):
    near = (mesh.shape["dp"], mesh.shape["fsdp"]) == (4, 8)
    return jax.shard_map(
        near_device if near else general,
        mesh=mesh,
        in_specs=(
            P(("dp", "fsdp"), None, None),
            P(("dp", "fsdp"), None),
            P(("dp", "fsdp"), None),
            P("fsdp", None),
            P("fsdp", None),
            P("fsdp", None),
            P("fsdp", None),
            P("fsdp", None),
            P("fsdp", None),
            P("fsdp", None),
            P(),
            P(),
            P(),
            P(),
            P(("dp", "fsdp"), None, None),
        ),
        out_specs=(
            P(("dp", "fsdp"), None, None),
            P(("dp", "fsdp"), None, None),
            P("fsdp", None),
            P("fsdp", None),
            P("fsdp", None),
            P("fsdp", None),
            P("fsdp", None),
            P("fsdp", None),
            P("fsdp", None),
            P(),
            P(),
            P(),
            P(),
        ),
        check_vma=False,
    )
```
